128 devices in a mesh: seq: 16 (over y, z), mp: 8 (over x, core).
Axes of the slice: x: 4, y: 4, z: 4, core: 2. Of those that a mesh axis runs over, the one named last changes fastest.
Arguments:
- stretch_x: bfloat16 [8192, 16384], P(('seq', 'mp')), may hold values from -6 to 6
- stretch_bc: bfloat16 [8192, 2, 2048], P(('seq', 'mp')), may hold values from -1.75 to 1.75
- stretch_dt: bfloat16 [8192, 256], P(('seq', 'mp')), may hold values from -5 to 5
- stretch_q: bfloat16 [8192, 8192], P(('seq', 'mp')), may hold values from -22 to 22
- stretch_kv: bfloat16 [8192, 2, 1024], P(('seq', 'mp')), may hold values from -6 to 6
- stretch_place: int32 [128], P('seq'), may hold values from 0 to 127, as said below
- segment_ids: int32 [8192], P('seq'), may hold values from 0 to 5, never falling along the last dimension, each value on 1 to 4096 neighbouring positions
- ssm_rate: float32 [256], replicated, may hold values from 0.001 to 1
- dt_bias: float32 [256], replicated, may hold values from -5 to -2
- skip_gain: float32 [256], replicated, may hold values from 0.5 to 1.5
Outputs:
- ssm_out: bfloat16 [8192, 16384], P('seq', 'mp')
- attn_out: bfloat16 [8192, 8192], P('seq', 'mp')
The draws below stay inside these ranges and needn't reach their ends.
Inputs may be any that keep to these rules, and one draw needn't show every extreme that they name: stretch_place holds each of 0 to 127 once. Stretch c goes to owner stretch_place[c] // 8; every owner receives 512 // 64 stretches; at most 1 of the stretches held by one index of seq go to one owner, and every index of seq sends exactly 1 to some owner. `segment_ids`: document ids never fall along the sequence; each document has 1 to 4096 tokens, one exactly that many.
All inputs are finite; a program needn't handle non-finite values.
Results may differ from the reference program's by a relative error of at most 0.0095.
Values may be sent and summed in bfloat16 or wider, within the bound.
No kernel may reach another device: no remote copies, remote signals or barrier semaphores. Data moves between devices by JAX's collectives and lax.ppermute only.
A program may use at most 192 MiB of HBM per device.

```python
import math
import jax
import jax.numpy as jnp
import numpy as np
from jax import lax

SSM_HEADS = 256
HEAD_DIM = 64
STATE = 256
GROUPS = 8
Q_HEADS = 64
KV_HEADS = 8
ATT_DIM = 128
STRETCH_LEN = 64
BLOCK = 256
SEGS = 6
TOK_DEV = 512
TOKENS = 8192
STRETCHES = 128


def draw_stretch_place(key, part):
    per_dev = TOK_DEV // STRETCH_LEN
    owners = STRETCHES // per_dev
    all_keys = jax.random.split(key, 4)
    offsets = jax.random.permutation(all_keys[0], owners)
    shuffle = jax.random.permutation(all_keys[1], owners)
    relabel = jax.random.permutation(all_keys[2], owners)
    rounds = jnp.arange(per_dev) % max(owners - 1, 1)
    target = relabel[(shuffle[:, None] + offsets[rounds][None, :]) % owners]
    slot_keys = jax.random.split(all_keys[3], owners)
    slot_perm = jax.vmap(lambda sub_key: jax.random.permutation(sub_key, per_dev))(slot_keys)
    round_idx = jnp.broadcast_to(jnp.arange(per_dev)[None, :], (owners, per_dev))
    local_slot = slot_perm[target, round_idx]
    return (target * per_dev + local_slot).reshape(-1).astype(jnp.int32)


def plant_rows(key):
    places = jax.random.randint(jax.random.fold_in(key, 11), (STRETCHES,), 2, STRETCH_LEN)
    sign_draw = jax.random.normal(jax.random.fold_in(key, 12), (STRETCHES, KV_HEADS * ATT_DIM), jnp.float32)
    signs = jnp.where(sign_draw >= 0.0, 1.0, -1.0)
    levels = jnp.array([9.0, 13.0, 17.0, 22.0], jnp.float32)[jnp.arange(STRETCHES) % 4]
    within = jnp.arange(TOKENS) % STRETCH_LEN
    owner = jnp.arange(TOKENS) // STRETCH_LEN
    at_plant = within == places[owner]
    before_plant = within == places[owner] - 1
    second_before = within == places[owner] - 2
    return (at_plant, before_plant, second_before, signs[owner], levels[owner])


def base_values(key, shape):
    return jnp.clip(jax.random.normal(key, shape, jnp.float32), -6.0, 6.0)


def draw_stretch_dt(key, part):
    shape = (TOKENS, SSM_HEADS)
    base = jnp.clip(jax.random.normal(jax.random.fold_in(key, 31), shape, jnp.float32), -5.0, 5.0)
    places = draw_stretch_place(key, part)
    per_block = BLOCK // STRETCH_LEN
    hot_block = jax.random.randint(jax.random.fold_in(key, 32), (), 0, TOKENS // BLOCK)
    hot_stretch = places // per_block == hot_block
    hot_rows = hot_stretch[jnp.arange(TOKENS) // STRETCH_LEN]
    high = jax.random.uniform(jax.random.fold_in(key, 33), shape, jnp.float32, 3.0, 5.0)
    return jnp.where(hot_rows[:, None], high, base).astype(jnp.bfloat16)


def draw_stretch_q(key, part):
    at_plant, before_plant, second_before, signs, levels = plant_rows(key)
    shape = (TOKENS, Q_HEADS * ATT_DIM)
    base = base_values(jax.random.fold_in(key, 21), shape)
    group_size = Q_HEADS // KV_HEADS
    aligned = (levels[:, None] * signs).reshape(TOKENS, KV_HEADS, 1, ATT_DIM)
    aligned = jnp.broadcast_to(aligned, (TOKENS, KV_HEADS, group_size, ATT_DIM)).reshape(shape)
    return jnp.where(at_plant[:, None], aligned, base).astype(jnp.bfloat16)


def draw_stretch_kv(key, part):
    at_plant, before_plant, second_before, signs, levels = plant_rows(key)
    shape = (TOKENS, 2, KV_HEADS * ATT_DIM)
    base = base_values(jax.random.fold_in(key, 22), shape)
    factor = jnp.where(at_plant, -0.5, jnp.where(before_plant, 1.0, 0.98828125))
    planted_keys = factor[:, None] * signs
    chosen = at_plant | before_plant | second_before
    keys = jnp.where(chosen[:, None], planted_keys, base[:, 0])
    return jnp.stack([keys, base[:, 1]], axis=1).astype(jnp.bfloat16)


def block_scale(key, shape, shards, low, largest):
    loudness, own = 1.0, jax.random.fold_in(key, 6)
    for position, parts in shards:
        draws = jnp.exp(jax.random.uniform(jax.random.fold_in(own, position), (parts,), jnp.float32, low / len(shards), largest / len(shards)))
        loudness = loudness * jnp.repeat(draws, shape[position] // parts).reshape([-1 if axis == position else 1 for axis in range(len(shape))])
    return loudness


def profile(number_of, total, bound, skew):
    loads = [(1 << 20) // math.isqrt(rank ** skew) + 1 for rank in range(2, number_of + 1)]
    spare, counts = total - bound - (number_of - 1), [1] * (number_of - 1)
    while spare > 0:
        candidates = [i for i in range(number_of - 1) if counts[i] < bound]
        whole, budget = sum([loads[i] for i in candidates]), spare
        for i in candidates:
            more = min(bound - counts[i], max(1, budget * loads[i] // whole), spare)
            counts[i] = counts[i] + more
            spare = spare - more
    return np.array([bound] + counts)


def ragged(rng, amount, total, bound, skew):
    if amount == 2:
        one = jax.random.randint(rng, (), max(1, total - bound), min(bound, total - 1) + 1)
        return jnp.stack([one, total - one])
    lengths = jnp.asarray(profile(amount, total, bound, skew), jnp.int32)
    couples = (amount - 1) // 2
    donor, taker = lengths[1:1 + 2 * couples:2], lengths[2:2 + 2 * couples:2]
    margin = jnp.minimum(donor - 1, bound - taker)
    passed = jax.random.randint(jax.random.fold_in(rng, 1), (couples,), 0, 1 << 20) % (margin + 1)
    lengths = lengths.at[1:1 + 2 * couples:2].set(donor - passed).at[2:2 + 2 * couples:2].set(taker + passed)
    return lengths[jax.random.permutation(jax.random.fold_in(rng, 2), amount)]


def noise(rng, shape, deviation, most, shards=(), kind=jnp.bfloat16):
    values = deviation * jax.random.normal(rng, shape, jnp.float32)
    if shards:
        values = values * block_scale(rng, shape, shards, -0.22, 0.18)
    return jnp.clip(values, -most, most).astype(kind)


def setup_inputs(seed: int = 0) -> dict:
    streams_of = jax.random.split(jax.random.key(seed), 11)
    stretch_x = noise(streams_of[0], (TOKENS, SSM_HEADS * HEAD_DIM), 1.0, 6.0, ((0, 128),))
    stretch_bc = noise(streams_of[1], (TOKENS, 2, GROUPS * STATE), 0.25, 1.75, ((0, 128),))
    stretch_dt = draw_stretch_dt(jax.random.fold_in(streams_of[10], 71), 0)
    stretch_q = draw_stretch_q(jax.random.fold_in(streams_of[10], 71), 0)
    stretch_kv = draw_stretch_kv(jax.random.fold_in(streams_of[10], 71), 0)
    stretch_place = draw_stretch_place(jax.random.fold_in(streams_of[10], 71), 0)
    segment_ids = jnp.searchsorted(jnp.cumsum(ragged(streams_of[6], SEGS, TOKENS, TOKENS // 2, 2)), jnp.arange(TOKENS), side="right").astype(jnp.int32)
    ssm_rate = jnp.clip(jnp.exp(jax.random.uniform(streams_of[7], (SSM_HEADS,), jnp.float32, math.log(0.001), math.log(1.0))), 0.001, 1.0)
    dt_bias = jnp.clip(jax.random.uniform(streams_of[8], (SSM_HEADS,), jnp.float32, -5.0, -2.0), -5.0, -2.0)
    skip_gain = jnp.clip(jax.random.uniform(streams_of[9], (SSM_HEADS,), jnp.float32, 0.5, 1.5), 0.5, 1.5)
    return {"stretch_x": stretch_x, "stretch_bc": stretch_bc, "stretch_dt": stretch_dt, "stretch_q": stretch_q, "stretch_kv": stretch_kv, "stretch_place": stretch_place, "segment_ids": segment_ids, "ssm_rate": ssm_rate, "dt_bias": dt_bias, "skip_gain": skip_gain}


NEG_BIG = -1.0e30


def block_scan(inputs_x, step_size, log_decay, b_rows, c_rows, seg_rows, block):
    length = inputs_x.shape[0]
    heads = inputs_x.shape[1]
    width = inputs_x.shape[2]
    count = length // block
    positions = jnp.arange(block)
    causal = positions[:, None] >= positions[None, :]
    state_start = jnp.zeros((heads, b_rows.shape[1], width), jnp.float32)

    def one_block(carry, pieces):
        state_in, prev_seg = carry
        x_blk, size_blk, decay_blk, b_blk, c_blk, seg_blk = pieces
        cumulative = jnp.cumsum(decay_blk, axis=0)
        allowed = causal & (seg_blk[:, None] == seg_blk[None, :])
        gram_matrix = jnp.dot(c_blk, b_blk.T, preferred_element_type=jnp.float32)
        by_head = cumulative.T
        log_gaps = by_head[:, :, None] - by_head[:, None, :]
        weights = jnp.exp(jnp.where(allowed[None], log_gaps, NEG_BIG))
        mixing = lax.optimization_barrier((gram_matrix[None] * weights).astype(jnp.bfloat16)).astype(jnp.float32)
        driven = lax.optimization_barrier(
            (size_blk[:, :, None] * x_blk.astype(jnp.float32)).astype(jnp.bfloat16)).astype(jnp.float32)
        result = jnp.einsum('hts,shp->thp', mixing, driven)
        carried = jnp.where((seg_blk == prev_seg)[:, None], jnp.exp(cumulative), 0.0)
        reached = jnp.einsum('tn,hnp->thp', c_blk.astype(jnp.float32), state_in, precision=lax.Precision.HIGHEST)
        result = result + carried[:, :, None] * reached
        last_seg = seg_blk[block - 1]
        keeping = jnp.where(last_seg == prev_seg, jnp.exp(cumulative[block - 1]), 0.0)
        tail_weight = jnp.where((seg_blk == last_seg)[:, None], jnp.exp(cumulative[block - 1][None, :] - cumulative), 0.0)
        loaded = lax.optimization_barrier(
            (tail_weight[:, :, None] * b_blk.astype(jnp.float32)[:, None, :]).astype(jnp.bfloat16)).astype(jnp.float32)
        state_out = keeping[:, None, None] * state_in + jnp.einsum('shn,shp->hnp', loaded, driven)
        return (state_out, last_seg), result

    stacked = (inputs_x.reshape(count, block, heads, width), step_size.reshape(count, block, heads),
               log_decay.reshape(count, block, heads), b_rows.reshape(count, block, b_rows.shape[1]),
               c_rows.reshape(count, block, c_rows.shape[1]), seg_rows.reshape(count, block))
    (state_end, last_seen), results = lax.scan(one_block, (state_start, seg_rows[0]), stacked)
    return results.reshape(length, heads, width)


def place_rows(rows_arr, stretch_place):
    shaped = rows_arr.reshape((STRETCHES, STRETCH_LEN) + rows_arr.shape[1:])
    return jnp.zeros_like(shaped).at[stretch_place].set(shaped).reshape(rows_arr.shape)


def reference(stretch_x, stretch_bc, stretch_dt, stretch_q, stretch_kv, stretch_place, segment_ids, ssm_rate, dt_bias, skip_gain):
    packed_x = place_rows(stretch_x, stretch_place)
    packed_bc = place_rows(stretch_bc, stretch_place)
    packed_dt = place_rows(stretch_dt, stretch_place)
    packed_q = place_rows(stretch_q, stretch_place)
    packed_kv = place_rows(stretch_kv, stretch_place)
    step_all = jax.nn.softplus(packed_dt.astype(jnp.float32) + dt_bias[None, :])
    decay_all = -ssm_rate[None, :] * step_all
    per_group = SSM_HEADS // GROUPS
    b_all = packed_bc[:, 0]
    c_all = packed_bc[:, 1]

    def group_out(group):
        first = (group * per_group).astype(jnp.int32)
        group_x = lax.dynamic_slice_in_dim(packed_x, first * HEAD_DIM, per_group * HEAD_DIM, 1).reshape(
            TOKENS, per_group, HEAD_DIM)
        size_cols = lax.dynamic_slice_in_dim(step_all, first, per_group, 1)
        decay_cols = lax.dynamic_slice_in_dim(decay_all, first, per_group, 1)
        b_rows = lax.dynamic_slice_in_dim(b_all, (group * STATE).astype(jnp.int32), STATE, 1)
        c_rows = lax.dynamic_slice_in_dim(c_all, (group * STATE).astype(jnp.int32), STATE, 1)
        scanned = block_scan(group_x, size_cols, decay_cols, b_rows, c_rows, segment_ids, BLOCK)
        gains = lax.dynamic_slice_in_dim(skip_gain, first, per_group, 0)
        summed = scanned + gains[None, :, None] * group_x.astype(jnp.float32)
        return summed.astype(jnp.bfloat16).reshape(TOKENS, per_group * HEAD_DIM)

    groups_out = lax.map(group_out, jnp.arange(GROUPS, dtype=jnp.int32))
    ssm_out = jnp.transpose(groups_out, (1, 0, 2)).reshape(TOKENS, SSM_HEADS * HEAD_DIM)

    group_size = Q_HEADS // KV_HEADS
    span = math.gcd(TOKENS, 512)
    scale = ATT_DIM ** -0.5
    positions = jnp.arange(TOKENS, dtype=jnp.int32)
    queries_all = packed_q.reshape(TOKENS, KV_HEADS, group_size, ATT_DIM)
    keys_all = packed_kv[:, 0].reshape(TOKENS, KV_HEADS, ATT_DIM)
    values_all = packed_kv[:, 1].reshape(TOKENS, KV_HEADS, ATT_DIM)

    def per_head(head):
        queries = lax.dynamic_index_in_dim(queries_all, head, 1, False)
        keys = lax.dynamic_index_in_dim(keys_all, head, 1, False).astype(jnp.float32)
        values = lax.dynamic_index_in_dim(values_all, head, 1, False).astype(jnp.float32)

        def per_block(start):
            q_blk = lax.dynamic_slice_in_dim(queries, start, span, 0).astype(jnp.float32)
            scores = jnp.einsum('tgd,sd->tgs', q_blk, keys) * scale
            q_pos = start + jnp.arange(span, dtype=jnp.int32)
            q_seg = lax.dynamic_slice_in_dim(segment_ids, start, span, 0)
            allowed = (positions[None, :] <= q_pos[:, None]) & (segment_ids[None, :] == q_seg[:, None])
            scores = jnp.where(allowed[:, None, :], scores, NEG_BIG)
            highest = jnp.max(scores, axis=-1, keepdims=True)
            expo = jnp.where(allowed[:, None, :], jnp.exp(scores - highest), 0.0)
            totals = jnp.sum(expo, axis=-1)
            rounded = lax.optimization_barrier(expo.astype(jnp.bfloat16)).astype(jnp.float32)
            mixed = jnp.einsum('tgs,sd->tgd', rounded, values)
            return mixed / totals[..., None]

        starts = jnp.arange(TOKENS // span, dtype=jnp.int32) * span
        blocks = lax.map(per_block, starts)
        return blocks.reshape(TOKENS, group_size, ATT_DIM)

    all_heads = lax.map(per_head, jnp.arange(KV_HEADS, dtype=jnp.int32))
    attn_out = jnp.transpose(all_heads, (1, 0, 2, 3)).reshape(TOKENS, Q_HEADS * ATT_DIM).astype(jnp.bfloat16)
    return ssm_out, attn_out
```

```python
import functools

import jax
import jax.numpy as jnp
from jax import lax
from jax.experimental import pallas as pl
from jax.experimental.pallas import tpu as pltpu
from jax.sharding import PartitionSpec as P

SSM_HEADS = 256
HEAD_DIM = 64
STATE = 256
GROUPS = 8
Q_HEADS = 64
KV_HEADS = 8
ATT_DIM = 128
LEN = 64
SEQ = 16
MP = 8
STRETCHES = 128
CHUNK = 512
HALF = 256
PER = CHUNK // LEN
LANES = 128
DOCS = 6
TOKENS = 8192

X_ROWS = LEN
BC_ROWS = 16
Q_ROWS = 32
BC_AT = X_ROWS
Q_AT = BC_AT + BC_ROWS
INFO_AT = Q_AT + Q_ROWS
HOP_ROWS = INFO_AT + 16
OWN_ROWS = X_ROWS + BC_ROWS
K_AT, V_AT, B_AT, DT_AT, G_ROWS = 0, 64, 128, 256, 272
NEG_BIG = -1e30
F32 = jnp.float32
BF16 = jnp.bfloat16
MIB = 1 << 20


def params(mib):
    return pltpu.CompilerParams(vmem_limit_bytes=mib * MIB)


def pack_kernel(x_ref, b_ref, c_ref, q_ref, k_ref, v_ref, dt_ref, info_ref, hop_ref, kvb_ref):
    info = info_ref[0:1, :]
    row = lax.broadcasted_iota(jnp.int32, (16, LANES), 0)
    tile = jnp.where(row == 0, jnp.broadcast_to(info, (16, LANES)), 0.0).astype(BF16)
    for s in range(SEQ):
        hop_ref[s, 0, 0:X_ROWS, :] = x_ref[:, s * LANES : (s + 1) * LANES]
        toks = pl.ds((s // 4) * 16, 16)
        source = b_ref if s % 4 < 2 else c_ref
        col = (s % 2) * LANES
        hop_ref[s, 0, BC_AT : BC_AT + BC_ROWS, :] = source[toks, col : col + LANES]
        hop_ref[s, 0, Q_AT : Q_AT + Q_ROWS, :] = q_ref[
            pl.ds((s % 2) * Q_ROWS, Q_ROWS), (s // 2) * LANES : (s // 2 + 1) * LANES
        ]
        hop_ref[s, 0, INFO_AT:HOP_ROWS, :] = tile
    kvb_ref[0, K_AT : K_AT + LEN, :] = k_ref[...]
    kvb_ref[0, V_AT : V_AT + LEN, :] = v_ref[...]
    kvb_ref[0, B_AT : B_AT + LEN, :] = b_ref[:, 0:LANES]
    kvb_ref[0, B_AT + LEN : B_AT + 2 * LEN, :] = b_ref[:, LANES : 2 * LANES]
    kvb_ref[0, DT_AT:G_ROWS, :] = dt_ref[...]


def pack(x, b, c, q, k, v, dt_rows, info):
    cols = lambda rows, width: pl.BlockSpec((rows, width), lambda m: (0, m))
    return pl.pallas_call(
        pack_kernel,
        grid=(MP,),
        in_specs=[
            cols(LEN, SEQ * LANES),
            cols(LEN, STATE),
            cols(LEN, STATE),
            cols(LEN, PER * LANES),
            cols(LEN, ATT_DIM),
            cols(LEN, ATT_DIM),
            pl.BlockSpec((16, LANES), lambda m: (m, 0)),
            pl.BlockSpec((8, LANES), lambda m: (0, 0)),
        ],
        out_specs=[
            pl.BlockSpec((SEQ, 1, HOP_ROWS, LANES), lambda m: (0, m, 0, 0)),
            pl.BlockSpec((1, G_ROWS, LANES), lambda m: (m, 0, 0)),
        ],
        out_shape=[
            jax.ShapeDtypeStruct((SEQ, MP, HOP_ROWS, LANES), BF16),
            jax.ShapeDtypeStruct((MP, G_ROWS, LANES), BF16),
        ],
        compiler_params=params(32),
        cost_estimate=pl.CostEstimate(flops=0, bytes_accessed=9 * MIB, transcendentals=0),
        name="pack",
    )(x, b, c, q, k, v, dt_rows, info)


def place_kernel(inv_ref, hop_ref, out_ref, sem):
    def start(p, carry):
        pltpu.make_async_copy(
            hop_ref.at[inv_ref[p], pl.ds(0, OWN_ROWS)], out_ref.at[p], sem
        ).start()
        return carry

    lax.fori_loop(0, STRETCHES, start, 0)
    pltpu.make_async_copy(out_ref, out_ref, sem).wait()


def place(inv, hop):
    return pl.pallas_call(
        place_kernel,
        grid_spec=pltpu.PrefetchScalarGridSpec(
            num_scalar_prefetch=1,
            grid=(),
            in_specs=[pl.BlockSpec(memory_space=pl.ANY)],
            out_specs=pl.BlockSpec(memory_space=pl.ANY),
            scratch_shapes=[pltpu.SemaphoreType.DMA],
        ),
        out_shape=jax.ShapeDtypeStruct((STRETCHES, OWN_ROWS, LANES), BF16),
        cost_estimate=pl.CostEstimate(flops=0, bytes_accessed=6 * MIB, transcendentals=0),
        name="place",
    )(inv, hop)


def doc_start(bounds_ref, pos):
    first = jnp.zeros_like(pos)
    for v in range(1, DOCS):
        first = jnp.maximum(first, jnp.where(bounds_ref[v] <= pos, bounds_ref[v], 0))
    return first


def next_doc(bounds_ref, pos):
    after = jnp.full_like(pos, TOKENS)
    for v in range(1, DOCS):
        after = jnp.minimum(after, jnp.where(bounds_ref[v] > pos, bounds_ref[v], TOKENS))
    return after


def running_sums(rows):
    width = rows.shape[1]
    upper = lax.broadcasted_iota(jnp.int32, (width, width), 0) <= lax.broadcasted_iota(
        jnp.int32, (width, width), 1
    )
    return lax.dot(
        rows, upper.astype(F32), precision=lax.Precision.HIGHEST, preferred_element_type=F32
    )


def mid_kernel(
    inv_ref,
    bounds_ref,
    gath_hbm,
    hop_hbm,
    step_ref,
    decay_ref,
    out_ref,
    gath,
    hop,
    sums,
    state,
    peak,
    total,
    acc,
    sem_g,
    sem_h,
):
    def start(p, carry):
        src = inv_ref[p]
        pltpu.make_async_copy(gath_hbm.at[src, pl.ds(0, DT_AT)], gath.at[p], sem_g).start()
        pltpu.make_async_copy(hop_hbm.at[src, pl.ds(0, INFO_AT)], hop.at[p], sem_h).start()
        return carry

    lax.fori_loop(0, STRETCHES, start, 0)
    sums[...] = running_sums(decay_ref[...].reshape(SEQ * 8, CHUNK)).reshape(SEQ, 8, CHUNK)
    state[...] = jnp.zeros_like(state)
    pltpu.make_async_copy(gath, gath, sem_g).wait()
    pltpu.make_async_copy(hop, hop, sem_h).wait()

    lane = lax.broadcasted_iota(jnp.int32, (1, LANES), 1)
    first_head = lane < HEAD_DIM

    def scan_chunk(c, carry):
        start_pos = c * CHUNK
        span = pl.ds(c * PER, PER)
        last_doc = doc_start(bounds_ref, start_pos + CHUNK - 1)
        log_sum = sums[c]
        log_end = log_sum[:, CHUNK - 1 : CHUNK]
        pos = lax.broadcasted_iota(jnp.int32, (8, CHUNK), 1) + start_pos
        weight = jnp.where(pos >= last_doc, step_ref[c] * jnp.exp(log_end - log_sum), 0.0)
        weight = jnp.transpose(weight)
        weight = jnp.where(first_head, weight[:, 0:1], weight[:, 1:2])
        xs = hop[span, 0:X_ROWS, :].reshape(CHUNK, LANES)
        driven = (weight * xs.astype(F32)).astype(BF16)
        keep = jnp.where(last_doc < start_pos, jnp.exp(log_end), 0.0)
        keep = jnp.where(first_head, keep[0:1, :], keep[1:2, :])
        out_ref[c, 0:STATE, :] = state[...].astype(BF16)
        for part in range(2):
            at = B_AT + part * LEN
            b_part = gath[span, at : at + LEN, :].reshape(CHUNK, LANES)
            added = lax.dot_general(
                b_part, driven, (((0,), (0,)), ((), ())), preferred_element_type=F32
            )
            rows = pl.ds(part * LANES, LANES)
            state[rows, :] = keep * state[rows, :] + added
        return carry

    lax.fori_loop(0, SEQ, scan_chunk, 0)

    half = bounds_ref[DOCS]
    q_rows = PER * Q_ROWS
    row = lax.broadcasted_iota(jnp.int32, (q_rows, 1), 0)
    in_chunk = (row // Q_ROWS) * LEN + half * Q_ROWS + row % Q_ROWS
    key_at = lax.broadcasted_iota(jnp.int32, (q_rows, CHUNK), 1)
    scale = ATT_DIM**-0.5 * 1.4426950408889634

    def attend_chunk(i, carry):
        span = pl.ds(i * PER, PER)
        queries = hop[span, Q_AT : Q_AT + Q_ROWS, :].reshape(q_rows, ATT_DIM)
        q_pos = i * CHUNK + in_chunk
        q_doc = doc_start(bounds_ref, q_pos)

        def scores_of(j):
            keys = gath[pl.ds(j * PER, PER), K_AT : K_AT + LEN, :].reshape(CHUNK, ATT_DIM)
            dots = lax.dot_general(
                queries, keys, (((1,), (1,)), ((), ())), preferred_element_type=F32
            )
            return dots * scale

        def mixed(probs, j):
            values = gath[pl.ds(j * PER, PER), V_AT : V_AT + LEN, :].reshape(CHUNK, ATT_DIM)
            return jnp.dot(probs.astype(BF16), values, preferred_element_type=F32)

        allowed = (key_at <= in_chunk) & (key_at >= q_doc - i * CHUNK)
        scores = jnp.where(allowed, scores_of(i), NEG_BIG)
        top = jnp.max(scores, axis=1, keepdims=True)
        probs = jnp.exp2(scores - top)
        peak[...] = top
        total[...] = jnp.sum(probs, axis=1, keepdims=True)
        acc[...] = mixed(probs, i)

        def one_tile(j, inner):
            scores = jnp.where(key_at >= q_doc - j * CHUNK, scores_of(j), NEG_BIG)
            old = peak[...]
            top = jnp.maximum(old, jnp.max(scores, axis=1, keepdims=True))
            probs = jnp.exp2(scores - top)
            factor = jnp.exp2(old - top)
            peak[...] = top
            total[...] = total[...] * factor + jnp.sum(probs, axis=1, keepdims=True)
            acc[...] = acc[...] * factor + mixed(probs, j)
            return inner

        lax.fori_loop(doc_start(bounds_ref, i * CHUNK) // CHUNK, i, one_tile, 0)
        out_ref[i, STATE:CHUNK, :] = (acc[...] / total[...]).astype(BF16)
        return carry

    lax.fori_loop(0, SEQ, attend_chunk, 0)


def mid(inv, bounds, gathered, hop, steps, decays):
    whole = lambda *shape: pl.BlockSpec(shape, lambda *_: (0,) * len(shape))
    return pl.pallas_call(
        mid_kernel,
        grid_spec=pltpu.PrefetchScalarGridSpec(
            num_scalar_prefetch=2,
            grid=(1,),
            in_specs=[
                pl.BlockSpec(memory_space=pl.ANY),
                pl.BlockSpec(memory_space=pl.ANY),
                whole(SEQ, 8, CHUNK),
                whole(SEQ, 8, CHUNK),
            ],
            out_specs=whole(SEQ, CHUNK, LANES),
            scratch_shapes=[
                pltpu.VMEM((STRETCHES, DT_AT, LANES), BF16),
                pltpu.VMEM((STRETCHES, INFO_AT, LANES), BF16),
                pltpu.VMEM((SEQ, 8, CHUNK), F32),
                pltpu.VMEM((STATE, LANES), F32),
                pltpu.VMEM((PER * Q_ROWS, 1), F32),
                pltpu.VMEM((PER * Q_ROWS, 1), F32),
                pltpu.VMEM((PER * Q_ROWS, ATT_DIM), F32),
                pltpu.SemaphoreType.DMA,
                pltpu.SemaphoreType.DMA,
            ],
        ),
        out_shape=jax.ShapeDtypeStruct((SEQ, CHUNK, LANES), BF16),
        compiler_params=params(40),
        cost_estimate=pl.CostEstimate(
            flops=8_000_000_000, bytes_accessed=16 * MIB, transcendentals=16 * MIB
        ),
        name="mid",
    )(inv, bounds, gathered, hop, steps, decays)


def own_kernel(
    bounds_ref,
    own_ref,
    state_ref,
    attn_ref,
    step_ref,
    decay_ref,
    gain_ref,
    ssm_ref,
    out_ref,
    proj,
    b_turned,
    grams,
    sums,
):
    pair = pl.program_id(0)
    base = bounds_ref[DOCS + 1] * CHUNK

    @pl.when(pair == 0)
    def _():
        for s in range(SEQ):
            piece = own_ref[s, :, X_ROWS:OWN_ROWS, :]
            proj[:, s // 4, :, (s % 4) * LANES : (s % 4 + 1) * LANES] = piece
        row = lax.broadcasted_iota(jnp.int32, (HALF, 1), 0)
        col = lax.broadcasted_iota(jnp.int32, (HALF, HALF), 1)
        for blk in range(2):
            part = proj[blk * 4 : blk * 4 + 4].reshape(HALF, 2 * STATE)
            b_blk, c_blk = part[:, :STATE], part[:, STATE:]
            gram = lax.dot_general(
                c_blk, b_blk, (((1,), (1,)), ((), ())), preferred_element_type=F32
            )
            pos = base + blk * HALF + row
            first = doc_start(bounds_ref, pos) - (base + blk * HALF)
            grams[blk] = jnp.where((col <= row) & (col >= first), gram, 0.0)
            if blk == 0:
                b_turned[...] = jnp.transpose(b_blk.astype(F32)).astype(BF16)
            part_sums = running_sums(
                decay_ref[:, :, blk * HALF : (blk + 1) * HALF].reshape(SEQ * 8, HALF)
            )
            sums[:, :, blk * HALF : (blk + 1) * HALF] = part_sums.reshape(SEQ, 8, HALF)
        for s in range(SEQ):
            for st in range(PER):
                at = st * LEN + (s % 2) * Q_ROWS
                out_ref[at : at + Q_ROWS, (s // 2) * LANES : (s // 2 + 1) * LANES] = attn_ref[
                    s, st * Q_ROWS : (st + 1) * Q_ROWS, :
                ]

    lane = lax.broadcasted_iota(jnp.int32, (1, LANES), 1)
    first_head = lane < HEAD_DIM
    both = lambda cols: jnp.where(first_head, cols[:, 0:1], cols[:, 1:2])
    log_sum = sums[pair]
    step = step_ref[pair]
    pos = lax.broadcasted_iota(jnp.int32, (8, CHUNK), 1) + base
    mid_pos = base + HALF - 1
    log_half = log_sum[:, HALF - 1 : HALF]
    load = jnp.where(pos >= doc_start(bounds_ref, mid_pos), jnp.exp(log_half - log_sum), 0.0)
    load = step * load
    reach_end = jnp.where(
        pos <= mid_pos,
        jnp.where(base > 0, next_doc(bounds_ref, base - 1), 0),
        next_doc(bounds_ref, mid_pos),
    )
    reach = jnp.where(pos < reach_end, jnp.exp(log_sum), 0.0)
    keep = jnp.where(
        (base > 0) & (doc_start(bounds_ref, mid_pos) < base), jnp.exp(log_half), 0.0
    )
    keep = jnp.where(first_head, keep[0:1, :], keep[1:2, :])
    step_col = jnp.transpose(step)
    sum_col = jnp.transpose(log_sum)
    reach_col = jnp.transpose(reach)
    load_col = jnp.transpose(load[:, :HALF])
    gain = gain_ref[pair][0:1, :]

    state_in = state_ref[0]
    for blk in range(2):
        rows = slice(blk * HALF, (blk + 1) * HALF)
        xs = own_ref[pair, blk * 4 : blk * 4 + 4, 0:X_ROWS, :].reshape(HALF, LANES).astype(F32)
        driven = (both(step_col[rows]) * xs).astype(BF16)
        c_blk = proj[blk * 4 : blk * 4 + 4, :, :, STATE:].reshape(HALF, STATE)
        gram = grams[blk]
        inner = []
        for head in range(2):
            gap = sum_col[rows, head : head + 1] - log_sum[head : head + 1, rows]
            mixing = (gram * jnp.exp(jnp.minimum(gap, 0.0))).astype(BF16)
            inner.append(jnp.dot(mixing, driven, preferred_element_type=F32))
        result = jnp.where(first_head, inner[0], inner[1])
        reached = jnp.dot(c_blk, state_in, preferred_element_type=F32)
        result = result + both(reach_col[rows]) * reached + gain * xs
        ssm_ref[rows, :] = result.astype(BF16)
        if blk == 0:
            loaded = (both(load_col) * xs).astype(BF16)
            added = jnp.dot(b_turned[...], loaded, preferred_element_type=F32)
            state_in = (keep * state_in.astype(F32) + added).astype(BF16)


def own(bounds, rows, mixed, steps, decays, gains):
    whole = lambda *shape: pl.BlockSpec(shape, lambda *_: (0,) * len(shape))
    return pl.pallas_call(
        own_kernel,
        grid_spec=pltpu.PrefetchScalarGridSpec(
            num_scalar_prefetch=1,
            grid=(SEQ,),
            in_specs=[
                whole(SEQ, PER, OWN_ROWS, LANES),
                pl.BlockSpec((1, STATE, LANES), lambda p, *_: (p, 0, 0)),
                pl.BlockSpec((SEQ, HALF, LANES), lambda p, *_: (0, 1, 0)),
                whole(SEQ, 8, CHUNK),
                whole(SEQ, 8, CHUNK),
                whole(SEQ, 8, LANES),
            ],
            out_specs=[
                pl.BlockSpec((CHUNK, LANES), lambda p, *_: (0, p)),
                whole(CHUNK, PER * LANES),
            ],
            scratch_shapes=[
                pltpu.VMEM((PER, 4, 16, 2 * STATE), BF16),
                pltpu.VMEM((STATE, HALF), BF16),
                pltpu.VMEM((2, HALF, HALF), F32),
                pltpu.VMEM((SEQ, 8, CHUNK), F32),
            ],
        ),
        out_shape=[
            jax.ShapeDtypeStruct((CHUNK, SEQ * LANES), BF16),
            jax.ShapeDtypeStruct((CHUNK, PER * LANES), BF16),
        ],
        compiler_params=params(40),
        cost_estimate=pl.CostEstimate(
            flops=4_000_000_000, bytes_accessed=10 * MIB, transcendentals=4 * MIB
        ),
        name="own",
    )(bounds, rows, mixed, mixed, steps, decays, gains)


def fold_steps(raw, bias, rate):
    step = jax.nn.softplus(raw.astype(F32) + bias[..., None])
    decay = -rate[..., None] * step
    widen = lambda rows: jnp.pad(rows, ((0, 0), (0, 6), (0, 0)))
    return widen(step), widen(decay)


def shards(
    stretch_x,
    stretch_bc,
    stretch_dt,
    stretch_q,
    stretch_kv,
    stretch_place,
    segment_ids,
    ssm_rate,
    dt_bias,
    skip_gain,
):
    seq_index = lax.axis_index("seq")
    mp_index = lax.axis_index("mp")
    exchange = functools.partial(lax.all_to_all, split_axis=0, concat_axis=0, tiled=True)

    my_docs = lax.dynamic_slice_in_dim(segment_ids, mp_index * LEN, LEN, 0)
    my_place = lax.dynamic_slice_in_dim(stretch_place, mp_index, 1, 0)
    info = jnp.concatenate([my_docs, my_place, jnp.zeros((LEN - 1,), jnp.int32)])
    info = jnp.broadcast_to(info.astype(F32)[None, :], (8, LANES))
    to_heads, to_groups = pack(
        stretch_x,
        stretch_bc[:, 0, :],
        stretch_bc[:, 1, :],
        stretch_q,
        stretch_kv[:, 0, :],
        stretch_kv[:, 1, :],
        stretch_dt.T.reshape(STRETCHES, LANES),
        info,
    )
    group_rows = exchange(to_groups, "mp")
    gathered = lax.all_gather(group_rows, "seq", axis=0, tiled=True)
    hop = exchange(to_heads.reshape(STRETCHES, HOP_ROWS, LANES), ("seq", "mp"))

    told = hop[:, INFO_AT, :].astype(jnp.int32)
    places, docs = told[:, LEN], told[:, :LEN]
    order = jnp.arange(STRETCHES, dtype=jnp.int32)
    inv = jnp.sum(jnp.where(places[None, :] == order[:, None], order[None, :], 0), axis=1)
    bounds = jnp.stack(
        [jnp.sum((docs < v).astype(jnp.int32)) for v in range(DOCS)]
        + [seq_index % 2, seq_index]
    )
    own_rows = exchange(place(inv, hop).reshape(SEQ, PER * OWN_ROWS, LANES), "seq")

    raw = gathered[:, DT_AT:G_ROWS, :]
    mine = lax.dynamic_index_in_dim(raw, seq_index, 1, False)
    chosen = (places[None, :] == order[:, None]).astype(BF16)
    pick = functools.partial(jnp.dot, preferred_element_type=F32)
    mine = pick(chosen, mine).reshape(SEQ, PER, 2, LEN)
    mine = jnp.transpose(mine, (0, 2, 1, 3)).reshape(SEQ, 2, CHUNK)
    heads = lambda vec, first, count: lax.dynamic_slice_in_dim(vec, first, count, 0)
    group_first = mp_index * (SSM_HEADS // GROUPS)
    head_first = group_first + seq_index * 2
    steps, decays = fold_steps(
        mine, heads(dt_bias, head_first, 2)[None], heads(ssm_rate, head_first, 2)[None]
    )
    mixed = exchange(mid(inv, bounds, gathered, hop, steps, decays), "seq")

    ours = pick(heads(chosen, seq_index * PER, PER), raw.reshape(STRETCHES, 16 * LANES))
    ours = ours.reshape(PER, SEQ, 2, LEN)
    ours = jnp.transpose(ours, (1, 2, 0, 3)).reshape(SEQ, 2, CHUNK)
    of_group = lambda vec: heads(vec, group_first, SSM_HEADS // GROUPS).reshape(SEQ, 2)
    own_steps, own_decays = fold_steps(ours, of_group(dt_bias), of_group(ssm_rate))
    gains = jnp.broadcast_to(
        jnp.repeat(of_group(skip_gain), HEAD_DIM, axis=1)[:, None, :], (SEQ, 8, LANES)
    )
    return own(
        bounds,
        own_rows.reshape(SEQ, PER, OWN_ROWS, LANES),
        mixed,
        own_steps,
        own_decays,
        gains,
    )


def solution(mesh):
    return jax.shard_map(
        shards,
        mesh=mesh,
        in_specs=(
            P(("seq", "mp"), None),
            P(("seq", "mp"), None, None),
            P(("seq", "mp"), None),
            P(("seq", "mp"), None),
            P(("seq", "mp"), None, None),
            P("seq"),
            P("seq"),
            P(),
            P(),
            P(),
        ),
        out_specs=(P("seq", "mp"), P("seq", "mp")),
        check_vma=False,
    )
```

```python
import functools

import jax
import jax.numpy as jnp
from jax import lax
from jax.experimental import pallas as pl
from jax.experimental.pallas import tpu as pltpu
from jax.sharding import PartitionSpec as P

SSM_HEADS = 256
HEAD_DIM = 64
STATE = 256
GROUPS = 8
Q_HEADS = 64
KV_HEADS = 8
ATT_DIM = 128
LEN = 64
SEQ = 16
MP = 8
STRETCHES = 128
CHUNK = 512
HALF = 256
PER = CHUNK // LEN
LANES = 128
DOCS = 6
TOKENS = 8192

X_ROWS = LEN
BC_ROWS = 16
Q_ROWS = 32
BC_AT = X_ROWS
Q_AT = BC_AT + BC_ROWS
INFO_AT = Q_AT + Q_ROWS
HOP_ROWS = INFO_AT + 16
OWN_ROWS = X_ROWS + BC_ROWS
OWNER_ROWS = PER * OWN_ROWS + 16
K_AT, V_AT, G_ROWS = 0, 64, 128
GROUP_HEADS = SSM_HEADS // GROUPS
PAIRS = 2
NEG_BIG = -1e30
F32 = jnp.float32
BF16 = jnp.bfloat16
MIB = 1 << 20


def params(mib):
    return pltpu.CompilerParams(vmem_limit_bytes=mib * MIB)


def pack_kernel(x_ref, bc_ref, q_ref, dt_ref, info_ref, hop_ref):
    row = lax.broadcasted_iota(jnp.int32, (16, LANES), 0)
    told = jnp.where(row == 0, jnp.broadcast_to(info_ref[0:1, :], (16, LANES)), 0.0)
    raw = dt_ref[...].astype(F32)
    for s in range(SEQ):
        hop_ref[s, 0, 0:X_ROWS, :] = x_ref[:, s * LANES : (s + 1) * LANES]
        col = (s % 2) * LANES
        hop_ref[s, 0, BC_AT : BC_AT + BC_ROWS, :] = bc_ref[
            pl.ds((s // 4) * 16, 16), (s % 4) // 2, col : col + LANES
        ]
        hop_ref[s, 0, Q_AT : Q_AT + Q_ROWS, :] = q_ref[
            pl.ds((s % 2) * Q_ROWS, Q_ROWS), (s // 2) * LANES : (s // 2 + 1) * LANES
        ]
        tile = jnp.where(row == 1, jnp.broadcast_to(raw[s : s + 1, :], (16, LANES)), told)
        hop_ref[s, 0, INFO_AT:HOP_ROWS, :] = tile.astype(BF16)


def pack(x, bc, q, dt_rows, info):
    cols = lambda width: pl.BlockSpec((LEN, width), lambda m: (0, m))
    return pl.pallas_call(
        pack_kernel,
        grid=(MP,),
        in_specs=[
            cols(SEQ * LANES),
            pl.BlockSpec((LEN, 2, STATE), lambda m: (0, 0, m)),
            cols(PER * LANES),
            pl.BlockSpec((16, LANES), lambda m: (m, 0)),
            pl.BlockSpec((8, LANES), lambda m: (0, 0)),
        ],
        out_specs=pl.BlockSpec((SEQ, 1, HOP_ROWS, LANES), lambda m: (0, m, 0, 0)),
        out_shape=jax.ShapeDtypeStruct((SEQ, MP, HOP_ROWS, LANES), BF16),
        compiler_params=params(32),
        cost_estimate=pl.CostEstimate(flops=0, bytes_accessed=9 * MIB, transcendentals=0),
        name="pack",
    )(x, bc, q, dt_rows, info)


def pack_kv_kernel(kv_ref, out_ref):
    for m in range(MP):
        for half in range(2):
            out_ref[m, half * LEN : (half + 1) * LEN, :] = kv_ref[
                :, half, m * ATT_DIM : (m + 1) * ATT_DIM
            ]


def pack_kv(kv):
    return pl.pallas_call(
        pack_kv_kernel,
        grid=(1,),
        in_specs=[pl.BlockSpec((LEN, 2, KV_HEADS * ATT_DIM), lambda _: (0, 0, 0))],
        out_specs=pl.BlockSpec((MP, G_ROWS, LANES), lambda _: (0, 0, 0)),
        out_shape=jax.ShapeDtypeStruct((MP, G_ROWS, LANES), BF16),
        compiler_params=params(16),
        name="pack_kv",
    )(kv)


def place_kernel(inv_ref, hop_ref, out_ref, q_ref):
    lane = lax.broadcasted_iota(jnp.int32, (1, LANES), 1)
    early = lane < LEN
    row = lax.broadcasted_iota(jnp.int32, (16, LANES), 0)

    def chunk(c, carry):
        raw = []
        for k in range(PER):
            src = inv_ref[c * PER + k]
            out_ref[c, k * OWN_ROWS : (k + 1) * OWN_ROWS, :] = hop_ref[src, 0:OWN_ROWS, :]
            q_ref[c, k * Q_ROWS : (k + 1) * Q_ROWS, :] = hop_ref[src, Q_AT : Q_AT + Q_ROWS, :]
            raw.append(hop_ref[src, INFO_AT:HOP_ROWS, :].astype(F32)[1:2, :])
        turned = [jnp.roll(r, LEN, axis=1) for r in raw]
        tile = jnp.zeros((16, LANES), F32)
        for q in range(4):
            first = jnp.where(early, raw[2 * q], turned[2 * q + 1])
            second = jnp.where(early, turned[2 * q], raw[2 * q + 1])
            tile = jnp.where(row == q, first, jnp.where(row == 4 + q, second, tile))
        out_ref[c, PER * OWN_ROWS : OWNER_ROWS, :] = tile.astype(BF16)
        return carry

    lax.fori_loop(0, SEQ, chunk, 0)


def place(inv, hop):
    return pl.pallas_call(
        place_kernel,
        grid_spec=pltpu.PrefetchScalarGridSpec(
            num_scalar_prefetch=1,
            grid=(1,),
            in_specs=[pl.BlockSpec((STRETCHES, HOP_ROWS, LANES), lambda *_: (0, 0, 0))],
            out_specs=[
                pl.BlockSpec((SEQ, OWNER_ROWS, LANES), lambda *_: (0, 0, 0)),
                pl.BlockSpec((SEQ, PER * Q_ROWS, LANES), lambda *_: (0, 0, 0)),
            ],
        ),
        out_shape=[
            jax.ShapeDtypeStruct((SEQ, OWNER_ROWS, LANES), BF16),
            jax.ShapeDtypeStruct((SEQ, PER * Q_ROWS, LANES), BF16),
        ],
        compiler_params=params(24),
        cost_estimate=pl.CostEstimate(flops=0, bytes_accessed=6 * MIB, transcendentals=0),
        name="place",
    )(inv, hop)


def doc_start(bounds_ref, pos):
    first = jnp.zeros_like(pos)
    for v in range(1, DOCS):
        first = jnp.maximum(first, jnp.where(bounds_ref[v] <= pos, bounds_ref[v], 0))
    return first


def next_doc(bounds_ref, pos):
    after = jnp.full_like(pos, TOKENS)
    for v in range(1, DOCS):
        after = jnp.minimum(after, jnp.where(bounds_ref[v] > pos, bounds_ref[v], TOKENS))
    return after


def running_sums(rows):
    width = rows.shape[1]
    upper = lax.broadcasted_iota(jnp.int32, (width, width), 0) <= lax.broadcasted_iota(
        jnp.int32, (width, width), 1
    )
    return lax.dot(
        rows, upper.astype(F32), precision=lax.Precision.HIGHEST, preferred_element_type=F32
    )


def whole(*shape):
    return pl.BlockSpec(shape, lambda *_: (0,) * len(shape))


SUM_ROWS = 16


def attend_kernel(
    inv_ref, bounds_ref, kv_hbm, q_hbm, out_ref, kv_ref, q_ref, keys_all, turned, peak, acc, top_far, acc_far, sems
):
    kv_copy = pltpu.make_async_copy(kv_hbm, kv_ref, sems.at[0])
    q_copy = pltpu.make_async_copy(q_hbm, q_ref, sems.at[1])
    kv_copy.start()
    q_copy.start()
    half = bounds_ref[DOCS]
    q_rows = PER * Q_ROWS

    def arrange(i, carry):
        values = []
        for k in range(PER):
            src = inv_ref[i * PER + k]
            keys_all[pl.ds(i * CHUNK + k * LEN, LEN), :] = kv_ref[src, K_AT : K_AT + LEN, :]
            values.append(kv_ref[src, V_AT : V_AT + LEN, :])
        turned[i, 0:ATT_DIM, :] = jnp.transpose(jnp.concatenate(values, axis=0))
        turned[i, ATT_DIM : ATT_DIM + SUM_ROWS, :] = jnp.ones((SUM_ROWS, CHUNK), BF16)
        return carry

    kv_copy.wait()
    lax.fori_loop(0, SEQ, arrange, 0, unroll=2)
    q_copy.wait()

    row = lax.broadcasted_iota(jnp.int32, (1, q_rows), 1)
    in_chunk = (row // Q_ROWS) * LEN + half * Q_ROWS + row % Q_ROWS
    key_at = lax.broadcasted_iota(jnp.int32, (CHUNK, q_rows), 0)
    scale = ATT_DIM**-0.5 * 1.4426950408889634

    def scores_of(queries, j):
        keys = keys_all[pl.ds(pl.multiple_of(j * CHUNK, CHUNK), CHUNK), :]
        return lax.dot_general(
            keys, queries, (((1,), (1,)), ((), ())), preferred_element_type=F32
        )

    def mixed(scores, top, j):
        probs = jnp.exp2((scores - top) * scale)
        return jnp.dot(turned[j], probs.astype(BF16), preferred_element_type=F32)

    def peak_of(scores):
        return jnp.max(scores, axis=0, keepdims=True)

    def near_tiles(i, carry):
        queries = q_ref[i]
        first = doc_start(bounds_ref, i * CHUNK + in_chunk) - i * CHUNK
        before = jnp.maximum(i - 1, 0)
        own = (key_at <= in_chunk) & (key_at >= first)
        here = jnp.where(own, scores_of(queries, i), NEG_BIG)
        there = jnp.where(key_at >= first + CHUNK, scores_of(queries, before), NEG_BIG)
        top = jnp.maximum(peak_of(here), peak_of(there))
        peak[i] = top
        acc[i] = mixed(here, top, i) + mixed(there, top, before)
        return carry

    lax.fori_loop(0, SEQ, near_tiles, 0, unroll=2)

    def far_tiles(i, carry):
        first = doc_start(bounds_ref, i * CHUNK) // CHUNK
        last_doc = doc_start(bounds_ref, i * CHUNK + CHUNK - 1)
        end = jnp.maximum(i - 1, first)
        clear = jnp.clip((last_doc + CHUNK - 1) // CHUNK, first, end)
        n_clear = (end - clear) // 2
        clear = end - 2 * n_clear
        n_mask = (clear - first) // 2

        queries = q_ref[i]
        q_doc = doc_start(bounds_ref, i * CHUNK + in_chunk)

        def add_tiles(js, masks):
            old = top_far[...]
            scores = [scores_of(queries, j) for j in js]
            if masks:
                scores = [
                    jnp.where(key_at >= q_doc - j * CHUNK, s, NEG_BIG) for s, j in zip(scores, js)
                ]
            top = old
            for s in scores:
                top = jnp.maximum(top, peak_of(s))
            top_far[...] = top
            added = sum(mixed(s, top, j) for s, j in zip(scores, js))
            acc_far[...] = acc_far[...] * jnp.exp2((old - top) * scale) + added

        top_far[...] = peak[i]
        acc_far[...] = acc[i]

        @pl.when((clear - first) % 2 == 1)
        def _():
            add_tiles([first], True)

        def masked(t, c):
            j = clear - 2 * n_mask + 2 * t
            add_tiles([j, j + 1], True)
            return c

        def plain(t, c):
            j = clear + 2 * t
            add_tiles([j, j + 1], False)
            return c

        lax.fori_loop(0, n_mask, masked, 0)
        lax.fori_loop(0, n_clear, plain, 0)
        acc[i] = acc_far[...]
        return carry

    lax.fori_loop(2, SEQ, far_tiles, 0)

    def finish(i, carry):
        result = acc[i, 0:ATT_DIM, :] / acc[i, ATT_DIM : ATT_DIM + 1, :]
        out_ref[i, STATE:CHUNK, :] = jnp.transpose(result).astype(BF16)
        return carry

    lax.fori_loop(0, SEQ, finish, 0, unroll=4)


def attend(inv, bounds, kv, queries):
    return pl.pallas_call(
        attend_kernel,
        grid_spec=pltpu.PrefetchScalarGridSpec(
            num_scalar_prefetch=2,
            grid=(1,),
            in_specs=[pl.BlockSpec(memory_space=pl.ANY), pl.BlockSpec(memory_space=pl.ANY)],
            out_specs=whole(SEQ, CHUNK, LANES),
            scratch_shapes=[
                pltpu.VMEM((STRETCHES, G_ROWS, LANES), BF16),
                pltpu.VMEM((SEQ, PER * Q_ROWS, LANES), BF16),
                pltpu.VMEM((TOKENS, ATT_DIM), BF16),
                pltpu.VMEM((SEQ, ATT_DIM + SUM_ROWS, CHUNK), BF16),
                pltpu.VMEM((SEQ, 1, PER * Q_ROWS), F32),
                pltpu.VMEM((SEQ, ATT_DIM + SUM_ROWS, PER * Q_ROWS), F32),
                pltpu.VMEM((1, PER * Q_ROWS), F32),
                pltpu.VMEM((ATT_DIM + SUM_ROWS, PER * Q_ROWS), F32),
                pltpu.SemaphoreType.DMA((2,)),
            ],
        ),
        out_shape=jax.ShapeDtypeStruct((SEQ, CHUNK, LANES), BF16),
        compiler_params=params(60),
        cost_estimate=pl.CostEstimate(flops=8_000_000_000, bytes_accessed=6 * MIB, transcendentals=8 * MIB),
        name="attend",
    )(inv, bounds, kv, queries)


def pair_lanes(first, width, rows):
    row = lax.broadcasted_iota(jnp.int32, (rows, width), 0) % GROUP_HEADS
    lane = lax.broadcasted_iota(jnp.int32, (rows, width), 1)
    return (row == first + lane // (width // 2)).astype(BF16)


def as_parts(rows, count):
    left = jnp.transpose(rows)
    parts = []
    for _ in range(count):
        part = left.astype(BF16)
        parts.append(part)
        left = left - part.astype(F32)
    return jnp.concatenate(parts, axis=1)


def spread_heads(parts, pair, width):
    sel = pair_lanes(2 * pair, width, parts.shape[1])
    return jnp.dot(parts, sel, preferred_element_type=F32)


def channels(own_ref, pair):
    parts = [own_ref[pair, st * OWN_ROWS : st * OWN_ROWS + X_ROWS, :] for st in range(PER)]
    return jnp.concatenate(parts, axis=0).astype(F32)


def gather_proj(own_ref, proj, group):
    for tg in range(4):
        for cg in range(2):
            for st in range(PER):
                at = st * OWN_ROWS + X_ROWS
                proj[st, tg, :, cg * LANES : (cg + 1) * LANES] = own_ref[
                    tg * 4 + group * 2 + cg, at : at + BC_ROWS, :
                ]


def softplus(v):
    return jnp.maximum(v, 0.0) + jnp.log1p(jnp.exp(-jnp.abs(v)))


def ends_kernel(bounds_ref, own_ref, bias_ref, rate_ref, out_ref, step_ref, decay_ref, proj, turned, parts):
    base = bounds_ref[DOCS + 1] * CHUNK

    @pl.when(pl.program_id(0) == 0)
    def _():
        for s in range(SEQ):
            tile = own_ref[s, PER * OWN_ROWS : OWNER_ROWS, :].astype(F32)
            for head in range(2):
                for q in range(4):
                    step_ref[2 * s + head : 2 * s + head + 1, q * LANES : (q + 1) * LANES] = tile[
                        4 * head + q : 4 * head + q + 1, :
                    ]
        step_ref[...] = softplus(step_ref[...] + bias_ref[...])
        decay_ref[...] = -rate_ref[...] * step_ref[...]
        gather_proj(own_ref, proj, 0)
        turned[...] = jnp.transpose(proj[...].reshape(CHUNK, STATE))
        log_sum = running_sums(decay_ref[...])
        pos = lax.broadcasted_iota(jnp.int32, (GROUP_HEADS, CHUNK), 1) + base
        last_doc = doc_start(bounds_ref, base + CHUNK - 1)
        load = jnp.exp(log_sum[:, CHUNK - 1 : CHUNK] - log_sum)
        parts[...] = as_parts(jnp.where(pos >= last_doc, step_ref[...] * load, 0.0), 2)

    for k in range(PAIRS):
        pair = pl.program_id(0) * PAIRS + k
        xs = channels(own_ref, pair)
        driven = (spread_heads(parts[...], pair, LANES) * xs).astype(BF16)
        out_ref[k] = jnp.dot(turned[...], driven, preferred_element_type=F32).astype(BF16)


def ends(bounds, rows, biases, rates):
    return pl.pallas_call(
        ends_kernel,
        grid_spec=pltpu.PrefetchScalarGridSpec(
            num_scalar_prefetch=1,
            grid=(SEQ // PAIRS,),
            in_specs=[
                whole(SEQ, OWNER_ROWS, LANES),
                whole(GROUP_HEADS, 1),
                whole(GROUP_HEADS, 1),
            ],
            out_specs=[
                pl.BlockSpec((PAIRS, STATE, LANES), lambda g, *_: (g, 0, 0)),
                whole(GROUP_HEADS, CHUNK),
                whole(GROUP_HEADS, CHUNK),
            ],
            scratch_shapes=[
                pltpu.VMEM((PER, 4, 16, STATE), BF16),
                pltpu.VMEM((STATE, CHUNK), BF16),
                pltpu.VMEM((CHUNK, 2 * GROUP_HEADS), BF16),
            ],
        ),
        out_shape=[
            jax.ShapeDtypeStruct((SEQ, STATE, LANES), BF16),
            jax.ShapeDtypeStruct((GROUP_HEADS, CHUNK), F32),
            jax.ShapeDtypeStruct((GROUP_HEADS, CHUNK), F32),
        ],
        compiler_params=params(24),
        cost_estimate=pl.CostEstimate(
            flops=1_000_000_000, bytes_accessed=4 * MIB, transcendentals=0
        ),
        name="ends",
    )(bounds, rows, biases, rates)


def chain_kernel(bounds_ref, ends_ref, total_ref, both_in, both_out, states, sem):
    state = jnp.zeros((STATE, LANES), F32)
    for c in range(SEQ):
        states[c] = state.astype(BF16)
        if c < SEQ - 1:
            last_doc = doc_start(bounds_ref, jnp.int32((c + 1) * CHUNK - 1))
            keep = jnp.where(last_doc < c * CHUNK, total_ref[c : c + 1, :], 0.0)
            state = keep * state + ends_ref[c].astype(F32)
    copy = pltpu.make_async_copy(states, both_out.at[:, pl.ds(0, STATE), :], sem)
    copy.start()
    copy.wait()


def chain(bounds, arrived, totals, both):
    return pl.pallas_call(
        chain_kernel,
        grid_spec=pltpu.PrefetchScalarGridSpec(
            num_scalar_prefetch=1,
            grid=(1,),
            in_specs=[
                whole(SEQ, STATE, LANES),
                whole(SEQ, LANES),
                pl.BlockSpec(memory_space=pl.ANY),
            ],
            out_specs=pl.BlockSpec(memory_space=pl.ANY),
            scratch_shapes=[pltpu.VMEM((SEQ, STATE, LANES), BF16), pltpu.SemaphoreType.DMA],
        ),
        out_shape=jax.ShapeDtypeStruct((SEQ, CHUNK, LANES), BF16),
        input_output_aliases={3: 0},
        compiler_params=params(60),
        cost_estimate=pl.CostEstimate(flops=0, bytes_accessed=3 * MIB, transcendentals=0),
        name="chain",
    )(bounds, arrived, totals, both)


def inner_kernel(
    bounds_ref,
    own_ref,
    step_ref,
    decay_ref,
    gain_ref,
    out_ref,
    c_out,
    reach_out,
    proj_b,
    proj_c,
    turned,
    grams,
    sums,
    sum_rows,
    sum_parts,
    step_parts,
    load_parts,
    reach_parts,
):
    base = bounds_ref[DOCS + 1] * CHUNK

    @pl.when(pl.program_id(0) == 0)
    def _():
        gather_proj(own_ref, proj_b, 0)
        gather_proj(own_ref, proj_c, 1)
        row = lax.broadcasted_iota(jnp.int32, (HALF, 1), 0)
        col = lax.broadcasted_iota(jnp.int32, (HALF, HALF), 1)
        for blk in range(2):
            b_blk = proj_b[blk * 4 : blk * 4 + 4].reshape(HALF, STATE)
            c_blk = proj_c[blk * 4 : blk * 4 + 4].reshape(HALF, STATE)
            c_out[blk * HALF : (blk + 1) * HALF, :] = c_blk
            gram = lax.dot_general(
                c_blk, b_blk, (((1,), (1,)), ((), ())), preferred_element_type=F32
            )
            start = base + blk * HALF
            first = doc_start(bounds_ref, start + row) - start
            grams[blk] = jnp.where((col <= row) & (col >= first), gram, 0.0)
            if blk == 0:
                turned[...] = jnp.transpose(b_blk)
            sums[:, blk * HALF : (blk + 1) * HALF] = running_sums(
                decay_ref[:, blk * HALF : (blk + 1) * HALF]
            )
        log_sum = sums[...]
        for head in range(GROUP_HEADS):
            sum_rows[head] = log_sum[head : head + 1, :]
        log_half = log_sum[:, HALF - 1 : HALF]
        pos = lax.broadcasted_iota(jnp.int32, (GROUP_HEADS, HALF), 1) + base
        mid_pos = base + HALF - 1
        load = jnp.where(
            pos >= doc_start(bounds_ref, mid_pos), jnp.exp(log_half - log_sum[:, :HALF]), 0.0
        )
        later = jnp.where(
            pos + HALF < next_doc(bounds_ref, mid_pos), jnp.exp(log_sum[:, HALF:]), 0.0
        )
        whole_sum = jnp.concatenate([log_sum[:, :HALF], log_sum[:, HALF:] + log_half], axis=1)
        pos = lax.broadcasted_iota(jnp.int32, (GROUP_HEADS, CHUNK), 1) + base
        reach_end = jnp.where(base > 0, next_doc(bounds_ref, base - 1), 0)
        reach = jnp.where(pos < reach_end, jnp.exp(whole_sum), 0.0)
        sum_parts[...] = as_parts(log_sum, 3)
        step_parts[...] = as_parts(step_ref[...], 2)
        load_parts[...] = as_parts(step_ref[:, :HALF] * load, 2)
        reach_parts[...] = as_parts(later, 2)
        reach_out[...] = as_parts(reach, 2)

    first_head = lax.broadcasted_iota(jnp.int32, (1, LANES), 1) < HEAD_DIM
    quarter = HALF // 2
    for k in range(PAIRS):
        pair = pl.program_id(0) * PAIRS + k
        gain = gain_ref[pair]
        sum_cols = spread_heads(sum_parts[...], pair, 2 * LANES)
        steps = spread_heads(step_parts[...], pair, LANES)
        loads = spread_heads(load_parts[...], pair, LANES)
        reach = spread_heads(reach_parts[...], pair, LANES)
        xs = channels(own_ref, pair)
        driven = (steps * xs).astype(BF16)
        loaded = (loads * xs[:HALF]).astype(BF16)
        state = jnp.dot(turned[...], loaded, preferred_element_type=F32).astype(BF16)
        for blk in range(2):
            for part in range(2):
                at = blk * HALF + part * quarter
                width = (part + 1) * quarter
                heads = []
                for head in range(2):
                    log_row = sum_rows[2 * pair + head][:, blk * HALF : blk * HALF + width]
                    log_col = sum_cols[at : at + quarter, head * LANES : (head + 1) * LANES]
                    log_col = jnp.concatenate([log_col] * (part + 1), axis=1)
                    weight = jnp.exp(jnp.minimum(log_col - log_row, 0.0))
                    gram = grams[blk, part * quarter : (part + 1) * quarter, 0:width]
                    heads.append(
                        jnp.dot(
                            (gram * weight).astype(BF16),
                            driven[blk * HALF : blk * HALF + width],
                            preferred_element_type=F32,
                        )
                    )
                result = jnp.where(first_head, heads[0], heads[1]) + gain * xs[at : at + quarter]
                if blk == 1:
                    c_part = c_out[at : at + quarter, :]
                    result += reach[part * quarter : (part + 1) * quarter] * jnp.dot(
                        c_part, state, preferred_element_type=F32
                    )
                out_ref[at : at + quarter, k * LANES : (k + 1) * LANES] = result


def inner(bounds, rows, steps, decays, gains):
    return pl.pallas_call(
        inner_kernel,
        grid_spec=pltpu.PrefetchScalarGridSpec(
            num_scalar_prefetch=1,
            grid=(SEQ // PAIRS,),
            in_specs=[
                whole(SEQ, OWNER_ROWS, LANES),
                whole(GROUP_HEADS, CHUNK),
                whole(GROUP_HEADS, CHUNK),
                whole(SEQ, 1, LANES),
            ],
            out_specs=[
                pl.BlockSpec((CHUNK, PAIRS * LANES), lambda g, *_: (0, g)),
                whole(CHUNK, STATE),
                whole(CHUNK, 2 * GROUP_HEADS),
            ],
            scratch_shapes=[
                pltpu.VMEM((PER, 4, 16, STATE), BF16),
                pltpu.VMEM((PER, 4, 16, STATE), BF16),
                pltpu.VMEM((STATE, HALF), BF16),
                pltpu.VMEM((2, HALF, HALF), F32),
                pltpu.VMEM((GROUP_HEADS, CHUNK), F32),
                pltpu.VMEM((GROUP_HEADS, 1, CHUNK), F32),
                pltpu.VMEM((CHUNK, 3 * GROUP_HEADS), BF16),
                pltpu.VMEM((CHUNK, 2 * GROUP_HEADS), BF16),
                pltpu.VMEM((HALF, 2 * GROUP_HEADS), BF16),
                pltpu.VMEM((HALF, 2 * GROUP_HEADS), BF16),
            ],
        ),
        out_shape=[
            jax.ShapeDtypeStruct((CHUNK, SEQ * LANES), F32),
            jax.ShapeDtypeStruct((CHUNK, STATE), BF16),
            jax.ShapeDtypeStruct((CHUNK, 2 * GROUP_HEADS), BF16),
        ],
        compiler_params=params(32),
        cost_estimate=pl.CostEstimate(
            flops=4_000_000_000, bytes_accessed=8 * MIB, transcendentals=4 * MIB
        ),
        name="inner",
    )(bounds, rows, steps, decays, gains)


def finish_kernel(state_ref, attn_ref, inner_ref, c_ref, reach_ref, ssm_ref, out_ref):
    @pl.when(pl.program_id(0) == 0)
    def _():
        for s in range(SEQ):
            for st in range(PER):
                at = st * LEN + (s % 2) * Q_ROWS
                out_ref[at : at + Q_ROWS, (s // 2) * LANES : (s // 2 + 1) * LANES] = attn_ref[
                    s, st * Q_ROWS : (st + 1) * Q_ROWS, :
                ]

    for k in range(PAIRS):
        pair = pl.program_id(0) * PAIRS + k
        cols = slice(k * LANES, (k + 1) * LANES)
        reached = jnp.dot(c_ref[...], state_ref[k], preferred_element_type=F32)
        reached = spread_heads(reach_ref[...], pair, LANES) * reached
        ssm_ref[:, cols] = (inner_ref[:, cols] + reached).astype(BF16)


def finish(both, inner_out, c_rows, reach):
    return pl.pallas_call(
        finish_kernel,
        grid=(SEQ // PAIRS,),
        in_specs=[
            pl.BlockSpec((PAIRS, STATE, LANES), lambda g: (g, 0, 0)),
            pl.BlockSpec((SEQ, HALF, LANES), lambda g: (0, 1, 0)),
            pl.BlockSpec((CHUNK, PAIRS * LANES), lambda g: (0, g)),
            whole(CHUNK, STATE),
            whole(CHUNK, 2 * GROUP_HEADS),
        ],
        out_specs=[
            pl.BlockSpec((CHUNK, PAIRS * LANES), lambda g: (0, g)),
            whole(CHUNK, PER * LANES),
        ],
        out_shape=[
            jax.ShapeDtypeStruct((CHUNK, SEQ * LANES), BF16),
            jax.ShapeDtypeStruct((CHUNK, PER * LANES), BF16),
        ],
        compiler_params=params(24),
        cost_estimate=pl.CostEstimate(
            flops=1_000_000_000, bytes_accessed=9 * MIB, transcendentals=0
        ),
        name="finish",
    )(both, both, inner_out, c_rows, reach)


def shards(
    stretch_x,
    stretch_bc,
    stretch_dt,
    stretch_q,
    stretch_kv,
    stretch_place,
    segment_ids,
    ssm_rate,
    dt_bias,
    skip_gain,
):
    seq_index = lax.axis_index("seq")
    mp_index = lax.axis_index("mp")
    exchange = functools.partial(lax.all_to_all, split_axis=0, concat_axis=0, tiled=True)
    cut = functools.partial(lax.dynamic_slice_in_dim, axis=0)

    my_docs = cut(segment_ids, mp_index * LEN, LEN)
    my_place = cut(stretch_place, mp_index, 1)
    info = jnp.concatenate([my_docs, my_place, jnp.zeros((LEN - 1,), jnp.int32)])
    info = jnp.broadcast_to(info.astype(F32)[None, :], (8, LANES))
    to_heads = pack(
        stretch_x, stretch_bc, stretch_q, stretch_dt.T.reshape(STRETCHES, LANES), info
    )
    kv_rows, to_heads = lax.optimization_barrier(
        (exchange(pack_kv(stretch_kv), "mp"), to_heads)
    )
    kv = lax.all_gather(kv_rows, "seq", axis=0, tiled=True)
    hop = exchange(to_heads.reshape(STRETCHES, HOP_ROWS, LANES), ("seq", "mp"))

    told = hop[:, INFO_AT, :].astype(jnp.int32)
    places, docs = told[:, LEN], told[:, :LEN]
    order = jnp.arange(STRETCHES, dtype=jnp.int32)
    inv = jnp.sum(jnp.where(places[None, :] == order[:, None], order[None, :], 0), axis=1)
    bounds = jnp.stack(
        [jnp.sum((docs < v).astype(jnp.int32)) for v in range(DOCS)] + [seq_index % 2, seq_index]
    )
    to_owners, queries = place(inv, hop)
    own_rows = exchange(to_owners, "seq")
    group_first = mp_index * GROUP_HEADS
    biases = cut(dt_bias, group_first, GROUP_HEADS)
    rates = cut(ssm_rate, group_first, GROUP_HEADS)
    gains = cut(skip_gain, group_first, GROUP_HEADS)
    own_ends, steps, decays = ends(bounds, own_rows, biases[:, None], rates[:, None])
    arrived = exchange(own_ends, "seq")

    mine = hop[:, INFO_AT + 1, :].astype(F32)
    mine = mine.reshape(STRETCHES, 2, LEN) + cut(biases, 2 * seq_index, 2)[:, None]
    lost = -cut(rates, 2 * seq_index, 2) * jnp.sum(jax.nn.softplus(mine), axis=2)
    chunk_of = (places // PER)[None, :, None] == jnp.arange(SEQ)[:, None, None]
    lost = jnp.sum(jnp.where(chunk_of, lost[None], 0.0), axis=1)
    totals = jnp.repeat(jnp.exp(lost), HEAD_DIM, axis=1)

    both = exchange(chain(bounds, arrived, totals, attend(inv, bounds, kv, queries)), "seq")
    inner_out, c_rows, reach = inner(
        bounds, own_rows, steps, decays, jnp.repeat(gains.reshape(SEQ, 1, 2), HEAD_DIM, axis=2)
    )
    return tuple(finish(both, inner_out, c_rows, reach))


def solution(mesh):
    return jax.shard_map(
        shards,
        mesh=mesh,
        in_specs=(
            P(("seq", "mp"), None),
            P(("seq", "mp"), None, None),
            P(("seq", "mp"), None),
            P(("seq", "mp"), None),
            P(("seq", "mp"), None, None),
            P("seq"),
            P("seq"),
            P(),
            P(),
            P(),
        ),
        out_specs=(P("seq", "mp"), P("seq", "mp")),
        check_vma=False,
    )
```

```python
import functools

import jax
import jax.numpy as jnp
from jax import lax
from jax.experimental import pallas as pl
from jax.experimental.pallas import tpu as pltpu
from jax.sharding import PartitionSpec as P

SSM_HEADS = 256
HEAD_DIM = 64
STATE = 256
GROUPS = 8
Q_HEADS = 64
KV_HEADS = 8
ATT_DIM = 128
LEN = 64
SEQ = 16
MP = 8
STRETCHES = 128
CHUNK = 512
HALF = 256
PER = CHUNK // LEN
LANES = 128
DOCS = 6
TOKENS = 8192

X_ROWS = LEN
BC_ROWS = 16
Q_ROWS = 32
BC_AT = X_ROWS
Q_AT = BC_AT + BC_ROWS
INFO_AT = Q_AT + Q_ROWS
INFO_ROWS = 8
HOP_ROWS = INFO_AT + INFO_ROWS
OWN_ROWS = X_ROWS + BC_ROWS
OWNER_ROWS = PER * OWN_ROWS + 16
K_AT, V_AT, G_ROWS = 0, 64, 128
GROUP_HEADS = SSM_HEADS // GROUPS
PAIRS = 2
NEG_BIG = -1e30
F32 = jnp.float32
BF16 = jnp.bfloat16
MIB = 1 << 20


def params(mib):
    return pltpu.CompilerParams(vmem_limit_bytes=mib * MIB)


def pack_kernel(x_ref, bc_ref, q_ref, dt_ref, info_ref, hop_ref):
    row = lax.broadcasted_iota(jnp.int32, (INFO_ROWS, LANES), 0)
    told = jnp.where(row == 0, jnp.broadcast_to(info_ref[0:1, :], (INFO_ROWS, LANES)), 0.0)
    raw = dt_ref[...].astype(F32)
    for s in range(SEQ):
        hop_ref[s, 0, 0:X_ROWS, :] = x_ref[:, s * LANES : (s + 1) * LANES]
        col = (s % 2) * LANES
        hop_ref[s, 0, BC_AT : BC_AT + BC_ROWS, :] = bc_ref[
            pl.ds((s // 4) * 16, 16), (s % 4) // 2, col : col + LANES
        ]
        hop_ref[s, 0, Q_AT : Q_AT + Q_ROWS, :] = q_ref[
            pl.ds((s % 2) * Q_ROWS, Q_ROWS), (s // 2) * LANES : (s // 2 + 1) * LANES
        ]
        tile = jnp.where(row == 1, jnp.broadcast_to(raw[s : s + 1, :], (INFO_ROWS, LANES)), told)
        hop_ref[s, 0, INFO_AT:HOP_ROWS, :] = tile.astype(BF16)


def pack(x, bc, q, dt_rows, info):
    cols = lambda width: pl.BlockSpec((LEN, width), lambda m: (0, m))
    return pl.pallas_call(
        pack_kernel,
        grid=(MP,),
        in_specs=[
            cols(SEQ * LANES),
            pl.BlockSpec((LEN, 2, STATE), lambda m: (0, 0, m)),
            cols(PER * LANES),
            pl.BlockSpec((16, LANES), lambda m: (m, 0)),
            pl.BlockSpec((8, LANES), lambda m: (0, 0)),
        ],
        out_specs=pl.BlockSpec((SEQ, 1, HOP_ROWS, LANES), lambda m: (0, m, 0, 0)),
        out_shape=jax.ShapeDtypeStruct((SEQ, MP, HOP_ROWS, LANES), BF16),
        compiler_params=params(60),
        cost_estimate=pl.CostEstimate(flops=0, bytes_accessed=9 * MIB, transcendentals=0),
        name="pack",
    )(x, bc, q, dt_rows, info)


def pack_kv_kernel(kv_ref, out_ref):
    for m in range(MP):
        for half in range(2):
            out_ref[m, half * LEN : (half + 1) * LEN, :] = kv_ref[
                :, half, m * ATT_DIM : (m + 1) * ATT_DIM
            ]


def pack_kv(kv):
    return pl.pallas_call(
        pack_kv_kernel,
        grid=(1,),
        in_specs=[pl.BlockSpec((LEN, 2, KV_HEADS * ATT_DIM), lambda _: (0, 0, 0))],
        out_specs=pl.BlockSpec((MP, G_ROWS, LANES), lambda _: (0, 0, 0)),
        out_shape=jax.ShapeDtypeStruct((MP, G_ROWS, LANES), BF16),
        compiler_params=params(16),
        name="pack_kv",
    )(kv)


def place_kernel(inv_ref, hop_ref, out_ref, q_ref):
    lane = lax.broadcasted_iota(jnp.int32, (1, LANES), 1)
    early = lane < LEN
    row = lax.broadcasted_iota(jnp.int32, (16, LANES), 0)

    def chunk(c, carry):
        raw = []
        for k in range(PER):
            src = inv_ref[c * PER + k]
            out_ref[c, k * OWN_ROWS : (k + 1) * OWN_ROWS, :] = hop_ref[src, 0:OWN_ROWS, :]
            q_ref[c, k * Q_ROWS : (k + 1) * Q_ROWS, :] = hop_ref[src, Q_AT : Q_AT + Q_ROWS, :]
            raw.append(hop_ref[src, INFO_AT:HOP_ROWS, :].astype(F32)[1:2, :])
        turned = [jnp.roll(r, LEN, axis=1) for r in raw]
        tile = jnp.zeros((16, LANES), F32)
        for q in range(4):
            first = jnp.where(early, raw[2 * q], turned[2 * q + 1])
            second = jnp.where(early, turned[2 * q], raw[2 * q + 1])
            tile = jnp.where(row == q, first, jnp.where(row == 4 + q, second, tile))
        out_ref[c, PER * OWN_ROWS : OWNER_ROWS, :] = tile.astype(BF16)
        return carry

    lax.fori_loop(0, SEQ, chunk, 0)


def place(inv, hop):
    return pl.pallas_call(
        place_kernel,
        grid_spec=pltpu.PrefetchScalarGridSpec(
            num_scalar_prefetch=1,
            grid=(1,),
            in_specs=[pl.BlockSpec((STRETCHES, HOP_ROWS, LANES), lambda *_: (0, 0, 0))],
            out_specs=[
                pl.BlockSpec((SEQ, OWNER_ROWS, LANES), lambda *_: (0, 0, 0)),
                pl.BlockSpec((SEQ, PER * Q_ROWS, LANES), lambda *_: (0, 0, 0)),
            ],
        ),
        out_shape=[
            jax.ShapeDtypeStruct((SEQ, OWNER_ROWS, LANES), BF16),
            jax.ShapeDtypeStruct((SEQ, PER * Q_ROWS, LANES), BF16),
        ],
        compiler_params=params(60),
        cost_estimate=pl.CostEstimate(flops=0, bytes_accessed=6 * MIB, transcendentals=0),
        name="place",
    )(inv, hop)


def doc_start(bounds_ref, pos):
    first = jnp.zeros_like(pos)
    for v in range(1, DOCS):
        first = jnp.maximum(first, jnp.where(bounds_ref[v] <= pos, bounds_ref[v], 0))
    return first


def next_doc(bounds_ref, pos):
    after = jnp.full_like(pos, TOKENS)
    for v in range(1, DOCS):
        after = jnp.minimum(after, jnp.where(bounds_ref[v] > pos, bounds_ref[v], TOKENS))
    return after


def running_sums(rows):
    width = rows.shape[1]
    upper = lax.broadcasted_iota(jnp.int32, (width, width), 0) <= lax.broadcasted_iota(
        jnp.int32, (width, width), 1
    )
    return lax.dot(
        rows, upper.astype(F32), precision=lax.Precision.HIGHEST, preferred_element_type=F32
    )


def whole(*shape):
    return pl.BlockSpec(shape, lambda *_: (0,) * len(shape))


SUM_ROWS = 16


def attend_kernel(
    inv_ref, bounds_ref, kv_hbm, q_hbm, out_ref, kv_ref, q_ref, keys_all, turned, peak, acc, top_far, acc_far, sems
):
    kv_copy = pltpu.make_async_copy(kv_hbm, kv_ref, sems.at[0])
    q_copy = pltpu.make_async_copy(q_hbm, q_ref, sems.at[1])
    kv_copy.start()
    q_copy.start()
    half = bounds_ref[DOCS]
    q_rows = PER * Q_ROWS

    def arrange(i, carry):
        values = []
        for k in range(PER):
            src = inv_ref[i * PER + k]
            keys_all[pl.ds(i * CHUNK + k * LEN, LEN), :] = kv_ref[src, K_AT : K_AT + LEN, :]
            values.append(kv_ref[src, V_AT : V_AT + LEN, :])
        turned[i, 0:ATT_DIM, :] = jnp.transpose(jnp.concatenate(values, axis=0))
        turned[i, ATT_DIM : ATT_DIM + SUM_ROWS, :] = jnp.ones((SUM_ROWS, CHUNK), BF16)
        return carry

    kv_copy.wait()
    lax.fori_loop(0, SEQ, arrange, 0, unroll=2)
    q_copy.wait()

    row = lax.broadcasted_iota(jnp.int32, (1, q_rows), 1)
    in_chunk = (row // Q_ROWS) * LEN + half * Q_ROWS + row % Q_ROWS
    key_at = lax.broadcasted_iota(jnp.int32, (CHUNK, q_rows), 0)
    scale = ATT_DIM**-0.5 * 1.4426950408889634

    def scores_of(queries, j):
        keys = keys_all[pl.ds(pl.multiple_of(j * CHUNK, CHUNK), CHUNK), :]
        return lax.dot_general(
            keys, queries, (((1,), (1,)), ((), ())), preferred_element_type=F32
        )

    def mixed(scores, top, j):
        probs = jnp.exp2((scores - top) * scale)
        return jnp.dot(turned[j], probs.astype(BF16), preferred_element_type=F32)

    def peak_of(scores):
        return jnp.max(scores, axis=0, keepdims=True)

    def near_tiles(i, carry):
        queries = q_ref[i]
        first = doc_start(bounds_ref, i * CHUNK + in_chunk) - i * CHUNK
        before = jnp.maximum(i - 1, 0)
        own = (key_at <= in_chunk) & (key_at >= first)
        here = jnp.where(own, scores_of(queries, i), NEG_BIG)
        there = jnp.where(key_at >= first + CHUNK, scores_of(queries, before), NEG_BIG)
        top = jnp.maximum(peak_of(here), peak_of(there))
        peak[i] = top
        acc[i] = mixed(here, top, i) + mixed(there, top, before)
        return carry

    lax.fori_loop(0, SEQ, near_tiles, 0, unroll=2)

    def far_tiles(i, carry):
        first = doc_start(bounds_ref, i * CHUNK) // CHUNK
        count = jnp.maximum(i - 1 - first, 0)
        fours = (count + 1) // 4
        queries = q_ref[i]
        q_doc = doc_start(bounds_ref, i * CHUNK + in_chunk)

        def add_tiles(last, number):
            old = top_far[...]
            scores = []
            for k in range(number):
                dots = scores_of(queries, jnp.maximum(last - k, 0))
                scores.append(jnp.where(key_at >= q_doc - (last - k) * CHUNK, dots, NEG_BIG))
            added, top = acc_far[...], old
            for k, dots in enumerate(scores):
                new = jnp.maximum(top, peak_of(dots))
                added = added * jnp.exp2((top - new) * scale) + mixed(
                    dots, new, jnp.maximum(last - k, 0)
                )
                top = new
            top_far[...] = top
            acc_far[...] = added

        @pl.when(count > 0)
        def _():
            top_far[...] = peak[i]
            acc_far[...] = acc[i]

            def four(t, c):
                add_tiles(i - 2 - 4 * t, 4)
                return c

            lax.fori_loop(0, fours, four, 0)

            @pl.when(count > 4 * fours)
            def _():
                add_tiles(i - 2 - 4 * fours, 2)

            acc[i] = acc_far[...]

        return carry

    lax.fori_loop(2, SEQ, far_tiles, 0)

    def finish(i, carry):
        result = acc[i, 0:ATT_DIM, :] / acc[i, ATT_DIM : ATT_DIM + 1, :]
        out_ref[i, STATE:CHUNK, :] = jnp.transpose(result).astype(BF16)
        return carry

    lax.fori_loop(0, SEQ, finish, 0, unroll=4)


def attend(inv, bounds, kv, queries):
    return pl.pallas_call(
        attend_kernel,
        grid_spec=pltpu.PrefetchScalarGridSpec(
            num_scalar_prefetch=2,
            grid=(1,),
            in_specs=[pl.BlockSpec(memory_space=pl.ANY), pl.BlockSpec(memory_space=pl.ANY)],
            out_specs=whole(SEQ, CHUNK, LANES),
            scratch_shapes=[
                pltpu.VMEM((STRETCHES, G_ROWS, LANES), BF16),
                pltpu.VMEM((SEQ, PER * Q_ROWS, LANES), BF16),
                pltpu.VMEM((TOKENS, ATT_DIM), BF16),
                pltpu.VMEM((SEQ, ATT_DIM + SUM_ROWS, CHUNK), BF16),
                pltpu.VMEM((SEQ, 1, PER * Q_ROWS), F32),
                pltpu.VMEM((SEQ, ATT_DIM + SUM_ROWS, PER * Q_ROWS), F32),
                pltpu.VMEM((1, PER * Q_ROWS), F32),
                pltpu.VMEM((ATT_DIM + SUM_ROWS, PER * Q_ROWS), F32),
                pltpu.SemaphoreType.DMA((2,)),
            ],
        ),
        out_shape=jax.ShapeDtypeStruct((SEQ, CHUNK, LANES), BF16),
        compiler_params=params(60),
        cost_estimate=pl.CostEstimate(flops=8_000_000_000, bytes_accessed=6 * MIB, transcendentals=8 * MIB),
        name="attend",
    )(inv, bounds, kv, queries)


def pair_lanes(first, width, rows):
    row = lax.broadcasted_iota(jnp.int32, (rows, width), 0) % GROUP_HEADS
    lane = lax.broadcasted_iota(jnp.int32, (rows, width), 1)
    return (row == first + lane // (width // 2)).astype(BF16)


def as_parts(rows, count):
    left = jnp.transpose(rows)
    parts = []
    for _ in range(count):
        part = left.astype(BF16)
        parts.append(part)
        left = left - part.astype(F32)
    return jnp.concatenate(parts, axis=1)


def spread_heads(parts, pair, width):
    sel = pair_lanes(2 * pair, width, parts.shape[1])
    return jnp.dot(parts, sel, preferred_element_type=F32)


def channels(own_ref, pair):
    parts = [own_ref[pair, st * OWN_ROWS : st * OWN_ROWS + X_ROWS, :] for st in range(PER)]
    return jnp.concatenate(parts, axis=0).astype(F32)


def gather_proj(own_ref, proj, group):
    for tg in range(4):
        for cg in range(2):
            for st in range(PER):
                at = st * OWN_ROWS + X_ROWS
                proj[st, tg, :, cg * LANES : (cg + 1) * LANES] = own_ref[
                    tg * 4 + group * 2 + cg, at : at + BC_ROWS, :
                ]


def softplus(v):
    return jnp.maximum(v, 0.0) + jnp.log1p(jnp.exp(-jnp.abs(v)))


def ends_kernel(bounds_ref, own_ref, bias_ref, rate_ref, out_ref, step_ref, decay_ref, proj, turned, parts):
    base = bounds_ref[DOCS + 1] * CHUNK

    @pl.when(pl.program_id(0) == 0)
    def _():
        for s in range(SEQ):
            tile = own_ref[s, PER * OWN_ROWS : OWNER_ROWS, :].astype(F32)
            for head in range(2):
                for q in range(4):
                    step_ref[2 * s + head : 2 * s + head + 1, q * LANES : (q + 1) * LANES] = tile[
                        4 * head + q : 4 * head + q + 1, :
                    ]
        step_ref[...] = softplus(step_ref[...] + bias_ref[...])
        decay_ref[...] = -rate_ref[...] * step_ref[...]
        gather_proj(own_ref, proj, 0)
        turned[...] = jnp.transpose(proj[...].reshape(CHUNK, STATE))
        log_sum = running_sums(decay_ref[...])
        pos = lax.broadcasted_iota(jnp.int32, (GROUP_HEADS, CHUNK), 1) + base
        last_doc = doc_start(bounds_ref, base + CHUNK - 1)
        load = jnp.exp(log_sum[:, CHUNK - 1 : CHUNK] - log_sum)
        parts[...] = as_parts(jnp.where(pos >= last_doc, step_ref[...] * load, 0.0), 2)

    for k in range(PAIRS):
        pair = pl.program_id(0) * PAIRS + k
        xs = channels(own_ref, pair)
        driven = (spread_heads(parts[...], pair, LANES) * xs).astype(BF16)
        out_ref[k] = jnp.dot(turned[...], driven, preferred_element_type=F32).astype(BF16)


def ends(bounds, rows, biases, rates):
    return pl.pallas_call(
        ends_kernel,
        grid_spec=pltpu.PrefetchScalarGridSpec(
            num_scalar_prefetch=1,
            grid=(SEQ // PAIRS,),
            in_specs=[
                whole(SEQ, OWNER_ROWS, LANES),
                whole(GROUP_HEADS, 1),
                whole(GROUP_HEADS, 1),
            ],
            out_specs=[
                pl.BlockSpec((PAIRS, STATE, LANES), lambda g, *_: (g, 0, 0)),
                whole(GROUP_HEADS, CHUNK),
                whole(GROUP_HEADS, CHUNK),
            ],
            scratch_shapes=[
                pltpu.VMEM((PER, 4, 16, STATE), BF16),
                pltpu.VMEM((STATE, CHUNK), BF16),
                pltpu.VMEM((CHUNK, 2 * GROUP_HEADS), BF16),
            ],
        ),
        out_shape=[
            jax.ShapeDtypeStruct((SEQ, STATE, LANES), BF16),
            jax.ShapeDtypeStruct((GROUP_HEADS, CHUNK), F32),
            jax.ShapeDtypeStruct((GROUP_HEADS, CHUNK), F32),
        ],
        compiler_params=params(24),
        cost_estimate=pl.CostEstimate(
            flops=1_000_000_000, bytes_accessed=4 * MIB, transcendentals=0
        ),
        name="ends",
    )(bounds, rows, biases, rates)


def chain_kernel(bounds_ref, ends_ref, total_ref, both_in, both_out, states, sem):
    state = jnp.zeros((STATE, LANES), F32)
    for c in range(SEQ):
        states[c] = state.astype(BF16)
        if c < SEQ - 1:
            last_doc = doc_start(bounds_ref, jnp.int32((c + 1) * CHUNK - 1))
            keep = jnp.where(last_doc < c * CHUNK, total_ref[c : c + 1, :], 0.0)
            state = keep * state + ends_ref[c].astype(F32)
    copy = pltpu.make_async_copy(states, both_out.at[:, pl.ds(0, STATE), :], sem)
    copy.start()
    copy.wait()


def chain(bounds, arrived, totals, both):
    return pl.pallas_call(
        chain_kernel,
        grid_spec=pltpu.PrefetchScalarGridSpec(
            num_scalar_prefetch=1,
            grid=(1,),
            in_specs=[
                whole(SEQ, STATE, LANES),
                whole(SEQ, LANES),
                pl.BlockSpec(memory_space=pl.ANY),
            ],
            out_specs=pl.BlockSpec(memory_space=pl.ANY),
            scratch_shapes=[pltpu.VMEM((SEQ, STATE, LANES), BF16), pltpu.SemaphoreType.DMA],
        ),
        out_shape=jax.ShapeDtypeStruct((SEQ, CHUNK, LANES), BF16),
        input_output_aliases={3: 0},
        compiler_params=params(60),
        cost_estimate=pl.CostEstimate(flops=0, bytes_accessed=3 * MIB, transcendentals=0),
        name="chain",
    )(bounds, arrived, totals, both)


def inner_kernel(
    bounds_ref,
    own_ref,
    step_ref,
    decay_ref,
    gain_ref,
    out_ref,
    c_out,
    reach_out,
    proj_b,
    proj_c,
    turned,
    grams,
    sums,
    sum_rows,
    sum_parts,
    step_parts,
    load_parts,
    reach_parts,
):
    base = bounds_ref[DOCS + 1] * CHUNK

    @pl.when(pl.program_id(0) == 0)
    def _():
        gather_proj(own_ref, proj_b, 0)
        gather_proj(own_ref, proj_c, 1)
        row = lax.broadcasted_iota(jnp.int32, (HALF, 1), 0)
        col = lax.broadcasted_iota(jnp.int32, (HALF, HALF), 1)
        for blk in range(2):
            b_blk = proj_b[blk * 4 : blk * 4 + 4].reshape(HALF, STATE)
            c_blk = proj_c[blk * 4 : blk * 4 + 4].reshape(HALF, STATE)
            c_out[blk * HALF : (blk + 1) * HALF, :] = c_blk
            gram = lax.dot_general(
                c_blk, b_blk, (((1,), (1,)), ((), ())), preferred_element_type=F32
            )
            start = base + blk * HALF
            first = doc_start(bounds_ref, start + row) - start
            grams[blk] = jnp.where((col <= row) & (col >= first), gram, 0.0)
            if blk == 0:
                turned[...] = jnp.transpose(b_blk)
            sums[:, blk * HALF : (blk + 1) * HALF] = running_sums(
                decay_ref[:, blk * HALF : (blk + 1) * HALF]
            )
        log_sum = sums[...]
        for head in range(GROUP_HEADS):
            sum_rows[head] = log_sum[head : head + 1, :]
        log_half = log_sum[:, HALF - 1 : HALF]
        pos = lax.broadcasted_iota(jnp.int32, (GROUP_HEADS, HALF), 1) + base
        mid_pos = base + HALF - 1
        load = jnp.where(
            pos >= doc_start(bounds_ref, mid_pos), jnp.exp(log_half - log_sum[:, :HALF]), 0.0
        )
        later = jnp.where(
            pos + HALF < next_doc(bounds_ref, mid_pos), jnp.exp(log_sum[:, HALF:]), 0.0
        )
        whole_sum = jnp.concatenate([log_sum[:, :HALF], log_sum[:, HALF:] + log_half], axis=1)
        pos = lax.broadcasted_iota(jnp.int32, (GROUP_HEADS, CHUNK), 1) + base
        reach_end = jnp.where(base > 0, next_doc(bounds_ref, base - 1), 0)
        reach = jnp.where(pos < reach_end, jnp.exp(whole_sum), 0.0)
        sum_parts[...] = as_parts(log_sum, 3)
        step_parts[...] = as_parts(step_ref[...], 2)
        load_parts[...] = as_parts(step_ref[:, :HALF] * load, 2)
        reach_parts[...] = as_parts(later, 2)
        reach_out[...] = as_parts(reach, 2)

    first_head = lax.broadcasted_iota(jnp.int32, (1, LANES), 1) < HEAD_DIM
    quarter = HALF // 2
    for k in range(PAIRS):
        pair = pl.program_id(0) * PAIRS + k
        gain = gain_ref[pair]
        sum_cols = spread_heads(sum_parts[...], pair, 2 * LANES)
        steps = spread_heads(step_parts[...], pair, LANES)
        loads = spread_heads(load_parts[...], pair, LANES)
        reach = spread_heads(reach_parts[...], pair, LANES)
        xs = channels(own_ref, pair)
        driven = (steps * xs).astype(BF16)
        loaded = (loads * xs[:HALF]).astype(BF16)
        state = jnp.dot(turned[...], loaded, preferred_element_type=F32).astype(BF16)
        for blk in range(2):
            for part in range(2):
                at = blk * HALF + part * quarter
                width = (part + 1) * quarter
                heads = []
                for head in range(2):
                    log_row = sum_rows[2 * pair + head][:, blk * HALF : blk * HALF + width]
                    log_col = sum_cols[at : at + quarter, head * LANES : (head + 1) * LANES]
                    log_col = jnp.concatenate([log_col] * (part + 1), axis=1)
                    weight = jnp.exp(jnp.minimum(log_col - log_row, 0.0))
                    gram = grams[blk, part * quarter : (part + 1) * quarter, 0:width]
                    heads.append(
                        jnp.dot(
                            (gram * weight).astype(BF16),
                            driven[blk * HALF : blk * HALF + width],
                            preferred_element_type=F32,
                        )
                    )
                result = jnp.where(first_head, heads[0], heads[1]) + gain * xs[at : at + quarter]
                if blk == 1:
                    c_part = c_out[at : at + quarter, :]
                    result += reach[part * quarter : (part + 1) * quarter] * jnp.dot(
                        c_part, state, preferred_element_type=F32
                    )
                out_ref[at : at + quarter, k * LANES : (k + 1) * LANES] = result.astype(BF16)


def inner(bounds, rows, steps, decays, gains):
    return pl.pallas_call(
        inner_kernel,
        grid_spec=pltpu.PrefetchScalarGridSpec(
            num_scalar_prefetch=1,
            grid=(SEQ // PAIRS,),
            in_specs=[
                whole(SEQ, OWNER_ROWS, LANES),
                whole(GROUP_HEADS, CHUNK),
                whole(GROUP_HEADS, CHUNK),
                whole(SEQ, 1, LANES),
            ],
            out_specs=[
                pl.BlockSpec((CHUNK, PAIRS * LANES), lambda g, *_: (0, g)),
                whole(CHUNK, STATE),
                whole(CHUNK, 2 * GROUP_HEADS),
            ],
            scratch_shapes=[
                pltpu.VMEM((PER, 4, 16, STATE), BF16),
                pltpu.VMEM((PER, 4, 16, STATE), BF16),
                pltpu.VMEM((STATE, HALF), BF16),
                pltpu.VMEM((2, HALF, HALF), F32),
                pltpu.VMEM((GROUP_HEADS, CHUNK), F32),
                pltpu.VMEM((GROUP_HEADS, 1, CHUNK), F32),
                pltpu.VMEM((CHUNK, 3 * GROUP_HEADS), BF16),
                pltpu.VMEM((CHUNK, 2 * GROUP_HEADS), BF16),
                pltpu.VMEM((HALF, 2 * GROUP_HEADS), BF16),
                pltpu.VMEM((HALF, 2 * GROUP_HEADS), BF16),
            ],
        ),
        out_shape=[
            jax.ShapeDtypeStruct((CHUNK, SEQ * LANES), BF16),
            jax.ShapeDtypeStruct((CHUNK, STATE), BF16),
            jax.ShapeDtypeStruct((CHUNK, 2 * GROUP_HEADS), BF16),
        ],
        compiler_params=params(32),
        cost_estimate=pl.CostEstimate(
            flops=4_000_000_000, bytes_accessed=8 * MIB, transcendentals=4 * MIB
        ),
        name="inner",
    )(bounds, rows, steps, decays, gains)


def finish_kernel(state_ref, attn_ref, inner_ref, c_ref, reach_ref, ssm_ref, out_ref):
    @pl.when(pl.program_id(0) == 0)
    def _():
        for s in range(SEQ):
            for st in range(PER):
                at = st * LEN + (s % 2) * Q_ROWS
                out_ref[at : at + Q_ROWS, (s // 2) * LANES : (s // 2 + 1) * LANES] = attn_ref[
                    s, st * Q_ROWS : (st + 1) * Q_ROWS, :
                ]

    for k in range(PAIRS):
        pair = pl.program_id(0) * PAIRS + k
        cols = slice(k * LANES, (k + 1) * LANES)
        reached = jnp.dot(c_ref[...], state_ref[k], preferred_element_type=F32)
        reached = spread_heads(reach_ref[...], pair, LANES) * reached
        ssm_ref[:, cols] = (inner_ref[:, cols].astype(F32) + reached).astype(BF16)


def finish(both, inner_out, c_rows, reach):
    return pl.pallas_call(
        finish_kernel,
        grid=(SEQ // PAIRS,),
        in_specs=[
            pl.BlockSpec((PAIRS, STATE, LANES), lambda g: (g, 0, 0)),
            pl.BlockSpec((SEQ, HALF, LANES), lambda g: (0, 1, 0)),
            pl.BlockSpec((CHUNK, PAIRS * LANES), lambda g: (0, g)),
            whole(CHUNK, STATE),
            whole(CHUNK, 2 * GROUP_HEADS),
        ],
        out_specs=[
            pl.BlockSpec((CHUNK, PAIRS * LANES), lambda g: (0, g)),
            whole(CHUNK, PER * LANES),
        ],
        out_shape=[
            jax.ShapeDtypeStruct((CHUNK, SEQ * LANES), BF16),
            jax.ShapeDtypeStruct((CHUNK, PER * LANES), BF16),
        ],
        compiler_params=params(24),
        cost_estimate=pl.CostEstimate(
            flops=1_000_000_000, bytes_accessed=9 * MIB, transcendentals=0
        ),
        name="finish",
    )(both, both, inner_out, c_rows, reach)


def shards(
    stretch_x,
    stretch_bc,
    stretch_dt,
    stretch_q,
    stretch_kv,
    stretch_place,
    segment_ids,
    ssm_rate,
    dt_bias,
    skip_gain,
):
    seq_index = lax.axis_index("seq")
    mp_index = lax.axis_index("mp")
    exchange = functools.partial(lax.all_to_all, split_axis=0, concat_axis=0, tiled=True)
    cut = functools.partial(lax.dynamic_slice_in_dim, axis=0)

    my_docs = cut(segment_ids, mp_index * LEN, LEN)
    my_place = cut(stretch_place, mp_index, 1)
    info = jnp.concatenate([my_docs, my_place, jnp.zeros((LEN - 1,), jnp.int32)])
    info = jnp.broadcast_to(info.astype(F32)[None, :], (8, LANES))
    kv = lax.all_gather(exchange(pack_kv(stretch_kv), "mp"), "seq", axis=0, tiled=True)
    to_heads = pack(
        stretch_x, stretch_bc, stretch_q, stretch_dt.T.reshape(STRETCHES, LANES), info
    )
    hop = exchange(to_heads.reshape(STRETCHES, HOP_ROWS, LANES), ("seq", "mp"))

    told = hop[:, INFO_AT, :].astype(jnp.int32)
    places, docs = told[:, LEN], told[:, :LEN]
    order = jnp.arange(STRETCHES, dtype=jnp.int32)
    inv = jnp.sum(jnp.where(places[None, :] == order[:, None], order[None, :], 0), axis=1)
    bounds = jnp.stack(
        [jnp.sum((docs < v).astype(jnp.int32)) for v in range(DOCS)] + [seq_index % 2, seq_index]
    )
    to_owners, queries = place(inv, hop)
    own_rows = exchange(to_owners, "seq")
    group_first = mp_index * GROUP_HEADS
    biases = cut(dt_bias, group_first, GROUP_HEADS)
    rates = cut(ssm_rate, group_first, GROUP_HEADS)
    gains = cut(skip_gain, group_first, GROUP_HEADS)
    attended, own_bounds = lax.optimization_barrier((attend(inv, bounds, kv, queries), bounds))
    own_ends, steps, decays = ends(own_bounds, own_rows, biases[:, None], rates[:, None])
    arrived = exchange(own_ends, "seq")

    mine = hop[:, INFO_AT + 1, :].astype(F32)
    mine = mine.reshape(STRETCHES, 2, LEN) + cut(biases, 2 * seq_index, 2)[:, None]
    lost = -cut(rates, 2 * seq_index, 2) * jnp.sum(jax.nn.softplus(mine), axis=2)
    chunk_of = (places // PER)[None, :, None] == jnp.arange(SEQ)[:, None, None]
    lost = jnp.sum(jnp.where(chunk_of, lost[None], 0.0), axis=1)
    totals = jnp.repeat(jnp.exp(lost), HEAD_DIM, axis=1)

    both = exchange(chain(bounds, arrived, totals, attended), "seq")
    inner_out, c_rows, reach = inner(
        bounds, own_rows, steps, decays, jnp.repeat(gains.reshape(SEQ, 1, 2), HEAD_DIM, axis=2)
    )
    return tuple(finish(both, inner_out, c_rows, reach))


def solution(mesh):
    return jax.shard_map(
        shards,
        mesh=mesh,
        in_specs=(
            P(("seq", "mp"), None),
            P(("seq", "mp"), None, None),
            P(("seq", "mp"), None),
            P(("seq", "mp"), None),
            P(("seq", "mp"), None, None),
            P("seq"),
            P("seq"),
            P(),
            P(),
            P(),
        ),
        out_specs=(P("seq", "mp"), P("seq", "mp")),
        check_vma=False,
    )
```

```python
import functools

import jax
import jax.numpy as jnp
from jax import lax
from jax.experimental import pallas as pl
from jax.experimental.pallas import tpu as pltpu
from jax.sharding import PartitionSpec as P

SSM_HEADS = 256
HEAD_DIM = 64
STATE = 256
GROUPS = 8
Q_HEADS = 64
KV_HEADS = 8
ATT_DIM = 128
LEN = 64
SEQ = 16
MP = 8
STRETCHES = 128
CHUNK = 512
HALF = 256
PER = CHUNK // LEN
LANES = 128
DOCS = 6
TOKENS = 8192

X_ROWS = LEN
BC_ROWS = 16
Q_ROWS = 32
BC_AT = X_ROWS
Q_AT = BC_AT + BC_ROWS
INFO_AT = Q_AT + Q_ROWS
INFO_ROWS = 8
HOP_ROWS = INFO_AT + INFO_ROWS
OWN_ROWS = X_ROWS + BC_ROWS
OWNER_ROWS = PER * OWN_ROWS + 16
K_AT, V_AT, G_ROWS = 0, 64, 128
GROUP_HEADS = SSM_HEADS // GROUPS
PAIRS = 2
NEG_BIG = -1e30
F32 = jnp.float32
BF16 = jnp.bfloat16
MIB = 1 << 20


def params(mib):
    return pltpu.CompilerParams(vmem_limit_bytes=mib * MIB)


def pack_kernel(x_ref, bc_ref, q_ref, dt_ref, info_ref, hop_ref):
    row = lax.broadcasted_iota(jnp.int32, (INFO_ROWS, LANES), 0)
    told = jnp.where(row == 0, jnp.broadcast_to(info_ref[0:1, :], (INFO_ROWS, LANES)), 0.0)
    raw = dt_ref[...].astype(F32)
    for s in range(SEQ):
        hop_ref[s, 0, 0:X_ROWS, :] = x_ref[:, s * LANES : (s + 1) * LANES]
        col = (s % 2) * LANES
        hop_ref[s, 0, BC_AT : BC_AT + BC_ROWS, :] = bc_ref[
            pl.ds((s // 4) * 16, 16), (s % 4) // 2, col : col + LANES
        ]
        hop_ref[s, 0, Q_AT : Q_AT + Q_ROWS, :] = q_ref[
            pl.ds((s % 2) * Q_ROWS, Q_ROWS), (s // 2) * LANES : (s // 2 + 1) * LANES
        ]
        tile = jnp.where(row == 1, jnp.broadcast_to(raw[s : s + 1, :], (INFO_ROWS, LANES)), told)
        hop_ref[s, 0, INFO_AT:HOP_ROWS, :] = tile.astype(BF16)


def pack(x, bc, q, dt_rows, info):
    cols = lambda width: pl.BlockSpec((LEN, width), lambda m: (0, m))
    return pl.pallas_call(
        pack_kernel,
        grid=(MP,),
        in_specs=[
            cols(SEQ * LANES),
            pl.BlockSpec((LEN, 2, STATE), lambda m: (0, 0, m)),
            cols(PER * LANES),
            pl.BlockSpec((16, LANES), lambda m: (m, 0)),
            pl.BlockSpec((8, LANES), lambda m: (0, 0)),
        ],
        out_specs=pl.BlockSpec((SEQ, 1, HOP_ROWS, LANES), lambda m: (0, m, 0, 0)),
        out_shape=jax.ShapeDtypeStruct((SEQ, MP, HOP_ROWS, LANES), BF16),
        compiler_params=params(60),
        cost_estimate=pl.CostEstimate(flops=0, bytes_accessed=9 * MIB, transcendentals=0),
        name="pack",
    )(x, bc, q, dt_rows, info)


def pack_kv_kernel(kv_ref, out_ref):
    for m in range(MP):
        for half in range(2):
            out_ref[m, half * LEN : (half + 1) * LEN, :] = kv_ref[
                :, half, m * ATT_DIM : (m + 1) * ATT_DIM
            ]


def pack_kv(kv):
    return pl.pallas_call(
        pack_kv_kernel,
        grid=(1,),
        in_specs=[pl.BlockSpec((LEN, 2, KV_HEADS * ATT_DIM), lambda _: (0, 0, 0))],
        out_specs=pl.BlockSpec((MP, G_ROWS, LANES), lambda _: (0, 0, 0)),
        out_shape=jax.ShapeDtypeStruct((MP, G_ROWS, LANES), BF16),
        compiler_params=params(16),
        name="pack_kv",
    )(kv)


def place_kernel(inv_ref, hop_ref, out_ref, q_ref):
    lane = lax.broadcasted_iota(jnp.int32, (1, LANES), 1)
    early = lane < LEN
    row = lax.broadcasted_iota(jnp.int32, (16, LANES), 0)

    def chunk(c, carry):
        raw = []
        for k in range(PER):
            src = inv_ref[c * PER + k]
            out_ref[c, k * OWN_ROWS : (k + 1) * OWN_ROWS, :] = hop_ref[src, 0:OWN_ROWS, :]
            q_ref[c, k * Q_ROWS : (k + 1) * Q_ROWS, :] = hop_ref[src, Q_AT : Q_AT + Q_ROWS, :]
            raw.append(hop_ref[src, INFO_AT:HOP_ROWS, :].astype(F32)[1:2, :])
        turned = [jnp.roll(r, LEN, axis=1) for r in raw]
        tile = jnp.zeros((16, LANES), F32)
        for q in range(4):
            first = jnp.where(early, raw[2 * q], turned[2 * q + 1])
            second = jnp.where(early, turned[2 * q], raw[2 * q + 1])
            tile = jnp.where(row == q, first, jnp.where(row == 4 + q, second, tile))
        out_ref[c, PER * OWN_ROWS : OWNER_ROWS, :] = tile.astype(BF16)
        return carry

    lax.fori_loop(0, SEQ, chunk, 0)


def place(inv, hop):
    return pl.pallas_call(
        place_kernel,
        grid_spec=pltpu.PrefetchScalarGridSpec(
            num_scalar_prefetch=1,
            grid=(1,),
            in_specs=[pl.BlockSpec((STRETCHES, HOP_ROWS, LANES), lambda *_: (0, 0, 0))],
            out_specs=[
                pl.BlockSpec((SEQ, OWNER_ROWS, LANES), lambda *_: (0, 0, 0)),
                pl.BlockSpec((SEQ, PER * Q_ROWS, LANES), lambda *_: (0, 0, 0)),
            ],
        ),
        out_shape=[
            jax.ShapeDtypeStruct((SEQ, OWNER_ROWS, LANES), BF16),
            jax.ShapeDtypeStruct((SEQ, PER * Q_ROWS, LANES), BF16),
        ],
        compiler_params=params(60),
        cost_estimate=pl.CostEstimate(flops=0, bytes_accessed=6 * MIB, transcendentals=0),
        name="place",
    )(inv, hop)


def doc_start(bounds_ref, pos):
    first = jnp.zeros_like(pos)
    for v in range(1, DOCS):
        first = jnp.maximum(first, jnp.where(bounds_ref[v] <= pos, bounds_ref[v], 0))
    return first


def next_doc(bounds_ref, pos):
    after = jnp.full_like(pos, TOKENS)
    for v in range(1, DOCS):
        after = jnp.minimum(after, jnp.where(bounds_ref[v] > pos, bounds_ref[v], TOKENS))
    return after


def running_sums(rows):
    width = rows.shape[1]
    upper = lax.broadcasted_iota(jnp.int32, (width, width), 0) <= lax.broadcasted_iota(
        jnp.int32, (width, width), 1
    )
    return lax.dot(
        rows, upper.astype(F32), precision=lax.Precision.HIGHEST, preferred_element_type=F32
    )


def whole(*shape):
    return pl.BlockSpec(shape, lambda *_: (0,) * len(shape))


CALL_CHUNKS = SEQ // 2
SUM_ROWS = 16


def attend_kernel(
    begin,
    inv_ref, bounds_ref, kv_hbm, q_hbm, out_ref, kv_ref, q_ref, keys_all, turned, peak, acc, top_far, acc_far, sems
):
    kv_copy = pltpu.make_async_copy(kv_hbm, kv_ref, sems.at[0])
    q_copy = pltpu.make_async_copy(q_hbm, q_ref, sems.at[1])
    kv_copy.start()
    q_copy.start()
    half = bounds_ref[DOCS]
    q_rows = PER * Q_ROWS

    def arrange(i, carry):
        values = []
        for k in range(PER):
            src = inv_ref[i * PER + k]
            keys_all[pl.ds(i * CHUNK + k * LEN, LEN), :] = kv_ref[src, K_AT : K_AT + LEN, :]
            values.append(kv_ref[src, V_AT : V_AT + LEN, :])
        turned[i, 0:ATT_DIM, :] = jnp.transpose(jnp.concatenate(values, axis=0))
        turned[i, ATT_DIM : ATT_DIM + SUM_ROWS, :] = jnp.ones((SUM_ROWS, CHUNK), BF16)
        return carry

    kv_copy.wait()
    lax.fori_loop(0, begin + CALL_CHUNKS, arrange, 0, unroll=2)
    q_copy.wait()

    row = lax.broadcasted_iota(jnp.int32, (1, q_rows), 1)
    in_chunk = (row // Q_ROWS) * LEN + half * Q_ROWS + row % Q_ROWS
    key_at = lax.broadcasted_iota(jnp.int32, (CHUNK, q_rows), 0)
    scale = ATT_DIM**-0.5 * 1.4426950408889634

    def scores_of(queries, j):
        keys = keys_all[pl.ds(pl.multiple_of(j * CHUNK, CHUNK), CHUNK), :]
        return lax.dot_general(
            keys, queries, (((1,), (1,)), ((), ())), preferred_element_type=F32
        )

    def mixed(scores, top, j):
        probs = jnp.exp2((scores - top) * scale)
        return jnp.dot(turned[j], probs.astype(BF16), preferred_element_type=F32)

    def peak_of(scores):
        return jnp.max(scores, axis=0, keepdims=True)

    def near_tiles(n, carry):
        i = begin + n
        queries = q_ref[i]
        first = doc_start(bounds_ref, i * CHUNK + in_chunk) - i * CHUNK
        before = jnp.maximum(i - 1, 0)
        own = (key_at <= in_chunk) & (key_at >= first)
        here = jnp.where(own, scores_of(queries, i), NEG_BIG)
        there = jnp.where(key_at >= first + CHUNK, scores_of(queries, before), NEG_BIG)
        top = jnp.maximum(peak_of(here), peak_of(there))
        peak[n] = top
        acc[n] = mixed(here, top, i) + mixed(there, top, before)
        return carry

    lax.fori_loop(0, CALL_CHUNKS, near_tiles, 0, unroll=2)

    def far_tiles(n, carry):
        i = begin + n
        first = doc_start(bounds_ref, i * CHUNK) // CHUNK
        count = jnp.maximum(i - 1 - first, 0)
        fours = (count + 1) // 4
        queries = q_ref[i]
        q_doc = doc_start(bounds_ref, i * CHUNK + in_chunk)

        def add_tiles(last, number):
            old = top_far[...]
            scores = []
            for k in range(number):
                dots = scores_of(queries, jnp.maximum(last - k, 0))
                scores.append(jnp.where(key_at >= q_doc - (last - k) * CHUNK, dots, NEG_BIG))
            added, top = acc_far[...], old
            for k, dots in enumerate(scores):
                new = jnp.maximum(top, peak_of(dots))
                added = added * jnp.exp2((top - new) * scale) + mixed(
                    dots, new, jnp.maximum(last - k, 0)
                )
                top = new
            top_far[...] = top
            acc_far[...] = added

        @pl.when(count > 0)
        def _():
            top_far[...] = peak[n]
            acc_far[...] = acc[n]

            def four(t, c):
                add_tiles(i - 2 - 4 * t, 4)
                return c

            lax.fori_loop(0, fours, four, 0)

            @pl.when(count > 4 * fours)
            def _():
                add_tiles(i - 2 - 4 * fours, 2)

            acc[n] = acc_far[...]

        return carry

    lax.fori_loop(2 if begin == 0 else 0, CALL_CHUNKS, far_tiles, 0)

    def finish(i, carry):
        result = acc[i, 0:ATT_DIM, :] / acc[i, ATT_DIM : ATT_DIM + 1, :]
        out_ref[i] = jnp.transpose(result).astype(BF16)
        return carry

    lax.fori_loop(0, CALL_CHUNKS, finish, 0, unroll=4)


def attend(begin, inv, bounds, kv, queries):
    return pl.pallas_call(
        functools.partial(attend_kernel, begin),
        grid_spec=pltpu.PrefetchScalarGridSpec(
            num_scalar_prefetch=2,
            grid=(1,),
            in_specs=[pl.BlockSpec(memory_space=pl.ANY), pl.BlockSpec(memory_space=pl.ANY)],
            out_specs=whole(CALL_CHUNKS, HALF, LANES),
            scratch_shapes=[
                pltpu.VMEM((STRETCHES, G_ROWS, LANES), BF16),
                pltpu.VMEM((SEQ, PER * Q_ROWS, LANES), BF16),
                pltpu.VMEM((TOKENS, ATT_DIM), BF16),
                pltpu.VMEM((SEQ, ATT_DIM + SUM_ROWS, CHUNK), BF16),
                pltpu.VMEM((CALL_CHUNKS, 1, PER * Q_ROWS), F32),
                pltpu.VMEM((CALL_CHUNKS, ATT_DIM + SUM_ROWS, PER * Q_ROWS), F32),
                pltpu.VMEM((1, PER * Q_ROWS), F32),
                pltpu.VMEM((ATT_DIM + SUM_ROWS, PER * Q_ROWS), F32),
                pltpu.SemaphoreType.DMA((2,)),
            ],
        ),
        out_shape=jax.ShapeDtypeStruct((CALL_CHUNKS, HALF, LANES), BF16),
        compiler_params=params(60),
        cost_estimate=pl.CostEstimate(flops=4_000_000_000, bytes_accessed=6 * MIB, transcendentals=4 * MIB),
        name=f"attend{begin}",
    )(inv, bounds, kv, queries)


def pair_lanes(first, width, rows):
    row = lax.broadcasted_iota(jnp.int32, (rows, width), 0) % GROUP_HEADS
    lane = lax.broadcasted_iota(jnp.int32, (rows, width), 1)
    return (row == first + lane // (width // 2)).astype(BF16)


def as_parts(rows, count):
    left = jnp.transpose(rows)
    parts = []
    for _ in range(count):
        part = left.astype(BF16)
        parts.append(part)
        left = left - part.astype(F32)
    return jnp.concatenate(parts, axis=1)


def spread_heads(parts, pair, width):
    sel = pair_lanes(2 * pair, width, parts.shape[1])
    return jnp.dot(parts, sel, preferred_element_type=F32)


def channels(own_ref, pair):
    parts = [own_ref[pair, st * OWN_ROWS : st * OWN_ROWS + X_ROWS, :] for st in range(PER)]
    return jnp.concatenate(parts, axis=0).astype(F32)


def gather_proj(own_ref, proj, group):
    for tg in range(4):
        for cg in range(2):
            for st in range(PER):
                at = st * OWN_ROWS + X_ROWS
                proj[st, tg, :, cg * LANES : (cg + 1) * LANES] = own_ref[
                    tg * 4 + group * 2 + cg, at : at + BC_ROWS, :
                ]


def softplus(v):
    return jnp.maximum(v, 0.0) + jnp.log1p(jnp.exp(-jnp.abs(v)))


def ends_kernel(bounds_ref, own_ref, bias_ref, rate_ref, out_ref, step_ref, decay_ref, proj, turned, parts):
    base = bounds_ref[DOCS + 1] * CHUNK

    @pl.when(pl.program_id(0) == 0)
    def _():
        for s in range(SEQ):
            tile = own_ref[s, PER * OWN_ROWS : OWNER_ROWS, :].astype(F32)
            for head in range(2):
                for q in range(4):
                    step_ref[2 * s + head : 2 * s + head + 1, q * LANES : (q + 1) * LANES] = tile[
                        4 * head + q : 4 * head + q + 1, :
                    ]
        step_ref[...] = softplus(step_ref[...] + bias_ref[...])
        decay_ref[...] = -rate_ref[...] * step_ref[...]
        gather_proj(own_ref, proj, 0)
        turned[...] = jnp.transpose(proj[...].reshape(CHUNK, STATE))
        log_sum = running_sums(decay_ref[...])
        pos = lax.broadcasted_iota(jnp.int32, (GROUP_HEADS, CHUNK), 1) + base
        last_doc = doc_start(bounds_ref, base + CHUNK - 1)
        load = jnp.exp(log_sum[:, CHUNK - 1 : CHUNK] - log_sum)
        parts[...] = as_parts(jnp.where(pos >= last_doc, step_ref[...] * load, 0.0), 2)

    for k in range(PAIRS):
        pair = pl.program_id(0) * PAIRS + k
        xs = channels(own_ref, pair)
        driven = (spread_heads(parts[...], pair, LANES) * xs).astype(BF16)
        out_ref[k] = jnp.dot(turned[...], driven, preferred_element_type=F32).astype(BF16)


def ends(bounds, rows, biases, rates):
    return pl.pallas_call(
        ends_kernel,
        grid_spec=pltpu.PrefetchScalarGridSpec(
            num_scalar_prefetch=1,
            grid=(SEQ // PAIRS,),
            in_specs=[
                whole(SEQ, OWNER_ROWS, LANES),
                whole(GROUP_HEADS, 1),
                whole(GROUP_HEADS, 1),
            ],
            out_specs=[
                pl.BlockSpec((PAIRS, STATE, LANES), lambda g, *_: (g, 0, 0)),
                whole(GROUP_HEADS, CHUNK),
                whole(GROUP_HEADS, CHUNK),
            ],
            scratch_shapes=[
                pltpu.VMEM((PER, 4, 16, STATE), BF16),
                pltpu.VMEM((STATE, CHUNK), BF16),
                pltpu.VMEM((CHUNK, 2 * GROUP_HEADS), BF16),
            ],
        ),
        out_shape=[
            jax.ShapeDtypeStruct((SEQ, STATE, LANES), BF16),
            jax.ShapeDtypeStruct((GROUP_HEADS, CHUNK), F32),
            jax.ShapeDtypeStruct((GROUP_HEADS, CHUNK), F32),
        ],
        compiler_params=params(24),
        cost_estimate=pl.CostEstimate(
            flops=1_000_000_000, bytes_accessed=4 * MIB, transcendentals=0
        ),
        name="ends",
    )(bounds, rows, biases, rates)


def chain_kernel(bounds_ref, ends_ref, total_ref, early_ref, late_ref, out_ref):
    state = jnp.zeros((STATE, LANES), F32)
    for c in range(SEQ):
        out_ref[c, 0:STATE, :] = state.astype(BF16)
        rows = early_ref if c < CALL_CHUNKS else late_ref
        out_ref[c, STATE:CHUNK, :] = rows[c % CALL_CHUNKS]
        if c < SEQ - 1:
            last_doc = doc_start(bounds_ref, jnp.int32((c + 1) * CHUNK - 1))
            keep = jnp.where(last_doc < c * CHUNK, total_ref[c : c + 1, :], 0.0)
            state = keep * state + ends_ref[c].astype(F32)


def chain(bounds, arrived, totals, early, late):
    return pl.pallas_call(
        chain_kernel,
        grid_spec=pltpu.PrefetchScalarGridSpec(
            num_scalar_prefetch=1,
            grid=(1,),
            in_specs=[
                whole(SEQ, STATE, LANES),
                whole(SEQ, LANES),
                whole(CALL_CHUNKS, HALF, LANES),
                whole(CALL_CHUNKS, HALF, LANES),
            ],
            out_specs=whole(SEQ, CHUNK, LANES),
        ),
        out_shape=jax.ShapeDtypeStruct((SEQ, CHUNK, LANES), BF16),
        compiler_params=params(24),
        cost_estimate=pl.CostEstimate(flops=0, bytes_accessed=5 * MIB, transcendentals=0),
        name="chain",
    )(bounds, arrived, totals, early, late)


def inner_kernel(
    bounds_ref,
    own_ref,
    step_ref,
    decay_ref,
    gain_ref,
    out_ref,
    c_out,
    reach_out,
    proj_b,
    proj_c,
    turned,
    grams,
    sums,
    sum_rows,
    sum_parts,
    step_parts,
    load_parts,
    reach_parts,
):
    base = bounds_ref[DOCS + 1] * CHUNK

    @pl.when(pl.program_id(0) == 0)
    def _():
        gather_proj(own_ref, proj_b, 0)
        gather_proj(own_ref, proj_c, 1)
        row = lax.broadcasted_iota(jnp.int32, (HALF, 1), 0)
        col = lax.broadcasted_iota(jnp.int32, (HALF, HALF), 1)
        for blk in range(2):
            b_blk = proj_b[blk * 4 : blk * 4 + 4].reshape(HALF, STATE)
            c_blk = proj_c[blk * 4 : blk * 4 + 4].reshape(HALF, STATE)
            c_out[blk * HALF : (blk + 1) * HALF, :] = c_blk
            gram = lax.dot_general(
                c_blk, b_blk, (((1,), (1,)), ((), ())), preferred_element_type=F32
            )
            start = base + blk * HALF
            first = doc_start(bounds_ref, start + row) - start
            grams[blk] = jnp.where((col <= row) & (col >= first), gram, 0.0)
            if blk == 0:
                turned[...] = jnp.transpose(b_blk)
            sums[:, blk * HALF : (blk + 1) * HALF] = running_sums(
                decay_ref[:, blk * HALF : (blk + 1) * HALF]
            )
        log_sum = sums[...]
        for head in range(GROUP_HEADS):
            sum_rows[head] = log_sum[head : head + 1, :]
        log_half = log_sum[:, HALF - 1 : HALF]
        pos = lax.broadcasted_iota(jnp.int32, (GROUP_HEADS, HALF), 1) + base
        mid_pos = base + HALF - 1
        load = jnp.where(
            pos >= doc_start(bounds_ref, mid_pos), jnp.exp(log_half - log_sum[:, :HALF]), 0.0
        )
        later = jnp.where(
            pos + HALF < next_doc(bounds_ref, mid_pos), jnp.exp(log_sum[:, HALF:]), 0.0
        )
        whole_sum = jnp.concatenate([log_sum[:, :HALF], log_sum[:, HALF:] + log_half], axis=1)
        pos = lax.broadcasted_iota(jnp.int32, (GROUP_HEADS, CHUNK), 1) + base
        reach_end = jnp.where(base > 0, next_doc(bounds_ref, base - 1), 0)
        reach = jnp.where(pos < reach_end, jnp.exp(whole_sum), 0.0)
        sum_parts[...] = as_parts(log_sum, 3)
        step_parts[...] = as_parts(step_ref[...], 2)
        load_parts[...] = as_parts(step_ref[:, :HALF] * load, 2)
        reach_parts[...] = as_parts(later, 2)
        reach_out[...] = as_parts(reach, 2)

    first_head = lax.broadcasted_iota(jnp.int32, (1, LANES), 1) < HEAD_DIM
    quarter = HALF // 2
    for k in range(PAIRS):
        pair = pl.program_id(0) * PAIRS + k
        gain = gain_ref[pair]
        sum_cols = spread_heads(sum_parts[...], pair, 2 * LANES)
        steps = spread_heads(step_parts[...], pair, LANES)
        loads = spread_heads(load_parts[...], pair, LANES)
        reach = spread_heads(reach_parts[...], pair, LANES)
        xs = channels(own_ref, pair)
        driven = (steps * xs).astype(BF16)
        loaded = (loads * xs[:HALF]).astype(BF16)
        state = jnp.dot(turned[...], loaded, preferred_element_type=F32).astype(BF16)
        for blk in range(2):
            for part in range(2):
                at = blk * HALF + part * quarter
                width = (part + 1) * quarter
                heads = []
                for head in range(2):
                    log_row = sum_rows[2 * pair + head][:, blk * HALF : blk * HALF + width]
                    log_col = sum_cols[at : at + quarter, head * LANES : (head + 1) * LANES]
                    log_col = jnp.concatenate([log_col] * (part + 1), axis=1)
                    weight = jnp.exp(jnp.minimum(log_col - log_row, 0.0))
                    gram = grams[blk, part * quarter : (part + 1) * quarter, 0:width]
                    heads.append(
                        jnp.dot(
                            (gram * weight).astype(BF16),
                            driven[blk * HALF : blk * HALF + width],
                            preferred_element_type=F32,
                        )
                    )
                result = jnp.where(first_head, heads[0], heads[1]) + gain * xs[at : at + quarter]
                if blk == 1:
                    c_part = c_out[at : at + quarter, :]
                    result += reach[part * quarter : (part + 1) * quarter] * jnp.dot(
                        c_part, state, preferred_element_type=F32
                    )
                out_ref[at : at + quarter, k * LANES : (k + 1) * LANES] = result.astype(BF16)


def inner(bounds, rows, steps, decays, gains):
    return pl.pallas_call(
        inner_kernel,
        grid_spec=pltpu.PrefetchScalarGridSpec(
            num_scalar_prefetch=1,
            grid=(SEQ // PAIRS,),
            in_specs=[
                whole(SEQ, OWNER_ROWS, LANES),
                whole(GROUP_HEADS, CHUNK),
                whole(GROUP_HEADS, CHUNK),
                whole(SEQ, 1, LANES),
            ],
            out_specs=[
                pl.BlockSpec((CHUNK, PAIRS * LANES), lambda g, *_: (0, g)),
                whole(CHUNK, STATE),
                whole(CHUNK, 2 * GROUP_HEADS),
            ],
            scratch_shapes=[
                pltpu.VMEM((PER, 4, 16, STATE), BF16),
                pltpu.VMEM((PER, 4, 16, STATE), BF16),
                pltpu.VMEM((STATE, HALF), BF16),
                pltpu.VMEM((2, HALF, HALF), F32),
                pltpu.VMEM((GROUP_HEADS, CHUNK), F32),
                pltpu.VMEM((GROUP_HEADS, 1, CHUNK), F32),
                pltpu.VMEM((CHUNK, 3 * GROUP_HEADS), BF16),
                pltpu.VMEM((CHUNK, 2 * GROUP_HEADS), BF16),
                pltpu.VMEM((HALF, 2 * GROUP_HEADS), BF16),
                pltpu.VMEM((HALF, 2 * GROUP_HEADS), BF16),
            ],
        ),
        out_shape=[
            jax.ShapeDtypeStruct((CHUNK, SEQ * LANES), BF16),
            jax.ShapeDtypeStruct((CHUNK, STATE), BF16),
            jax.ShapeDtypeStruct((CHUNK, 2 * GROUP_HEADS), BF16),
        ],
        compiler_params=params(32),
        cost_estimate=pl.CostEstimate(
            flops=4_000_000_000, bytes_accessed=8 * MIB, transcendentals=4 * MIB
        ),
        name="inner",
    )(bounds, rows, steps, decays, gains)


def finish_kernel(state_ref, attn_ref, inner_ref, c_ref, reach_ref, ssm_ref, out_ref):
    @pl.when(pl.program_id(0) == 0)
    def _():
        for s in range(SEQ):
            for st in range(PER):
                at = st * LEN + (s % 2) * Q_ROWS
                out_ref[at : at + Q_ROWS, (s // 2) * LANES : (s // 2 + 1) * LANES] = attn_ref[
                    s, st * Q_ROWS : (st + 1) * Q_ROWS, :
                ]

    for k in range(PAIRS):
        pair = pl.program_id(0) * PAIRS + k
        cols = slice(k * LANES, (k + 1) * LANES)
        reached = jnp.dot(c_ref[...], state_ref[k], preferred_element_type=F32)
        reached = spread_heads(reach_ref[...], pair, LANES) * reached
        ssm_ref[:, cols] = (inner_ref[:, cols].astype(F32) + reached).astype(BF16)


def finish(both, inner_out, c_rows, reach):
    return pl.pallas_call(
        finish_kernel,
        grid=(SEQ // PAIRS,),
        in_specs=[
            pl.BlockSpec((PAIRS, STATE, LANES), lambda g: (g, 0, 0)),
            pl.BlockSpec((SEQ, HALF, LANES), lambda g: (0, 1, 0)),
            pl.BlockSpec((CHUNK, PAIRS * LANES), lambda g: (0, g)),
            whole(CHUNK, STATE),
            whole(CHUNK, 2 * GROUP_HEADS),
        ],
        out_specs=[
            pl.BlockSpec((CHUNK, PAIRS * LANES), lambda g: (0, g)),
            whole(CHUNK, PER * LANES),
        ],
        out_shape=[
            jax.ShapeDtypeStruct((CHUNK, SEQ * LANES), BF16),
            jax.ShapeDtypeStruct((CHUNK, PER * LANES), BF16),
        ],
        compiler_params=params(24),
        cost_estimate=pl.CostEstimate(
            flops=1_000_000_000, bytes_accessed=9 * MIB, transcendentals=0
        ),
        name="finish",
    )(both, both, inner_out, c_rows, reach)


def shards(
    stretch_x,
    stretch_bc,
    stretch_dt,
    stretch_q,
    stretch_kv,
    stretch_place,
    segment_ids,
    ssm_rate,
    dt_bias,
    skip_gain,
):
    seq_index = lax.axis_index("seq")
    mp_index = lax.axis_index("mp")
    exchange = functools.partial(lax.all_to_all, split_axis=0, concat_axis=0, tiled=True)
    cut = functools.partial(lax.dynamic_slice_in_dim, axis=0)

    my_docs = cut(segment_ids, mp_index * LEN, LEN)
    my_place = cut(stretch_place, mp_index, 1)
    info = jnp.concatenate([my_docs, my_place, jnp.zeros((LEN - 1,), jnp.int32)])
    info = jnp.broadcast_to(info.astype(F32)[None, :], (8, LANES))
    kv = lax.all_gather(exchange(pack_kv(stretch_kv), "mp"), "seq", axis=0, tiled=True)
    to_heads = pack(
        stretch_x, stretch_bc, stretch_q, stretch_dt.T.reshape(STRETCHES, LANES), info
    )
    hop = exchange(to_heads.reshape(STRETCHES, HOP_ROWS, LANES), ("seq", "mp"))

    told = hop[:, INFO_AT, :].astype(jnp.int32)
    places, docs = told[:, LEN], told[:, :LEN]
    order = jnp.arange(STRETCHES, dtype=jnp.int32)
    inv = jnp.sum(jnp.where(places[None, :] == order[:, None], order[None, :], 0), axis=1)
    bounds = jnp.stack(
        [jnp.sum((docs < v).astype(jnp.int32)) for v in range(DOCS)] + [seq_index % 2, seq_index]
    )
    to_owners, queries = place(inv, hop)
    own_rows = exchange(to_owners, "seq")
    group_first = mp_index * GROUP_HEADS
    biases = cut(dt_bias, group_first, GROUP_HEADS)
    rates = cut(ssm_rate, group_first, GROUP_HEADS)
    gains = cut(skip_gain, group_first, GROUP_HEADS)
    early, own_bounds = lax.optimization_barrier((attend(0, inv, bounds, kv, queries), bounds))
    late = attend(CALL_CHUNKS, inv, own_bounds, kv, queries)
    own_ends, steps, decays = ends(own_bounds, own_rows, biases[:, None], rates[:, None])
    arrived = exchange(own_ends, "seq")

    mine = hop[:, INFO_AT + 1, :].astype(F32)
    mine = mine.reshape(STRETCHES, 2, LEN) + cut(biases, 2 * seq_index, 2)[:, None]
    lost = -cut(rates, 2 * seq_index, 2) * jnp.sum(jax.nn.softplus(mine), axis=2)
    chunk_of = (places // PER)[None, :, None] == jnp.arange(SEQ)[:, None, None]
    lost = jnp.sum(jnp.where(chunk_of, lost[None], 0.0), axis=1)
    totals = jnp.repeat(jnp.exp(lost), HEAD_DIM, axis=1)

    both = exchange(chain(bounds, arrived, totals, early, late), "seq")
    inner_out, c_rows, reach = inner(
        bounds, own_rows, steps, decays, jnp.repeat(gains.reshape(SEQ, 1, 2), HEAD_DIM, axis=2)
    )
    return tuple(finish(both, inner_out, c_rows, reach))


def solution(mesh):
    return jax.shard_map(
        shards,
        mesh=mesh,
        in_specs=(
            P(("seq", "mp"), None),
            P(("seq", "mp"), None, None),
            P(("seq", "mp"), None),
            P(("seq", "mp"), None),
            P(("seq", "mp"), None, None),
            P("seq"),
            P("seq"),
            P(),
            P(),
            P(),
        ),
        out_specs=(P("seq", "mp"), P("seq", "mp")),
        check_vma=False,
    )
```

```python
import functools

import jax
import jax.numpy as jnp
from jax import lax
from jax.experimental import pallas as pl
from jax.experimental.pallas import tpu as pltpu
from jax.sharding import PartitionSpec as P

SSM_HEADS = 256
HEAD_DIM = 64
STATE = 256
GROUPS = 8
Q_HEADS = 64
KV_HEADS = 8
ATT_DIM = 128
LEN = 64
SEQ = 16
MP = 8
STRETCHES = 128
CHUNK = 512
HALF = 256
PER = CHUNK // LEN
LANES = 128
DOCS = 6
TOKENS = 8192

X_ROWS = LEN
BC_ROWS = 16
Q_ROWS = 32
BC_AT = X_ROWS
Q_AT = BC_AT + BC_ROWS
INFO_AT = Q_AT + Q_ROWS
INFO_ROWS = 8
HOP_ROWS = INFO_AT + INFO_ROWS
OWN_ROWS = X_ROWS + BC_ROWS
OWNER_ROWS = PER * OWN_ROWS + 16
K_AT, V_AT, G_ROWS = 0, 64, 128
GROUP_HEADS = SSM_HEADS // GROUPS
PAIRS = 2
MANY = 4
NEG_BIG = -1e30
F32 = jnp.float32
BF16 = jnp.bfloat16
MIB = 1 << 20


def params(mib):
    return pltpu.CompilerParams(vmem_limit_bytes=mib * MIB)


def pack_kernel(x_ref, bc_ref, q_ref, dt_ref, info_ref, hop_ref):
    row = lax.broadcasted_iota(jnp.int32, (INFO_ROWS, LANES), 0)
    told = jnp.where(row == 0, jnp.broadcast_to(info_ref[0:1, :], (INFO_ROWS, LANES)), 0.0)
    raw = dt_ref[...].astype(F32)
    for s in range(SEQ):
        hop_ref[s, 0, 0:X_ROWS, :] = x_ref[:, s * LANES : (s + 1) * LANES]
        col = (s % 2) * LANES
        hop_ref[s, 0, BC_AT : BC_AT + BC_ROWS, :] = bc_ref[
            pl.ds((s // 4) * 16, 16), (s % 4) // 2, col : col + LANES
        ]
        hop_ref[s, 0, Q_AT : Q_AT + Q_ROWS, :] = q_ref[
            pl.ds((s % 2) * Q_ROWS, Q_ROWS), (s // 2) * LANES : (s // 2 + 1) * LANES
        ]
        tile = jnp.where(row == 1, jnp.broadcast_to(raw[s : s + 1, :], (INFO_ROWS, LANES)), told)
        hop_ref[s, 0, INFO_AT:HOP_ROWS, :] = tile.astype(BF16)


def pack(x, bc, q, dt_rows, info):
    cols = lambda width: pl.BlockSpec((LEN, width), lambda m: (0, m))
    return pl.pallas_call(
        pack_kernel,
        grid=(MP,),
        in_specs=[
            cols(SEQ * LANES),
            pl.BlockSpec((LEN, 2, STATE), lambda m: (0, 0, m)),
            cols(PER * LANES),
            pl.BlockSpec((16, LANES), lambda m: (m, 0)),
            pl.BlockSpec((8, LANES), lambda m: (0, 0)),
        ],
        out_specs=pl.BlockSpec((SEQ, 1, HOP_ROWS, LANES), lambda m: (0, m, 0, 0)),
        out_shape=jax.ShapeDtypeStruct((SEQ, MP, HOP_ROWS, LANES), BF16),
        compiler_params=params(60),
        cost_estimate=pl.CostEstimate(flops=0, bytes_accessed=9 * MIB, transcendentals=0),
        name="pack",
    )(x, bc, q, dt_rows, info)


def pack_kv_kernel(kv_ref, out_ref):
    for m in range(MP):
        for half in range(2):
            out_ref[m, half * LEN : (half + 1) * LEN, :] = kv_ref[
                :, half, m * ATT_DIM : (m + 1) * ATT_DIM
            ]


def pack_kv(kv):
    return pl.pallas_call(
        pack_kv_kernel,
        grid=(1,),
        in_specs=[pl.BlockSpec((LEN, 2, KV_HEADS * ATT_DIM), lambda _: (0, 0, 0))],
        out_specs=pl.BlockSpec((MP, G_ROWS, LANES), lambda _: (0, 0, 0)),
        out_shape=jax.ShapeDtypeStruct((MP, G_ROWS, LANES), BF16),
        compiler_params=params(16),
        name="pack_kv",
    )(kv)


def place_kernel(inv_ref, hop_ref, out_ref, q_ref):
    lane = lax.broadcasted_iota(jnp.int32, (1, LANES), 1)
    early = lane < LEN
    row = lax.broadcasted_iota(jnp.int32, (16, LANES), 0)

    def chunk(c, carry):
        raw = []
        for k in range(PER):
            src = inv_ref[c * PER + k]
            out_ref[c, k * OWN_ROWS : (k + 1) * OWN_ROWS, :] = hop_ref[src, 0:OWN_ROWS, :]
            q_ref[c, k * Q_ROWS : (k + 1) * Q_ROWS, :] = hop_ref[src, Q_AT : Q_AT + Q_ROWS, :]
            raw.append(hop_ref[src, INFO_AT:HOP_ROWS, :].astype(F32)[1:2, :])
        turned = [jnp.roll(r, LEN, axis=1) for r in raw]
        tile = jnp.zeros((16, LANES), F32)
        for q in range(4):
            first = jnp.where(early, raw[2 * q], turned[2 * q + 1])
            second = jnp.where(early, turned[2 * q], raw[2 * q + 1])
            tile = jnp.where(row == q, first, jnp.where(row == 4 + q, second, tile))
        out_ref[c, PER * OWN_ROWS : OWNER_ROWS, :] = tile.astype(BF16)
        return carry

    lax.fori_loop(0, SEQ, chunk, 0)


def place(inv, hop):
    return pl.pallas_call(
        place_kernel,
        grid_spec=pltpu.PrefetchScalarGridSpec(
            num_scalar_prefetch=1,
            grid=(1,),
            in_specs=[pl.BlockSpec((STRETCHES, HOP_ROWS, LANES), lambda *_: (0, 0, 0))],
            out_specs=[
                pl.BlockSpec((SEQ, OWNER_ROWS, LANES), lambda *_: (0, 0, 0)),
                pl.BlockSpec((SEQ, PER * Q_ROWS, LANES), lambda *_: (0, 0, 0)),
            ],
        ),
        out_shape=[
            jax.ShapeDtypeStruct((SEQ, OWNER_ROWS, LANES), BF16),
            jax.ShapeDtypeStruct((SEQ, PER * Q_ROWS, LANES), BF16),
        ],
        compiler_params=params(60),
        cost_estimate=pl.CostEstimate(flops=0, bytes_accessed=6 * MIB, transcendentals=0),
        name="place",
    )(inv, hop)


def doc_start(bounds_ref, pos):
    first = jnp.zeros_like(pos)
    for v in range(1, DOCS):
        first = jnp.maximum(first, jnp.where(bounds_ref[v] <= pos, bounds_ref[v], 0))
    return first


def next_doc(bounds_ref, pos):
    after = jnp.full_like(pos, TOKENS)
    for v in range(1, DOCS):
        after = jnp.minimum(after, jnp.where(bounds_ref[v] > pos, bounds_ref[v], TOKENS))
    return after


def running_sums(rows):
    width = rows.shape[1]
    upper = lax.broadcasted_iota(jnp.int32, (width, width), 0) <= lax.broadcasted_iota(
        jnp.int32, (width, width), 1
    )
    upper = upper.astype(BF16)
    total = jnp.zeros_like(rows)
    for _ in range(3):
        part = rows.astype(BF16)
        rows = rows - part.astype(F32)
        total = total + jnp.dot(part, upper, preferred_element_type=F32)
    return total


def whole(*shape):
    return pl.BlockSpec(shape, lambda *_: (0,) * len(shape))


CALL_CHUNKS = SEQ // 2
SUM_ROWS = 16


def attend_kernel(
    begin,
    inv_ref, bounds_ref, kv_hbm, q_hbm, out_ref, kv_ref, q_ref, keys_all, turned, peak, acc, top_far, acc_far, sems
):
    kv_copy = pltpu.make_async_copy(kv_hbm, kv_ref, sems.at[0])
    q_copy = pltpu.make_async_copy(q_hbm, q_ref, sems.at[1])
    kv_copy.start()
    q_copy.start()
    half = bounds_ref[DOCS]
    q_rows = PER * Q_ROWS

    def arrange(i, carry):
        values = []
        for k in range(PER):
            src = inv_ref[i * PER + k]
            keys_all[pl.ds(i * CHUNK + k * LEN, LEN), :] = kv_ref[src, K_AT : K_AT + LEN, :]
            values.append(kv_ref[src, V_AT : V_AT + LEN, :])
        turned[i, 0:ATT_DIM, :] = jnp.transpose(jnp.concatenate(values, axis=0))
        turned[i, ATT_DIM : ATT_DIM + SUM_ROWS, :] = jnp.ones((SUM_ROWS, CHUNK), BF16)
        return carry

    kv_copy.wait()
    lax.fori_loop(0, begin + CALL_CHUNKS, arrange, 0, unroll=2)
    q_copy.wait()

    row = lax.broadcasted_iota(jnp.int32, (1, q_rows), 1)
    in_chunk = (row // Q_ROWS) * LEN + half * Q_ROWS + row % Q_ROWS
    key_at = lax.broadcasted_iota(jnp.int32, (CHUNK, q_rows), 0)
    scale = ATT_DIM**-0.5 * 1.4426950408889634

    def scores_of(queries, j):
        keys = keys_all[pl.ds(pl.multiple_of(j * CHUNK, CHUNK), CHUNK), :]
        return lax.dot_general(
            keys, queries, (((1,), (1,)), ((), ())), preferred_element_type=F32
        )

    def mixed(scores, top, j):
        probs = jnp.exp2((scores - top) * scale)
        return jnp.dot(turned[j], probs.astype(BF16), preferred_element_type=F32)

    def peak_of(scores):
        return jnp.max(scores, axis=0, keepdims=True)

    def near_tiles(n, carry):
        i = begin + n
        queries = q_ref[i]
        first = doc_start(bounds_ref, i * CHUNK + in_chunk) - i * CHUNK
        before = jnp.maximum(i - 1, 0)
        own = (key_at <= in_chunk) & (key_at >= first)
        here = jnp.where(own, scores_of(queries, i), NEG_BIG)
        there = jnp.where(key_at >= first + CHUNK, scores_of(queries, before), NEG_BIG)
        top = jnp.maximum(peak_of(here), peak_of(there))
        peak[n] = top
        acc[n] = mixed(here, top, i) + mixed(there, top, before)
        return carry

    lax.fori_loop(0, CALL_CHUNKS, near_tiles, 0, unroll=2)

    def far_tiles(n, carry):
        i = begin + n
        first = doc_start(bounds_ref, i * CHUNK) // CHUNK
        count = jnp.maximum(i - 1 - first, 0)
        fours = (count + 1) // 4
        queries = q_ref[i]
        q_doc = doc_start(bounds_ref, i * CHUNK + in_chunk)

        def add_tiles(last, number):
            old = top_far[...]
            scores = []
            for k in range(number):
                dots = scores_of(queries, jnp.maximum(last - k, 0))
                scores.append(jnp.where(key_at >= q_doc - (last - k) * CHUNK, dots, NEG_BIG))
            added, top = acc_far[...], old
            for k, dots in enumerate(scores):
                new = jnp.maximum(top, peak_of(dots))
                added = added * jnp.exp2((top - new) * scale) + mixed(
                    dots, new, jnp.maximum(last - k, 0)
                )
                top = new
            top_far[...] = top
            acc_far[...] = added

        @pl.when(count > 0)
        def _():
            top_far[...] = peak[n]
            acc_far[...] = acc[n]

            def four(t, c):
                add_tiles(i - 2 - 4 * t, 4)
                return c

            lax.fori_loop(0, fours, four, 0)

            @pl.when(count > 4 * fours)
            def _():
                add_tiles(i - 2 - 4 * fours, 2)

            acc[n] = acc_far[...]

        return carry

    lax.fori_loop(2 if begin == 0 else 0, CALL_CHUNKS, far_tiles, 0)

    def finish(i, carry):
        result = acc[i, 0:ATT_DIM, :] / acc[i, ATT_DIM : ATT_DIM + 1, :]
        out_ref[i] = jnp.transpose(result).astype(BF16)
        return carry

    lax.fori_loop(0, CALL_CHUNKS, finish, 0, unroll=4)


def attend(begin, inv, bounds, kv, queries):
    return pl.pallas_call(
        functools.partial(attend_kernel, begin),
        grid_spec=pltpu.PrefetchScalarGridSpec(
            num_scalar_prefetch=2,
            grid=(1,),
            in_specs=[pl.BlockSpec(memory_space=pl.ANY), pl.BlockSpec(memory_space=pl.ANY)],
            out_specs=whole(CALL_CHUNKS, HALF, LANES),
            scratch_shapes=[
                pltpu.VMEM((STRETCHES, G_ROWS, LANES), BF16),
                pltpu.VMEM((SEQ, PER * Q_ROWS, LANES), BF16),
                pltpu.VMEM((TOKENS, ATT_DIM), BF16),
                pltpu.VMEM((SEQ, ATT_DIM + SUM_ROWS, CHUNK), BF16),
                pltpu.VMEM((CALL_CHUNKS, 1, PER * Q_ROWS), F32),
                pltpu.VMEM((CALL_CHUNKS, ATT_DIM + SUM_ROWS, PER * Q_ROWS), F32),
                pltpu.VMEM((1, PER * Q_ROWS), F32),
                pltpu.VMEM((ATT_DIM + SUM_ROWS, PER * Q_ROWS), F32),
                pltpu.SemaphoreType.DMA((2,)),
            ],
        ),
        out_shape=jax.ShapeDtypeStruct((CALL_CHUNKS, HALF, LANES), BF16),
        compiler_params=params(60),
        cost_estimate=pl.CostEstimate(flops=4_000_000_000, bytes_accessed=6 * MIB, transcendentals=4 * MIB),
        name=f"attend{begin}",
    )(inv, bounds, kv, queries)


def pair_lanes(first, width, rows):
    row = lax.broadcasted_iota(jnp.int32, (rows, width), 0) % GROUP_HEADS
    lane = lax.broadcasted_iota(jnp.int32, (rows, width), 1)
    return (row == first + lane // (width // 2)).astype(BF16)


def as_parts(rows, count):
    left = jnp.transpose(rows)
    parts = []
    for _ in range(count):
        part = left.astype(BF16)
        parts.append(part)
        left = left - part.astype(F32)
    return jnp.concatenate(parts, axis=1)


def spread_heads(parts, pair, width):
    sel = pair_lanes(2 * pair, width, parts.shape[1])
    return jnp.dot(parts, sel, preferred_element_type=F32)


def channels(own_ref, pair):
    parts = [own_ref[pair, st * OWN_ROWS : st * OWN_ROWS + X_ROWS, :] for st in range(PER)]
    return jnp.concatenate(parts, axis=0).astype(F32)


def gather_proj(own_ref, proj, group):
    for tg in range(4):
        for cg in range(2):
            for st in range(PER):
                at = st * OWN_ROWS + X_ROWS
                proj[st, tg, :, cg * LANES : (cg + 1) * LANES] = own_ref[
                    tg * 4 + group * 2 + cg, at : at + BC_ROWS, :
                ]


def softplus(v):
    return jnp.maximum(v, 0.0) + jnp.log1p(jnp.exp(-jnp.abs(v)))


def ends_kernel(bounds_ref, own_ref, bias_ref, rate_ref, out_ref, step_ref, decay_ref, proj, turned, parts):
    base = bounds_ref[DOCS + 1] * CHUNK

    @pl.when(pl.program_id(0) == 0)
    def _():
        for s in range(SEQ):
            tile = own_ref[s, PER * OWN_ROWS : OWNER_ROWS, :].astype(F32)
            for head in range(2):
                for q in range(4):
                    step_ref[2 * s + head : 2 * s + head + 1, q * LANES : (q + 1) * LANES] = tile[
                        4 * head + q : 4 * head + q + 1, :
                    ]
        step_ref[...] = softplus(step_ref[...] + bias_ref[...])
        decay_ref[...] = -rate_ref[...] * step_ref[...]
        gather_proj(own_ref, proj, 0)
        turned[...] = jnp.transpose(proj[...].reshape(CHUNK, STATE))
        log_sum = running_sums(decay_ref[...])
        pos = lax.broadcasted_iota(jnp.int32, (GROUP_HEADS, CHUNK), 1) + base
        last_doc = doc_start(bounds_ref, base + CHUNK - 1)
        load = jnp.exp(log_sum[:, CHUNK - 1 : CHUNK] - log_sum)
        parts[...] = as_parts(jnp.where(pos >= last_doc, step_ref[...] * load, 0.0), 2)

    for k in range(MANY):
        pair = pl.program_id(0) * MANY + k
        xs = channels(own_ref, pair)
        driven = (spread_heads(parts[...], pair, LANES) * xs).astype(BF16)
        out_ref[k] = jnp.dot(turned[...], driven, preferred_element_type=F32).astype(BF16)


def ends(bounds, rows, biases, rates):
    return pl.pallas_call(
        ends_kernel,
        grid_spec=pltpu.PrefetchScalarGridSpec(
            num_scalar_prefetch=1,
            grid=(SEQ // MANY,),
            in_specs=[
                whole(SEQ, OWNER_ROWS, LANES),
                whole(GROUP_HEADS, 1),
                whole(GROUP_HEADS, 1),
            ],
            out_specs=[
                pl.BlockSpec((MANY, STATE, LANES), lambda g, *_: (g, 0, 0)),
                whole(GROUP_HEADS, CHUNK),
                whole(GROUP_HEADS, CHUNK),
            ],
            scratch_shapes=[
                pltpu.VMEM((PER, 4, 16, STATE), BF16),
                pltpu.VMEM((STATE, CHUNK), BF16),
                pltpu.VMEM((CHUNK, 2 * GROUP_HEADS), BF16),
            ],
        ),
        out_shape=[
            jax.ShapeDtypeStruct((SEQ, STATE, LANES), BF16),
            jax.ShapeDtypeStruct((GROUP_HEADS, CHUNK), F32),
            jax.ShapeDtypeStruct((GROUP_HEADS, CHUNK), F32),
        ],
        compiler_params=params(24),
        cost_estimate=pl.CostEstimate(
            flops=1_000_000_000, bytes_accessed=4 * MIB, transcendentals=0
        ),
        name="ends",
    )(bounds, rows, biases, rates)


def chain_kernel(bounds_ref, ends_ref, total_ref, early_ref, late_ref, out_ref):
    state = jnp.zeros((STATE, LANES), F32)
    for c in range(SEQ):
        out_ref[c, 0:STATE, :] = state.astype(BF16)
        rows = early_ref if c < CALL_CHUNKS else late_ref
        out_ref[c, STATE:CHUNK, :] = rows[c % CALL_CHUNKS]
        if c < SEQ - 1:
            last_doc = doc_start(bounds_ref, jnp.int32((c + 1) * CHUNK - 1))
            keep = jnp.where(last_doc < c * CHUNK, total_ref[c : c + 1, :], 0.0)
            state = keep * state + ends_ref[c].astype(F32)


def chain(bounds, arrived, totals, early, late):
    return pl.pallas_call(
        chain_kernel,
        grid_spec=pltpu.PrefetchScalarGridSpec(
            num_scalar_prefetch=1,
            grid=(1,),
            in_specs=[
                whole(SEQ, STATE, LANES),
                whole(SEQ, LANES),
                whole(CALL_CHUNKS, HALF, LANES),
                whole(CALL_CHUNKS, HALF, LANES),
            ],
            out_specs=whole(SEQ, CHUNK, LANES),
        ),
        out_shape=jax.ShapeDtypeStruct((SEQ, CHUNK, LANES), BF16),
        compiler_params=params(24),
        cost_estimate=pl.CostEstimate(flops=0, bytes_accessed=5 * MIB, transcendentals=0),
        name="chain",
    )(bounds, arrived, totals, early, late)


def inner_kernel(
    bounds_ref,
    own_ref,
    step_ref,
    decay_ref,
    gain_ref,
    out_ref,
    c_out,
    reach_out,
    proj_b,
    proj_c,
    turned,
    grams,
    sums,
    sum_rows,
    sum_parts,
    step_parts,
    load_parts,
    reach_parts,
):
    base = bounds_ref[DOCS + 1] * CHUNK

    @pl.when(pl.program_id(0) == 0)
    def _():
        gather_proj(own_ref, proj_b, 0)
        gather_proj(own_ref, proj_c, 1)
        row = lax.broadcasted_iota(jnp.int32, (HALF, 1), 0)
        col = lax.broadcasted_iota(jnp.int32, (HALF, HALF), 1)
        for blk in range(2):
            b_blk = proj_b[blk * 4 : blk * 4 + 4].reshape(HALF, STATE)
            c_blk = proj_c[blk * 4 : blk * 4 + 4].reshape(HALF, STATE)
            c_out[blk * HALF : (blk + 1) * HALF, :] = c_blk
            gram = lax.dot_general(
                c_blk, b_blk, (((1,), (1,)), ((), ())), preferred_element_type=F32
            )
            start = base + blk * HALF
            first = doc_start(bounds_ref, start + row) - start
            grams[blk] = jnp.where((col <= row) & (col >= first), gram, 0.0)
            if blk == 0:
                turned[...] = jnp.transpose(b_blk)
            sums[:, blk * HALF : (blk + 1) * HALF] = running_sums(
                decay_ref[:, blk * HALF : (blk + 1) * HALF]
            )
        log_sum = sums[...]
        for head in range(GROUP_HEADS):
            sum_rows[head] = log_sum[head : head + 1, :]
        log_half = log_sum[:, HALF - 1 : HALF]
        pos = lax.broadcasted_iota(jnp.int32, (GROUP_HEADS, HALF), 1) + base
        mid_pos = base + HALF - 1
        load = jnp.where(
            pos >= doc_start(bounds_ref, mid_pos), jnp.exp(log_half - log_sum[:, :HALF]), 0.0
        )
        later = jnp.where(
            pos + HALF < next_doc(bounds_ref, mid_pos), jnp.exp(log_sum[:, HALF:]), 0.0
        )
        whole_sum = jnp.concatenate([log_sum[:, :HALF], log_sum[:, HALF:] + log_half], axis=1)
        pos = lax.broadcasted_iota(jnp.int32, (GROUP_HEADS, CHUNK), 1) + base
        reach_end = jnp.where(base > 0, next_doc(bounds_ref, base - 1), 0)
        reach = jnp.where(pos < reach_end, jnp.exp(whole_sum), 0.0)
        sum_parts[...] = as_parts(log_sum, 3)
        step_parts[...] = as_parts(step_ref[...], 2)
        load_parts[...] = as_parts(step_ref[:, :HALF] * load, 2)
        reach_parts[...] = as_parts(later, 2)
        reach_out[...] = as_parts(reach, 2)

    first_head = lax.broadcasted_iota(jnp.int32, (1, LANES), 1) < HEAD_DIM
    quarter = HALF // 2
    for k in range(PAIRS):
        pair = pl.program_id(0) * PAIRS + k
        gain = gain_ref[pair]
        sum_cols = spread_heads(sum_parts[...], pair, 2 * LANES)
        steps = spread_heads(step_parts[...], pair, LANES)
        loads = spread_heads(load_parts[...], pair, LANES)
        reach = spread_heads(reach_parts[...], pair, LANES)
        xs = channels(own_ref, pair)
        driven = (steps * xs).astype(BF16)
        loaded = (loads * xs[:HALF]).astype(BF16)
        state = jnp.dot(turned[...], loaded, preferred_element_type=F32).astype(BF16)
        for blk in range(2):
            for part in range(2):
                at = blk * HALF + part * quarter
                width = (part + 1) * quarter
                heads = []
                for head in range(2):
                    log_row = sum_rows[2 * pair + head][:, blk * HALF : blk * HALF + width]
                    log_col = sum_cols[at : at + quarter, head * LANES : (head + 1) * LANES]
                    log_col = jnp.concatenate([log_col] * (part + 1), axis=1)
                    weight = jnp.exp(jnp.minimum(log_col - log_row, 0.0))
                    gram = grams[blk, part * quarter : (part + 1) * quarter, 0:width]
                    heads.append(
                        jnp.dot(
                            (gram * weight).astype(BF16),
                            driven[blk * HALF : blk * HALF + width],
                            preferred_element_type=F32,
                        )
                    )
                result = jnp.where(first_head, heads[0], heads[1]) + gain * xs[at : at + quarter]
                if blk == 1:
                    c_part = c_out[at : at + quarter, :]
                    result += reach[part * quarter : (part + 1) * quarter] * jnp.dot(
                        c_part, state, preferred_element_type=F32
                    )
                out_ref[at : at + quarter, k * LANES : (k + 1) * LANES] = result.astype(BF16)


def inner(bounds, rows, steps, decays, gains):
    return pl.pallas_call(
        inner_kernel,
        grid_spec=pltpu.PrefetchScalarGridSpec(
            num_scalar_prefetch=1,
            grid=(SEQ // PAIRS,),
            in_specs=[
                whole(SEQ, OWNER_ROWS, LANES),
                whole(GROUP_HEADS, CHUNK),
                whole(GROUP_HEADS, CHUNK),
                whole(SEQ, 1, LANES),
            ],
            out_specs=[
                pl.BlockSpec((CHUNK, PAIRS * LANES), lambda g, *_: (0, g)),
                whole(CHUNK, STATE),
                whole(CHUNK, 2 * GROUP_HEADS),
            ],
            scratch_shapes=[
                pltpu.VMEM((PER, 4, 16, STATE), BF16),
                pltpu.VMEM((PER, 4, 16, STATE), BF16),
                pltpu.VMEM((STATE, HALF), BF16),
                pltpu.VMEM((2, HALF, HALF), F32),
                pltpu.VMEM((GROUP_HEADS, CHUNK), F32),
                pltpu.VMEM((GROUP_HEADS, 1, CHUNK), F32),
                pltpu.VMEM((CHUNK, 3 * GROUP_HEADS), BF16),
                pltpu.VMEM((CHUNK, 2 * GROUP_HEADS), BF16),
                pltpu.VMEM((HALF, 2 * GROUP_HEADS), BF16),
                pltpu.VMEM((HALF, 2 * GROUP_HEADS), BF16),
            ],
        ),
        out_shape=[
            jax.ShapeDtypeStruct((CHUNK, SEQ * LANES), BF16),
            jax.ShapeDtypeStruct((CHUNK, STATE), BF16),
            jax.ShapeDtypeStruct((CHUNK, 2 * GROUP_HEADS), BF16),
        ],
        compiler_params=params(32),
        cost_estimate=pl.CostEstimate(
            flops=4_000_000_000, bytes_accessed=8 * MIB, transcendentals=4 * MIB
        ),
        name="inner",
    )(bounds, rows, steps, decays, gains)


def finish_kernel(state_ref, attn_ref, inner_ref, c_ref, reach_ref, ssm_ref, out_ref):
    @pl.when(pl.program_id(0) == 0)
    def _():
        for s in range(SEQ):
            for st in range(PER):
                at = st * LEN + (s % 2) * Q_ROWS
                out_ref[at : at + Q_ROWS, (s // 2) * LANES : (s // 2 + 1) * LANES] = attn_ref[
                    s, st * Q_ROWS : (st + 1) * Q_ROWS, :
                ]

    for k in range(MANY):
        pair = pl.program_id(0) * MANY + k
        cols = slice(k * LANES, (k + 1) * LANES)
        reached = jnp.dot(c_ref[...], state_ref[k], preferred_element_type=F32)
        reached = spread_heads(reach_ref[...], pair, LANES) * reached
        ssm_ref[:, cols] = (inner_ref[:, cols].astype(F32) + reached).astype(BF16)


def finish(both, inner_out, c_rows, reach):
    return pl.pallas_call(
        finish_kernel,
        grid=(SEQ // MANY,),
        in_specs=[
            pl.BlockSpec((MANY, STATE, LANES), lambda g: (g, 0, 0)),
            pl.BlockSpec((SEQ, HALF, LANES), lambda g: (0, 1, 0)),
            pl.BlockSpec((CHUNK, MANY * LANES), lambda g: (0, g)),
            whole(CHUNK, STATE),
            whole(CHUNK, 2 * GROUP_HEADS),
        ],
        out_specs=[
            pl.BlockSpec((CHUNK, MANY * LANES), lambda g: (0, g)),
            whole(CHUNK, PER * LANES),
        ],
        out_shape=[
            jax.ShapeDtypeStruct((CHUNK, SEQ * LANES), BF16),
            jax.ShapeDtypeStruct((CHUNK, PER * LANES), BF16),
        ],
        compiler_params=params(24),
        cost_estimate=pl.CostEstimate(
            flops=1_000_000_000, bytes_accessed=9 * MIB, transcendentals=0
        ),
        name="finish",
    )(both, both, inner_out, c_rows, reach)


def shards(
    stretch_x,
    stretch_bc,
    stretch_dt,
    stretch_q,
    stretch_kv,
    stretch_place,
    segment_ids,
    ssm_rate,
    dt_bias,
    skip_gain,
):
    seq_index = lax.axis_index("seq")
    mp_index = lax.axis_index("mp")
    exchange = functools.partial(lax.all_to_all, split_axis=0, concat_axis=0, tiled=True)
    cut = functools.partial(lax.dynamic_slice_in_dim, axis=0)

    my_docs = cut(segment_ids, mp_index * LEN, LEN)
    my_place = cut(stretch_place, mp_index, 1)
    info = jnp.concatenate([my_docs, my_place, jnp.zeros((LEN - 1,), jnp.int32)])
    info = jnp.broadcast_to(info.astype(F32)[None, :], (8, LANES))
    kv = lax.all_gather(exchange(pack_kv(stretch_kv), "mp"), "seq", axis=0, tiled=True)
    to_heads = pack(
        stretch_x, stretch_bc, stretch_q, stretch_dt.T.reshape(STRETCHES, LANES), info
    )
    hop = exchange(to_heads.reshape(STRETCHES, HOP_ROWS, LANES), ("seq", "mp"))

    told = hop[:, INFO_AT, :].astype(jnp.int32)
    places, docs = told[:, LEN], told[:, :LEN]
    order = jnp.arange(STRETCHES, dtype=jnp.int32)
    inv = jnp.sum(jnp.where(places[None, :] == order[:, None], order[None, :], 0), axis=1)
    bounds = jnp.stack(
        [jnp.sum((docs < v).astype(jnp.int32)) for v in range(DOCS)] + [seq_index % 2, seq_index]
    )
    to_owners, queries = place(inv, hop)
    own_rows = exchange(to_owners, "seq")
    group_first = mp_index * GROUP_HEADS
    biases = cut(dt_bias, group_first, GROUP_HEADS)
    rates = cut(ssm_rate, group_first, GROUP_HEADS)
    gains = cut(skip_gain, group_first, GROUP_HEADS)
    early, own_bounds = lax.optimization_barrier((attend(0, inv, bounds, kv, queries), bounds))
    late = attend(CALL_CHUNKS, inv, own_bounds, kv, queries)
    own_ends, steps, decays = ends(own_bounds, own_rows, biases[:, None], rates[:, None])
    arrived = exchange(own_ends, "seq")

    mine = hop[:, INFO_AT + 1, :].astype(F32)
    mine = mine.reshape(STRETCHES, 2, LEN) + cut(biases, 2 * seq_index, 2)[:, None]
    lost = -cut(rates, 2 * seq_index, 2) * jnp.sum(jax.nn.softplus(mine), axis=2)
    chunk_of = (places // PER)[None, :, None] == jnp.arange(SEQ)[:, None, None]
    lost = jnp.sum(jnp.where(chunk_of, lost[None], 0.0), axis=1)
    totals = jnp.repeat(jnp.exp(lost), HEAD_DIM, axis=1)

    both = exchange(chain(bounds, arrived, totals, early, late), "seq")
    inner_out, c_rows, reach = inner(
        bounds, own_rows, steps, decays, jnp.repeat(gains.reshape(SEQ, 1, 2), HEAD_DIM, axis=2)
    )
    return tuple(finish(both, inner_out, c_rows, reach))


def solution(mesh):
    return jax.shard_map(
        shards,
        mesh=mesh,
        in_specs=(
            P(("seq", "mp"), None),
            P(("seq", "mp"), None, None),
            P(("seq", "mp"), None),
            P(("seq", "mp"), None),
            P(("seq", "mp"), None, None),
            P("seq"),
            P("seq"),
            P(),
            P(),
            P(),
        ),
        out_specs=(P("seq", "mp"), P("seq", "mp")),
        check_vma=False,
    )
```

```python
import functools

import jax
import jax.numpy as jnp
from jax import lax
from jax.experimental import pallas as pl
from jax.experimental.pallas import tpu as pltpu
from jax.sharding import PartitionSpec as P

SSM_HEADS = 256
HEAD_DIM = 64
STATE = 256
GROUPS = 8
Q_HEADS = 64
KV_HEADS = 8
ATT_DIM = 128
LEN = 64
SEQ = 16
MP = 8
STRETCHES = 128
CHUNK = 512
HALF = 256
PER = CHUNK // LEN
LANES = 128
DOCS = 6
TOKENS = 8192

X_ROWS = LEN
BC_ROWS = 16
Q_ROWS = 32
BC_AT = X_ROWS
Q_AT = BC_AT + BC_ROWS
INFO_AT = Q_AT + Q_ROWS
INFO_ROWS = 8
HOP_ROWS = INFO_AT + INFO_ROWS
OWN_ROWS = X_ROWS + BC_ROWS
OWNER_ROWS = PER * OWN_ROWS + 16
K_AT, V_AT, G_ROWS = 0, 64, 128
GROUP_HEADS = SSM_HEADS // GROUPS
PAIRS = 2
MANY = 8
NEG_BIG = -1e30
F32 = jnp.float32
BF16 = jnp.bfloat16
MIB = 1 << 20


def params(mib):
    return pltpu.CompilerParams(vmem_limit_bytes=mib * MIB)


def pack_kernel(x_ref, bc_ref, q_ref, dt_ref, info_ref, hop_ref):
    row = lax.broadcasted_iota(jnp.int32, (INFO_ROWS, LANES), 0)
    told = jnp.where(row == 0, jnp.broadcast_to(info_ref[0:1, :], (INFO_ROWS, LANES)), 0.0)
    raw = dt_ref[...].astype(F32)
    for s in range(SEQ):
        hop_ref[s, 0, 0:X_ROWS, :] = x_ref[:, s * LANES : (s + 1) * LANES]
        col = (s % 2) * LANES
        hop_ref[s, 0, BC_AT : BC_AT + BC_ROWS, :] = bc_ref[
            pl.ds((s // 4) * 16, 16), (s % 4) // 2, col : col + LANES
        ]
        hop_ref[s, 0, Q_AT : Q_AT + Q_ROWS, :] = q_ref[
            pl.ds((s % 2) * Q_ROWS, Q_ROWS), (s // 2) * LANES : (s // 2 + 1) * LANES
        ]
        tile = jnp.where(row == 1, jnp.broadcast_to(raw[s : s + 1, :], (INFO_ROWS, LANES)), told)
        hop_ref[s, 0, INFO_AT:HOP_ROWS, :] = tile.astype(BF16)


def pack(x, bc, q, dt_rows, info):
    cols = lambda width: pl.BlockSpec((LEN, width), lambda m: (0, m))
    return pl.pallas_call(
        pack_kernel,
        grid=(MP,),
        in_specs=[
            cols(SEQ * LANES),
            pl.BlockSpec((LEN, 2, STATE), lambda m: (0, 0, m)),
            cols(PER * LANES),
            pl.BlockSpec((16, LANES), lambda m: (m, 0)),
            pl.BlockSpec((8, LANES), lambda m: (0, 0)),
        ],
        out_specs=pl.BlockSpec((SEQ, 1, HOP_ROWS, LANES), lambda m: (0, m, 0, 0)),
        out_shape=jax.ShapeDtypeStruct((SEQ, MP, HOP_ROWS, LANES), BF16),
        compiler_params=params(60),
        cost_estimate=pl.CostEstimate(flops=0, bytes_accessed=9 * MIB, transcendentals=0),
        name="pack",
    )(x, bc, q, dt_rows, info)


def pack_kv_kernel(kv_ref, out_ref):
    for m in range(MP):
        for half in range(2):
            out_ref[m, half * LEN : (half + 1) * LEN, :] = kv_ref[
                :, half, m * ATT_DIM : (m + 1) * ATT_DIM
            ]


def pack_kv(kv):
    return pl.pallas_call(
        pack_kv_kernel,
        grid=(1,),
        in_specs=[pl.BlockSpec((LEN, 2, KV_HEADS * ATT_DIM), lambda _: (0, 0, 0))],
        out_specs=pl.BlockSpec((MP, G_ROWS, LANES), lambda _: (0, 0, 0)),
        out_shape=jax.ShapeDtypeStruct((MP, G_ROWS, LANES), BF16),
        compiler_params=params(16),
        name="pack_kv",
    )(kv)


def place_kernel(inv_ref, hop_ref, out_ref, q_ref):
    lane = lax.broadcasted_iota(jnp.int32, (1, LANES), 1)
    early = lane < LEN
    row = lax.broadcasted_iota(jnp.int32, (16, LANES), 0)

    def chunk(c, carry):
        raw = []
        for k in range(PER):
            src = inv_ref[c * PER + k]
            out_ref[c, k * OWN_ROWS : (k + 1) * OWN_ROWS, :] = hop_ref[src, 0:OWN_ROWS, :]
            q_ref[c, k * Q_ROWS : (k + 1) * Q_ROWS, :] = hop_ref[src, Q_AT : Q_AT + Q_ROWS, :]
            raw.append(hop_ref[src, INFO_AT:HOP_ROWS, :].astype(F32)[1:2, :])
        turned = [jnp.roll(r, LEN, axis=1) for r in raw]
        tile = jnp.zeros((16, LANES), F32)
        for q in range(4):
            first = jnp.where(early, raw[2 * q], turned[2 * q + 1])
            second = jnp.where(early, turned[2 * q], raw[2 * q + 1])
            tile = jnp.where(row == q, first, jnp.where(row == 4 + q, second, tile))
        out_ref[c, PER * OWN_ROWS : OWNER_ROWS, :] = tile.astype(BF16)
        return carry

    lax.fori_loop(0, SEQ, chunk, 0)


def place(inv, hop):
    return pl.pallas_call(
        place_kernel,
        grid_spec=pltpu.PrefetchScalarGridSpec(
            num_scalar_prefetch=1,
            grid=(1,),
            in_specs=[pl.BlockSpec((STRETCHES, HOP_ROWS, LANES), lambda *_: (0, 0, 0))],
            out_specs=[
                pl.BlockSpec((SEQ, OWNER_ROWS, LANES), lambda *_: (0, 0, 0)),
                pl.BlockSpec((SEQ, PER * Q_ROWS, LANES), lambda *_: (0, 0, 0)),
            ],
        ),
        out_shape=[
            jax.ShapeDtypeStruct((SEQ, OWNER_ROWS, LANES), BF16),
            jax.ShapeDtypeStruct((SEQ, PER * Q_ROWS, LANES), BF16),
        ],
        compiler_params=params(60),
        cost_estimate=pl.CostEstimate(flops=0, bytes_accessed=6 * MIB, transcendentals=0),
        name="place",
    )(inv, hop)


def doc_start(bounds_ref, pos):
    first = jnp.zeros_like(pos)
    for v in range(1, DOCS):
        first = jnp.maximum(first, jnp.where(bounds_ref[v] <= pos, bounds_ref[v], 0))
    return first


def next_doc(bounds_ref, pos):
    after = jnp.full_like(pos, TOKENS)
    for v in range(1, DOCS):
        after = jnp.minimum(after, jnp.where(bounds_ref[v] > pos, bounds_ref[v], TOKENS))
    return after


def running_sums(rows):
    width = rows.shape[1]
    upper = lax.broadcasted_iota(jnp.int32, (width, width), 0) <= lax.broadcasted_iota(
        jnp.int32, (width, width), 1
    )
    upper = upper.astype(BF16)
    total = jnp.zeros_like(rows)
    for _ in range(3):
        part = rows.astype(BF16)
        rows = rows - part.astype(F32)
        total = total + jnp.dot(part, upper, preferred_element_type=F32)
    return total


def whole(*shape):
    return pl.BlockSpec(shape, lambda *_: (0,) * len(shape))


CALL_CHUNKS = SEQ // 2
SUM_ROWS = 16


def attend_kernel(
    begin,
    inv_ref, bounds_ref, kv_hbm, q_hbm, out_ref, kv_ref, q_ref, keys_all, turned, peak, acc, top_far, acc_far, sems
):
    kv_copy = pltpu.make_async_copy(kv_hbm, kv_ref, sems.at[0])
    q_copy = pltpu.make_async_copy(q_hbm, q_ref, sems.at[1])
    kv_copy.start()
    q_copy.start()
    half = bounds_ref[DOCS]
    q_rows = PER * Q_ROWS

    def arrange(i, carry):
        values = []
        for k in range(PER):
            src = inv_ref[i * PER + k]
            keys_all[pl.ds(i * CHUNK + k * LEN, LEN), :] = kv_ref[src, K_AT : K_AT + LEN, :]
            values.append(kv_ref[src, V_AT : V_AT + LEN, :])
        turned[i, 0:ATT_DIM, :] = jnp.transpose(jnp.concatenate(values, axis=0))
        turned[i, ATT_DIM : ATT_DIM + SUM_ROWS, :] = jnp.ones((SUM_ROWS, CHUNK), BF16)
        return carry

    kv_copy.wait()
    lax.fori_loop(0, begin + CALL_CHUNKS, arrange, 0, unroll=2)
    q_copy.wait()

    row = lax.broadcasted_iota(jnp.int32, (1, q_rows), 1)
    in_chunk = (row // Q_ROWS) * LEN + half * Q_ROWS + row % Q_ROWS
    key_at = lax.broadcasted_iota(jnp.int32, (CHUNK, q_rows), 0)
    scale = ATT_DIM**-0.5 * 1.4426950408889634

    def scores_of(queries, j):
        keys = keys_all[pl.ds(pl.multiple_of(j * CHUNK, CHUNK), CHUNK), :]
        return lax.dot_general(
            keys, queries, (((1,), (1,)), ((), ())), preferred_element_type=F32
        )

    def mixed(scores, top, j):
        probs = jnp.exp2((scores - top) * scale)
        return jnp.dot(turned[j], probs.astype(BF16), preferred_element_type=F32)

    def peak_of(scores):
        return jnp.max(scores, axis=0, keepdims=True)

    def near_tiles(n, carry):
        i = begin + n
        queries = q_ref[i]
        first = doc_start(bounds_ref, i * CHUNK + in_chunk) - i * CHUNK
        before = jnp.maximum(i - 1, 0)
        own = (key_at <= in_chunk) & (key_at >= first)
        here = jnp.where(own, scores_of(queries, i), NEG_BIG)
        there = jnp.where(key_at >= first + CHUNK, scores_of(queries, before), NEG_BIG)
        top = jnp.maximum(peak_of(here), peak_of(there))
        peak[n] = top
        acc[n] = mixed(here, top, i) + mixed(there, top, before)
        return carry

    lax.fori_loop(0, CALL_CHUNKS, near_tiles, 0, unroll=2)

    def far_tiles(n, carry):
        i = begin + n
        first = doc_start(bounds_ref, i * CHUNK) // CHUNK
        count = jnp.maximum(i - 1 - first, 0)
        fours = (count + 1) // 4
        queries = q_ref[i]
        q_doc = doc_start(bounds_ref, i * CHUNK + in_chunk)

        def add_tiles(last, number):
            old = top_far[...]
            scores = []
            for k in range(number):
                dots = scores_of(queries, jnp.maximum(last - k, 0))
                scores.append(jnp.where(key_at >= q_doc - (last - k) * CHUNK, dots, NEG_BIG))
            added, top = acc_far[...], old
            for k, dots in enumerate(scores):
                new = jnp.maximum(top, peak_of(dots))
                added = added * jnp.exp2((top - new) * scale) + mixed(
                    dots, new, jnp.maximum(last - k, 0)
                )
                top = new
            top_far[...] = top
            acc_far[...] = added

        @pl.when(count > 0)
        def _():
            top_far[...] = peak[n]
            acc_far[...] = acc[n]

            def four(t, c):
                add_tiles(i - 2 - 4 * t, 4)
                return c

            lax.fori_loop(0, fours, four, 0)

            @pl.when(count > 4 * fours)
            def _():
                add_tiles(i - 2 - 4 * fours, 2)

            acc[n] = acc_far[...]

        return carry

    lax.fori_loop(2 if begin == 0 else 0, CALL_CHUNKS, far_tiles, 0)

    def finish(i, carry):
        result = acc[i, 0:ATT_DIM, :] / acc[i, ATT_DIM : ATT_DIM + 1, :]
        out_ref[i] = jnp.transpose(result).astype(BF16)
        return carry

    lax.fori_loop(0, CALL_CHUNKS, finish, 0, unroll=4)


def attend(begin, inv, bounds, kv, queries):
    return pl.pallas_call(
        functools.partial(attend_kernel, begin),
        grid_spec=pltpu.PrefetchScalarGridSpec(
            num_scalar_prefetch=2,
            grid=(1,),
            in_specs=[pl.BlockSpec(memory_space=pl.ANY), pl.BlockSpec(memory_space=pl.ANY)],
            out_specs=whole(CALL_CHUNKS, HALF, LANES),
            scratch_shapes=[
                pltpu.VMEM((STRETCHES, G_ROWS, LANES), BF16),
                pltpu.VMEM((SEQ, PER * Q_ROWS, LANES), BF16),
                pltpu.VMEM((TOKENS, ATT_DIM), BF16),
                pltpu.VMEM((SEQ, ATT_DIM + SUM_ROWS, CHUNK), BF16),
                pltpu.VMEM((CALL_CHUNKS, 1, PER * Q_ROWS), F32),
                pltpu.VMEM((CALL_CHUNKS, ATT_DIM + SUM_ROWS, PER * Q_ROWS), F32),
                pltpu.VMEM((1, PER * Q_ROWS), F32),
                pltpu.VMEM((ATT_DIM + SUM_ROWS, PER * Q_ROWS), F32),
                pltpu.SemaphoreType.DMA((2,)),
            ],
        ),
        out_shape=jax.ShapeDtypeStruct((CALL_CHUNKS, HALF, LANES), BF16),
        compiler_params=params(60),
        cost_estimate=pl.CostEstimate(flops=4_000_000_000, bytes_accessed=6 * MIB, transcendentals=4 * MIB),
        name=f"attend{begin}",
    )(inv, bounds, kv, queries)


def pair_lanes(first, width, rows):
    row = lax.broadcasted_iota(jnp.int32, (rows, width), 0) % GROUP_HEADS
    lane = lax.broadcasted_iota(jnp.int32, (rows, width), 1)
    return (row == first + lane // (width // 2)).astype(BF16)


def as_parts(rows, count):
    left = jnp.transpose(rows)
    parts = []
    for _ in range(count):
        part = left.astype(BF16)
        parts.append(part)
        left = left - part.astype(F32)
    return jnp.concatenate(parts, axis=1)


def spread_heads(parts, pair, width):
    sel = pair_lanes(2 * pair, width, parts.shape[1])
    return jnp.dot(parts, sel, preferred_element_type=F32)


def channels(own_ref, pair):
    parts = [own_ref[pair, st * OWN_ROWS : st * OWN_ROWS + X_ROWS, :] for st in range(PER)]
    return jnp.concatenate(parts, axis=0).astype(F32)


def gather_proj(own_ref, proj, group):
    for tg in range(4):
        for cg in range(2):
            for st in range(PER):
                at = st * OWN_ROWS + X_ROWS
                proj[st, tg, :, cg * LANES : (cg + 1) * LANES] = own_ref[
                    tg * 4 + group * 2 + cg, at : at + BC_ROWS, :
                ]


def softplus(v):
    return jnp.maximum(v, 0.0) + jnp.log1p(jnp.exp(-jnp.abs(v)))


def ends_kernel(bounds_ref, own_ref, bias_ref, rate_ref, out_ref, step_ref, decay_ref, proj, turned, parts):
    base = bounds_ref[DOCS + 1] * CHUNK

    @pl.when(pl.program_id(0) == 0)
    def _():
        for s in range(SEQ):
            tile = own_ref[s, PER * OWN_ROWS : OWNER_ROWS, :].astype(F32)
            for head in range(2):
                for q in range(4):
                    step_ref[2 * s + head : 2 * s + head + 1, q * LANES : (q + 1) * LANES] = tile[
                        4 * head + q : 4 * head + q + 1, :
                    ]
        step_ref[...] = softplus(step_ref[...] + bias_ref[...])
        decay_ref[...] = -rate_ref[...] * step_ref[...]
        gather_proj(own_ref, proj, 0)
        turned[...] = jnp.transpose(proj[...].reshape(CHUNK, STATE))
        log_sum = running_sums(decay_ref[...])
        pos = lax.broadcasted_iota(jnp.int32, (GROUP_HEADS, CHUNK), 1) + base
        last_doc = doc_start(bounds_ref, base + CHUNK - 1)
        load = jnp.exp(log_sum[:, CHUNK - 1 : CHUNK] - log_sum)
        parts[...] = as_parts(jnp.where(pos >= last_doc, step_ref[...] * load, 0.0), 2)

    for k in range(MANY):
        pair = pl.program_id(0) * MANY + k
        xs = channels(own_ref, pair)
        driven = (spread_heads(parts[...], pair, LANES) * xs).astype(BF16)
        out_ref[k] = jnp.dot(turned[...], driven, preferred_element_type=F32).astype(BF16)


def ends(bounds, rows, biases, rates):
    return pl.pallas_call(
        ends_kernel,
        grid_spec=pltpu.PrefetchScalarGridSpec(
            num_scalar_prefetch=1,
            grid=(SEQ // MANY,),
            in_specs=[
                whole(SEQ, OWNER_ROWS, LANES),
                whole(GROUP_HEADS, 1),
                whole(GROUP_HEADS, 1),
            ],
            out_specs=[
                pl.BlockSpec((MANY, STATE, LANES), lambda g, *_: (g, 0, 0)),
                whole(GROUP_HEADS, CHUNK),
                whole(GROUP_HEADS, CHUNK),
            ],
            scratch_shapes=[
                pltpu.VMEM((PER, 4, 16, STATE), BF16),
                pltpu.VMEM((STATE, CHUNK), BF16),
                pltpu.VMEM((CHUNK, 2 * GROUP_HEADS), BF16),
            ],
        ),
        out_shape=[
            jax.ShapeDtypeStruct((SEQ, STATE, LANES), BF16),
            jax.ShapeDtypeStruct((GROUP_HEADS, CHUNK), F32),
            jax.ShapeDtypeStruct((GROUP_HEADS, CHUNK), F32),
        ],
        compiler_params=params(24),
        cost_estimate=pl.CostEstimate(
            flops=1_000_000_000, bytes_accessed=4 * MIB, transcendentals=0
        ),
        name="ends",
    )(bounds, rows, biases, rates)


def chain_kernel(bounds_ref, ends_ref, total_ref, early_ref, late_ref, out_ref):
    state = jnp.zeros((STATE, LANES), F32)
    for c in range(SEQ):
        out_ref[c, 0:STATE, :] = state.astype(BF16)
        rows = early_ref if c < CALL_CHUNKS else late_ref
        out_ref[c, STATE:CHUNK, :] = rows[c % CALL_CHUNKS]
        if c < SEQ - 1:
            last_doc = doc_start(bounds_ref, jnp.int32((c + 1) * CHUNK - 1))
            keep = jnp.where(last_doc < c * CHUNK, total_ref[c : c + 1, :], 0.0)
            state = keep * state + ends_ref[c].astype(F32)


def chain(bounds, arrived, totals, early, late):
    return pl.pallas_call(
        chain_kernel,
        grid_spec=pltpu.PrefetchScalarGridSpec(
            num_scalar_prefetch=1,
            grid=(1,),
            in_specs=[
                whole(SEQ, STATE, LANES),
                whole(SEQ, LANES),
                whole(CALL_CHUNKS, HALF, LANES),
                whole(CALL_CHUNKS, HALF, LANES),
            ],
            out_specs=whole(SEQ, CHUNK, LANES),
        ),
        out_shape=jax.ShapeDtypeStruct((SEQ, CHUNK, LANES), BF16),
        compiler_params=params(24),
        cost_estimate=pl.CostEstimate(flops=0, bytes_accessed=5 * MIB, transcendentals=0),
        name="chain",
    )(bounds, arrived, totals, early, late)


def inner_kernel(
    bounds_ref,
    own_ref,
    step_ref,
    decay_ref,
    gain_ref,
    out_ref,
    c_out,
    reach_out,
    proj_b,
    proj_c,
    turned,
    grams,
    sums,
    sum_rows,
    sum_parts,
    step_parts,
    load_parts,
    reach_parts,
):
    base = bounds_ref[DOCS + 1] * CHUNK

    @pl.when(pl.program_id(0) == 0)
    def _():
        gather_proj(own_ref, proj_b, 0)
        gather_proj(own_ref, proj_c, 1)
        row = lax.broadcasted_iota(jnp.int32, (HALF, 1), 0)
        col = lax.broadcasted_iota(jnp.int32, (HALF, HALF), 1)
        for blk in range(2):
            b_blk = proj_b[blk * 4 : blk * 4 + 4].reshape(HALF, STATE)
            c_blk = proj_c[blk * 4 : blk * 4 + 4].reshape(HALF, STATE)
            c_out[blk * HALF : (blk + 1) * HALF, :] = c_blk
            gram = lax.dot_general(
                c_blk, b_blk, (((1,), (1,)), ((), ())), preferred_element_type=F32
            )
            start = base + blk * HALF
            first = doc_start(bounds_ref, start + row) - start
            grams[blk] = jnp.where((col <= row) & (col >= first), gram, 0.0)
            if blk == 0:
                turned[...] = jnp.transpose(b_blk)
            sums[:, blk * HALF : (blk + 1) * HALF] = running_sums(
                decay_ref[:, blk * HALF : (blk + 1) * HALF]
            )
        log_sum = sums[...]
        for head in range(GROUP_HEADS):
            sum_rows[head] = log_sum[head : head + 1, :]
        log_half = log_sum[:, HALF - 1 : HALF]
        pos = lax.broadcasted_iota(jnp.int32, (GROUP_HEADS, HALF), 1) + base
        mid_pos = base + HALF - 1
        load = jnp.where(
            pos >= doc_start(bounds_ref, mid_pos), jnp.exp(log_half - log_sum[:, :HALF]), 0.0
        )
        later = jnp.where(
            pos + HALF < next_doc(bounds_ref, mid_pos), jnp.exp(log_sum[:, HALF:]), 0.0
        )
        whole_sum = jnp.concatenate([log_sum[:, :HALF], log_sum[:, HALF:] + log_half], axis=1)
        pos = lax.broadcasted_iota(jnp.int32, (GROUP_HEADS, CHUNK), 1) + base
        reach_end = jnp.where(base > 0, next_doc(bounds_ref, base - 1), 0)
        reach = jnp.where(pos < reach_end, jnp.exp(whole_sum), 0.0)
        sum_parts[...] = as_parts(log_sum, 3)
        step_parts[...] = as_parts(step_ref[...], 2)
        load_parts[...] = as_parts(step_ref[:, :HALF] * load, 2)
        reach_parts[...] = as_parts(later, 2)
        reach_out[...] = as_parts(reach, 2)

    first_head = lax.broadcasted_iota(jnp.int32, (1, LANES), 1) < HEAD_DIM
    quarter = HALF // 2
    for k in range(PAIRS):
        pair = pl.program_id(0) * PAIRS + k
        gain = gain_ref[pair]
        sum_cols = spread_heads(sum_parts[...], pair, 2 * LANES)
        steps = spread_heads(step_parts[...], pair, LANES)
        loads = spread_heads(load_parts[...], pair, LANES)
        reach = spread_heads(reach_parts[...], pair, LANES)
        xs = channels(own_ref, pair)
        driven = (steps * xs).astype(BF16)
        loaded = (loads * xs[:HALF]).astype(BF16)
        state = jnp.dot(turned[...], loaded, preferred_element_type=F32).astype(BF16)
        for blk in range(2):
            for part in range(2):
                at = blk * HALF + part * quarter
                width = (part + 1) * quarter
                heads = []
                for head in range(2):
                    log_row = sum_rows[2 * pair + head][:, blk * HALF : blk * HALF + width]
                    log_col = sum_cols[at : at + quarter, head * LANES : (head + 1) * LANES]
                    log_col = jnp.concatenate([log_col] * (part + 1), axis=1)
                    weight = jnp.exp(jnp.minimum(log_col - log_row, 0.0))
                    gram = grams[blk, part * quarter : (part + 1) * quarter, 0:width]
                    heads.append(
                        jnp.dot(
                            (gram * weight).astype(BF16),
                            driven[blk * HALF : blk * HALF + width],
                            preferred_element_type=F32,
                        )
                    )
                result = jnp.where(first_head, heads[0], heads[1]) + gain * xs[at : at + quarter]
                if blk == 1:
                    c_part = c_out[at : at + quarter, :]
                    result += reach[part * quarter : (part + 1) * quarter] * jnp.dot(
                        c_part, state, preferred_element_type=F32
                    )
                out_ref[at : at + quarter, k * LANES : (k + 1) * LANES] = result.astype(BF16)


def inner(bounds, rows, steps, decays, gains):
    return pl.pallas_call(
        inner_kernel,
        grid_spec=pltpu.PrefetchScalarGridSpec(
            num_scalar_prefetch=1,
            grid=(SEQ // PAIRS,),
            in_specs=[
                whole(SEQ, OWNER_ROWS, LANES),
                whole(GROUP_HEADS, CHUNK),
                whole(GROUP_HEADS, CHUNK),
                whole(SEQ, 1, LANES),
            ],
            out_specs=[
                pl.BlockSpec((CHUNK, PAIRS * LANES), lambda g, *_: (0, g)),
                whole(CHUNK, STATE),
                whole(CHUNK, 2 * GROUP_HEADS),
            ],
            scratch_shapes=[
                pltpu.VMEM((PER, 4, 16, STATE), BF16),
                pltpu.VMEM((PER, 4, 16, STATE), BF16),
                pltpu.VMEM((STATE, HALF), BF16),
                pltpu.VMEM((2, HALF, HALF), F32),
                pltpu.VMEM((GROUP_HEADS, CHUNK), F32),
                pltpu.VMEM((GROUP_HEADS, 1, CHUNK), F32),
                pltpu.VMEM((CHUNK, 3 * GROUP_HEADS), BF16),
                pltpu.VMEM((CHUNK, 2 * GROUP_HEADS), BF16),
                pltpu.VMEM((HALF, 2 * GROUP_HEADS), BF16),
                pltpu.VMEM((HALF, 2 * GROUP_HEADS), BF16),
            ],
        ),
        out_shape=[
            jax.ShapeDtypeStruct((CHUNK, SEQ * LANES), BF16),
            jax.ShapeDtypeStruct((CHUNK, STATE), BF16),
            jax.ShapeDtypeStruct((CHUNK, 2 * GROUP_HEADS), BF16),
        ],
        compiler_params=params(32),
        cost_estimate=pl.CostEstimate(
            flops=4_000_000_000, bytes_accessed=8 * MIB, transcendentals=4 * MIB
        ),
        name="inner",
    )(bounds, rows, steps, decays, gains)


def finish_kernel(state_ref, attn_ref, inner_ref, c_ref, reach_ref, ssm_ref, out_ref):
    @pl.when(pl.program_id(0) == 0)
    def _():
        for s in range(SEQ):
            for st in range(PER):
                at = st * LEN + (s % 2) * Q_ROWS
                out_ref[at : at + Q_ROWS, (s // 2) * LANES : (s // 2 + 1) * LANES] = attn_ref[
                    s, st * Q_ROWS : (st + 1) * Q_ROWS, :
                ]

    for k in range(MANY):
        pair = pl.program_id(0) * MANY + k
        cols = slice(k * LANES, (k + 1) * LANES)
        reached = jnp.dot(c_ref[...], state_ref[k], preferred_element_type=F32)
        reached = spread_heads(reach_ref[...], pair, LANES) * reached
        ssm_ref[:, cols] = (inner_ref[:, cols].astype(F32) + reached).astype(BF16)


def finish(both, inner_out, c_rows, reach):
    return pl.pallas_call(
        finish_kernel,
        grid=(SEQ // MANY,),
        in_specs=[
            pl.BlockSpec((MANY, STATE, LANES), lambda g: (g, 0, 0)),
            pl.BlockSpec((SEQ, HALF, LANES), lambda g: (0, 1, 0)),
            pl.BlockSpec((CHUNK, MANY * LANES), lambda g: (0, g)),
            whole(CHUNK, STATE),
            whole(CHUNK, 2 * GROUP_HEADS),
        ],
        out_specs=[
            pl.BlockSpec((CHUNK, MANY * LANES), lambda g: (0, g)),
            whole(CHUNK, PER * LANES),
        ],
        out_shape=[
            jax.ShapeDtypeStruct((CHUNK, SEQ * LANES), BF16),
            jax.ShapeDtypeStruct((CHUNK, PER * LANES), BF16),
        ],
        compiler_params=params(24),
        cost_estimate=pl.CostEstimate(
            flops=1_000_000_000, bytes_accessed=9 * MIB, transcendentals=0
        ),
        name="finish",
    )(both, both, inner_out, c_rows, reach)


def shards(
    stretch_x,
    stretch_bc,
    stretch_dt,
    stretch_q,
    stretch_kv,
    stretch_place,
    segment_ids,
    ssm_rate,
    dt_bias,
    skip_gain,
):
    seq_index = lax.axis_index("seq")
    mp_index = lax.axis_index("mp")
    exchange = functools.partial(lax.all_to_all, split_axis=0, concat_axis=0, tiled=True)
    cut = functools.partial(lax.dynamic_slice_in_dim, axis=0)

    my_docs = cut(segment_ids, mp_index * LEN, LEN)
    my_place = cut(stretch_place, mp_index, 1)
    info = jnp.concatenate([my_docs, my_place, jnp.zeros((LEN - 1,), jnp.int32)])
    info = jnp.broadcast_to(info.astype(F32)[None, :], (8, LANES))
    kv = lax.all_gather(exchange(pack_kv(stretch_kv), "mp"), "seq", axis=0, tiled=True)
    to_heads = pack(
        stretch_x, stretch_bc, stretch_q, stretch_dt.T.reshape(STRETCHES, LANES), info
    )
    hop = exchange(to_heads.reshape(STRETCHES, HOP_ROWS, LANES), ("seq", "mp"))

    told = hop[:, INFO_AT, :].astype(jnp.int32)
    places, docs = told[:, LEN], told[:, :LEN]
    order = jnp.arange(STRETCHES, dtype=jnp.int32)
    inv = jnp.sum(jnp.where(places[None, :] == order[:, None], order[None, :], 0), axis=1)
    bounds = jnp.stack(
        [jnp.sum((docs < v).astype(jnp.int32)) for v in range(DOCS)] + [seq_index % 2, seq_index]
    )
    to_owners, queries = place(inv, hop)
    own_rows = exchange(to_owners, "seq")
    group_first = mp_index * GROUP_HEADS
    biases = cut(dt_bias, group_first, GROUP_HEADS)
    rates = cut(ssm_rate, group_first, GROUP_HEADS)
    gains = cut(skip_gain, group_first, GROUP_HEADS)
    early, own_bounds = lax.optimization_barrier((attend(0, inv, bounds, kv, queries), bounds))
    late = attend(CALL_CHUNKS, inv, own_bounds, kv, queries)
    own_ends, steps, decays = ends(own_bounds, own_rows, biases[:, None], rates[:, None])
    arrived = exchange(own_ends, "seq")

    mine = hop[:, INFO_AT + 1, :].astype(F32)
    mine = mine.reshape(STRETCHES, 2, LEN) + cut(biases, 2 * seq_index, 2)[:, None]
    lost = -cut(rates, 2 * seq_index, 2) * jnp.sum(jax.nn.softplus(mine), axis=2)
    chunk_of = (places // PER)[None, :, None] == jnp.arange(SEQ)[:, None, None]
    lost = jnp.sum(jnp.where(chunk_of, lost[None], 0.0), axis=1)
    totals = jnp.repeat(jnp.exp(lost), HEAD_DIM, axis=1)

    both = exchange(chain(bounds, arrived, totals, early, late), "seq")
    inner_out, c_rows, reach = inner(
        bounds, own_rows, steps, decays, jnp.repeat(gains.reshape(SEQ, 1, 2), HEAD_DIM, axis=2)
    )
    return tuple(finish(both, inner_out, c_rows, reach))


def solution(mesh):
    return jax.shard_map(
        shards,
        mesh=mesh,
        in_specs=(
            P(("seq", "mp"), None),
            P(("seq", "mp"), None, None),
            P(("seq", "mp"), None),
            P(("seq", "mp"), None),
            P(("seq", "mp"), None, None),
            P("seq"),
            P("seq"),
            P(),
            P(),
            P(),
        ),
        out_specs=(P("seq", "mp"), P("seq", "mp")),
        check_vma=False,
    )
```
